32 devices in a mesh: fsdp: 16 (over z, x, core), rep: 2 (over y).
Axes of the slice: x: 2, y: 2, z: 4, core: 2. Of those that a mesh axis runs over, the one named last changes fastest.
Arguments:
- tokens: bfloat16 [1024, 64, 768], P(('fsdp', 'rep')), may hold values from -6 to 6
- counts: int32 [1024], P(('fsdp', 'rep')), may hold values from 40 to 60, as said below
- cotangent: bfloat16 [1024, 64, 768], P(('fsdp', 'rep')), may hold values from -6 to 6
- first_gain: bfloat16 [768], P('fsdp'), may hold values from 0.25 to 1.75
- first_shift: bfloat16 [768], P('fsdp'), may hold values from -1.75 to 1.75
- in_proj: bfloat16 [768, 2304], P('fsdp'), may hold values from -0.21875 to 0.21875
- query_bias: bfloat16 [768], P('fsdp'), may hold values from -3 to 3
- value_bias: bfloat16 [768], P('fsdp'), may hold values from -3 to 3
- out_proj: bfloat16 [768, 768], P('fsdp'), may hold values from -0.875 to 0.875
- out_bias: bfloat16 [768], P('fsdp'), may hold values from -1.75 to 1.75
- second_gain: bfloat16 [768], P('fsdp'), may hold values from 0.25 to 1.75
- second_shift: bfloat16 [768], P('fsdp'), may hold values from -1.75 to 1.75
- up_proj: bfloat16 [768, 3072], P('fsdp'), may hold values from -0.21875 to 0.21875
- hidden_bias: bfloat16 [3072], P('fsdp'), may hold values from -3 to 3
- down_proj: bfloat16 [3072, 768], P('fsdp'), may hold values from -0.15625 to 0.15625
- down_bias: bfloat16 [768], P('fsdp'), may hold values from -1.75 to 1.75
Outputs:
- mixed: bfloat16 [1024, 64, 768], P(('fsdp', 'rep'))
- tokens_grad: bfloat16 [1024, 64, 768], P(('fsdp', 'rep'))
- first_gain_grad: float32 [768], P('fsdp')
- first_shift_grad: float32 [768], P('fsdp')
- in_proj_grad: float32 [768, 2304], P('fsdp')
- query_bias_grad: float32 [768], P('fsdp')
- value_bias_grad: float32 [768], P('fsdp')
- out_proj_grad: float32 [768, 768], P('fsdp')
- out_bias_grad: float32 [768], P('fsdp')
- second_gain_grad: float32 [768], P('fsdp')
- second_shift_grad: float32 [768], P('fsdp')
- up_proj_grad: float32 [768, 3072], P('fsdp')
- hidden_bias_grad: float32 [3072], P('fsdp')
- down_proj_grad: float32 [3072, 768], P('fsdp')
- down_bias_grad: float32 [768], P('fsdp')
The draws below stay inside these ranges and needn't reach their ends.
Inputs may be any that keep to these rules, and one draw needn't show every extreme that they name: Rows 0 to counts[i] of image i hold its class token and visible patches; the rest of its 64 rows are padding.
All inputs are finite; a program needn't handle non-finite values.
Results may differ from the reference program's by a relative error of at most 0.015.
Values may be sent and summed in bfloat16 or wider, within the bound.
No kernel may reach another device: no remote copies, remote signals or barrier semaphores. Data moves between devices by JAX's collectives and lax.ppermute only.
A program may use at most 256 MiB of HBM per device.

```python
import jax
import jax.numpy as jnp
from jax import lax

D = 768
FF = 3072
HEADS = 12
HEAD = 64
ROWS = 64
LEAST = 40
MOST = 60
IMAGES = 1024


def draw_counts(key, part):
    key = jax.random.fold_in(key, 7)
    key_base, key_high, key_low = jax.random.split(key, 3)
    values = jax.random.randint(key_base, (IMAGES,), LEAST, MOST + 1).astype(jnp.int32)
    high_at = jax.random.randint(key_high, (), 0, IMAGES)
    low_at = (high_at + 1 + jax.random.randint(key_low, (), 0, IMAGES - 1)) % IMAGES
    values = values.at[high_at].set(MOST)
    values = values.at[low_at].set(LEAST)
    return values.astype(jnp.int32)


def raised(entries, rng, source, target, shards_of, factor):
    def block_of(dim):
        return (jnp.arange(entries.shape[dim]) // (entries.shape[dim] // shards_of)).reshape((-1,) + (1,) * (entries.ndim - 1 - dim))

    near = jax.random.permutation(rng, shards_of)[block_of(target)]
    far = (block_of(target) + shards_of // 2) % shards_of
    return jnp.where((block_of(source) == near) | (block_of(source) == far), factor * entries, entries)


def steps_of(rng, shape, shards, least, high):
    level = 1.0
    for dim, blocks in shards:
        draws = jax.random.uniform(jax.random.fold_in(jax.random.fold_in(rng, 6), dim), (blocks,), jnp.float32, least / len(shards), high / len(shards))
        level = level * jnp.repeat(jnp.exp(draws), shape[dim] // blocks).reshape((-1,) + (1,) * (len(shape) - 1 - dim))
    return level


def noise(key, extent, deviation, reach, cuts=(), kind=jnp.bfloat16):
    level = steps_of(key, extent, cuts, -0.22, 0.18) if cuts else 1.0
    values = jax.random.normal(key, extent, jnp.float32) * deviation * level
    return jnp.minimum(jnp.maximum(values, -reach), reach).astype(kind)


def bell_draw_with(stream_key, dims, spread, limit, cuts, heavy, held_as=jnp.bfloat16):
    array = spread * jax.random.normal(stream_key, dims, jnp.float32)
    if cuts:
        array = array * steps_of(stream_key, dims, cuts, -0.22, 0.18)
    return jnp.clip(raised(array, jax.random.fold_in(stream_key, 3), *heavy), -limit, limit).astype(held_as)


def setup_inputs(seed: int = 0) -> dict:
    key_list = jax.random.split(jax.random.key(seed), 17)
    tokens = bell_draw_with(key_list[0], (IMAGES, ROWS, D), 1.0, 6.0, ((0, 32),), (0, 2, 32, 2.75))
    counts = draw_counts(jax.random.fold_in(key_list[16], 71), 0)
    cotangent = noise(key_list[2], (IMAGES, ROWS, D), 1.0, 6.0, ((0, 32),))
    first_gain = jnp.clip(1.0 + 0.15 * jax.random.normal(key_list[3], (D,), jnp.float32), 0.25, 1.75).astype(jnp.bfloat16)
    first_shift = noise(key_list[4], (D,), 0.3, 1.75, ((0, 16),))
    in_proj = noise(key_list[5], (D, 3 * D), D ** -0.5, 0.21875, ((0, 16),))
    query_bias = noise(key_list[6], (D,), 0.5, 3.0, ((0, 16),))
    value_bias = noise(key_list[7], (D,), 0.5, 3.0, ((0, 16),))
    out_proj = noise(key_list[8], (D, D), (D // 16) ** -0.5, 0.875, ((0, 16),))
    out_bias = noise(key_list[9], (D,), 0.3, 1.75, ((0, 16),))
    second_gain = jnp.clip(1.0 + 0.15 * jax.random.normal(key_list[10], (D,), jnp.float32), 0.25, 1.75).astype(jnp.bfloat16)
    second_shift = noise(key_list[11], (D,), 0.3, 1.75, ((0, 16),))
    up_proj = noise(key_list[12], (D, FF), D ** -0.5, 0.21875, ((0, 16),))
    hidden_bias = noise(key_list[13], (FF,), 0.5, 3.0, ((0, 16),))
    down_proj = noise(key_list[14], (FF, D), (FF // 2) ** -0.5, 0.15625, ((0, 16),))
    down_bias = noise(key_list[15], (D,), 0.3, 1.75, ((0, 16),))
    return dict(tokens=tokens, counts=counts, cotangent=cotangent, first_gain=first_gain, first_shift=first_shift, in_proj=in_proj, query_bias=query_bias, value_bias=value_bias, out_proj=out_proj, out_bias=out_bias, second_gain=second_gain, second_shift=second_shift, up_proj=up_proj, hidden_bias=hidden_bias, down_proj=down_proj, down_bias=down_bias)


@jax.custom_vjp
def low(v):
    return lax.optimization_barrier(v.astype(jnp.bfloat16)).astype(jnp.float32)

@jax.custom_vjp
def low_back(v):
    return v

def low_keep(v):
    return (low(v), None)

def low_pass(kept, grad):
    return (grad,)

def back_keep(v):
    return (v, None)

def back_low(kept, grad):
    return (low(grad),)
low.defvjp(low_keep, low_pass)
low_back.defvjp(back_keep, back_low)
EPS = 1e-06
GROUP = 32

def norm_rows(v, gain, shift):
    center = v - lax.optimization_barrier(jnp.mean(v, axis=-1, keepdims=True))
    var = lax.optimization_barrier(jnp.mean(center * center, axis=-1, keepdims=True))
    return center * lax.rsqrt(var + EPS) * gain + shift

def gelu_exact(v):
    return 0.5 * v * (1.0 + lax.erf(v * 0.7071067811865476))

def matmul(left, right):
    return jnp.dot(left, right, precision=lax.Precision.HIGHEST)

def group_layer(params, xgroup, cgroup):
    first_gain, first_shift, in_proj, query_bias, value_bias, out_proj, out_bias, second_gain, second_shift, up_proj, hidden_bias, down_proj, down_bias = params
    images = xgroup.shape[0]
    positions = lax.broadcasted_iota(jnp.int32, (images, ROWS), 1)
    usable = positions <= cgroup[:, None]
    valid = usable.astype(jnp.float32).reshape(images * ROWS, 1)
    x = xgroup.reshape(images * ROWS, D)
    first = low(norm_rows(x, first_gain, first_shift))
    bias_all = jnp.concatenate([query_bias, jnp.zeros((D,), jnp.float32), value_bias])
    qkv = low(low_back(matmul(first, in_proj) + bias_all))
    qkv = qkv.reshape(images, ROWS, 3, HEADS, HEAD)
    query, key, value = (qkv[:, :, 0], qkv[:, :, 1], qkv[:, :, 2])
    scores = jnp.einsum('iqhe,ikhe->ihqk', query, key, precision=lax.Precision.HIGHEST) * 0.125
    scores = low_back(jnp.where(usable[:, None, None, :], scores, -1000000000.0))
    expo = jnp.exp(scores - lax.optimization_barrier(jnp.max(scores, axis=-1, keepdims=True)))
    probs = low(expo / lax.optimization_barrier(jnp.sum(expo, axis=-1, keepdims=True)))
    attended = jnp.einsum('ihqk,ikhe->iqhe', probs, value, precision=lax.Precision.HIGHEST)
    attended = low(low_back(attended.reshape(images * ROWS, D)))
    middle = x + low_back(matmul(attended, out_proj)) + out_bias
    second = low(norm_rows(middle, second_gain, second_shift))
    hidden = low_back(matmul(second, up_proj) + hidden_bias)
    act = low(gelu_exact(hidden))
    result = valid * (middle + low_back(matmul(act, down_proj)) + down_bias)
    return result.reshape(images, ROWS, D)

def reference(tokens, counts, cotangent, first_gain, first_shift, in_proj, query_bias, value_bias, out_proj, out_bias, second_gain, second_shift, up_proj, hidden_bias, down_proj, down_bias):
    params = tuple((p.astype(jnp.float32) for p in (first_gain, first_shift, in_proj, query_bias, value_bias, out_proj, out_bias, second_gain, second_shift, up_proj, hidden_bias, down_proj, down_bias)))
    groups = IMAGES // GROUP
    count_groups = counts.reshape(groups, GROUP)
    checked = jax.checkpoint(group_layer)

    def forward(x, *weights):
        xs = x.reshape(groups, GROUP, ROWS, D)

        def step(carry, inputs):
            return (carry, checked(weights, inputs[0], inputs[1]))
        unused, outs = lax.scan(step, jnp.zeros((), jnp.float32), (xs, count_groups))
        return outs.reshape(IMAGES, ROWS, D)
    result, pullback = jax.vjp(forward, tokens.astype(jnp.float32), *params)
    grads = pullback(cotangent.astype(jnp.float32))
    return (result.astype(jnp.bfloat16), grads[0].astype(jnp.bfloat16), grads[1], grads[2], grads[3], grads[4], grads[5], grads[6], grads[7], grads[8], grads[9], grads[10], grads[11], grads[12], grads[13])
```

```python
import functools
import jax
import jax.numpy as jnp
from jax import lax
from jax.experimental import pallas as pl
from jax.experimental.pallas import tpu as pltpu
from jax.sharding import PartitionSpec as P

HEADS = 12
HEAD = 64
EPS = 1e-06
BF = jnp.bfloat16
F32 = jnp.float32
VMEM = 60 << 20


def dot(a, b):
    return jnp.dot(a, b, preferred_element_type=F32)


def dot_rt(a, b):
    return lax.dot_general(a, b, (((1,), (1,)), ((), ())), preferred_element_type=F32)


def dot_lt(a, b):
    return lax.dot_general(a, b, (((0,), (0,)), ((), ())), preferred_element_type=F32)


def norm_stats(v):
    center = v - jnp.mean(v, axis=-1, keepdims=True)
    inv = lax.rsqrt(jnp.mean(center * center, axis=-1, keepdims=True) + EPS)
    return center, inv


def params(**kw):
    return pltpu.CompilerParams(vmem_limit_bytes=VMEM, **kw)


def full(shape):
    zeros = (0,) * len(shape)
    return pl.BlockSpec(shape, lambda *_: zeros, pipeline_mode=pl.Buffered(buffer_count=1))


def split_heads(pair, left):
    zero = jnp.zeros_like(pair)
    return jnp.concatenate([jnp.where(left, pair, zero), jnp.where(left, zero, pair)], axis=0)


def pair_cols(width, p):
    return [slice(j * width + p * 128, j * width + (p + 1) * 128) for j in range(3)]


def attn_fwd_kernel(unroll, counts, x_ref, cot_ref, vec, w_in, w_out,
                    qkv_ref, probs_ref, att_ref, mid_ref, sec_ref, back_ref, db_ref):
    step = pl.program_id(0)
    rows, width = x_ref.shape
    per = rows // 64
    x = x_ref[...].astype(F32)
    center, inv = norm_stats(x)
    first = (center * inv * vec[0:1] + vec[1:2]).astype(BF)
    for j in range(3):
        cols = slice(j * width, (j + 1) * width)
        qkv_ref[:, cols] = (dot(first, w_in[:, cols]) + vec[2 + j:3 + j]).astype(BF)
    left = lax.broadcasted_iota(jnp.int32, (64, 128), 1) < HEAD
    row = lax.broadcasted_iota(jnp.int32, (64, 128), 0)
    pos = lax.broadcasted_iota(jnp.int32, (64, width), 0)

    def images(group, total):
        work = []
        for u in range(unroll):
            i = group * unroll + u
            count = counts[step * per + i]
            at = pl.ds(pl.multiple_of(i * 64, 64), 64)
            work += [(i, at, row <= count, pair_cols(width, p), p) for p in range(HEADS // 2)]
            back = jnp.where(pos <= count, cot_ref[at, :].astype(F32), 0.0)
            back_ref[at, :] = back.astype(BF)
            total = total + jnp.sum(back, axis=0, keepdims=True)
        scores = [dot_rt(qkv_ref[at, c[1]], split_heads(qkv_ref[at, c[0]], left)) for i, at, usable, c, p in work]
        lows = []
        for (i, at, usable, c, p), s in zip(work, scores):
            s = jnp.where(usable, s * 0.125, -1000000000.0)
            e = jnp.exp(s - jnp.max(s, axis=0, keepdims=True))
            low = (e * (1.0 / jnp.sum(e, axis=0, keepdims=True))).astype(BF)
            probs_ref[i, p] = low
            lows.append(low)
        for (i, at, usable, c, p), low in zip(work, lows):
            o = dot_lt(low, qkv_ref[at, c[2]])
            att_ref[at, c[0]] = jnp.where(left, o[:64], o[64:]).astype(BF)
        return total

    total = lax.fori_loop(0, per // unroll, images, jnp.zeros((1, width), F32))

    @pl.when(step == 0)
    def _():
        db_ref[...] = total

    @pl.when(step > 0)
    def _():
        db_ref[...] += total

    mid = x + dot(att_ref[...], w_out[...]) + vec[5:6]
    mid_ref[...] = mid
    center, inv = norm_stats(mid)
    sec_ref[...] = (center * inv * vec[6:7] + vec[7:8]).astype(BF)


def attn_fwd(counts, x, cot, vec, w_in, w_out, rows=512, unroll=4):
    total, width = x.shape
    per = rows // 64
    blk = lambda w: pl.BlockSpec((rows, w), lambda i: (i, 0))
    return pl.pallas_call(
        functools.partial(attn_fwd_kernel, unroll),
        grid=(total // rows,),
        in_specs=[pl.BlockSpec(memory_space=pltpu.SMEM), blk(width), blk(width)]
        + [full(a.shape) for a in (vec, w_in, w_out)],
        out_specs=[blk(3 * width), pl.BlockSpec((per, HEADS // 2, 64, 128), lambda i: (i, 0, 0, 0)),
                   blk(width), blk(width), blk(width), blk(width), pl.BlockSpec((1, width), lambda i: (0, 0))],
        out_shape=[jax.ShapeDtypeStruct((total, 3 * width), BF),
                   jax.ShapeDtypeStruct((total // 64, HEADS // 2, 64, 128), BF),
                   jax.ShapeDtypeStruct((total, width), BF),
                   jax.ShapeDtypeStruct((total, width), F32),
                   jax.ShapeDtypeStruct((total, width), BF),
                   jax.ShapeDtypeStruct((total, width), BF),
                   jax.ShapeDtypeStruct((1, width), F32)],
        compiler_params=params(),
        name="attn_fwd",
    )(counts, x, cot, vec, w_in, w_out)


def gelu_parts(h):
    cdf = 0.5 + 0.5 * lax.erf(h * 0.7071067811865476)
    pdf = jnp.exp(h * h * -0.5) * 0.3989422804014327
    return (h * cdf).astype(BF), cdf + h * pdf


def mlp_kernel(chunk, sec_ref, back_ref, vec, up, down, act_ref, hg_ref, dg_ref, ug_ref, hb_ref):
    rows = sec_ref.shape[0]
    bias = vec[pl.ds(9 + pl.program_id(0), 1), :]
    sums = jnp.zeros((8, hb_ref.shape[1]), F32)
    for r in range(rows // chunk):
        at = slice(r * chunk, (r + 1) * chunk)
        act, slope = gelu_parts(dot(sec_ref[at], up[...]) + bias)
        act_ref[at] = act
        hg = (dot_rt(back_ref[at], down[...]) * slope).astype(BF)
        hg_ref[at] = hg
        sums = sums + jnp.sum(hg.astype(F32).reshape(chunk // 8, 8, -1), axis=0)
    hb_ref[...] = jnp.sum(sums, axis=0, keepdims=True)
    dg_ref[...] = dot_lt(act_ref[...], back_ref[...]).astype(BF)
    ug_ref[...] = dot_lt(sec_ref[...], hg_ref[...]).astype(BF)


def mlp(sec, back, vec, up, down, chunk=256):
    total, width = sec.shape
    ff = up.shape[1]
    f = width
    col = lambda r: pl.BlockSpec((r, f), lambda i: (0, i))
    row = pl.BlockSpec((f, width), lambda i: (i, 0))
    return pl.pallas_call(
        functools.partial(mlp_kernel, chunk),
        grid=(ff // f,),
        in_specs=[full(sec.shape), full(back.shape), full(vec.shape), col(width), row],
        out_specs=[col(total), col(total), row, col(width), col(1)],
        out_shape=[jax.ShapeDtypeStruct((total, ff), BF), jax.ShapeDtypeStruct((total, ff), BF),
                   jax.ShapeDtypeStruct((ff, width), BF), jax.ShapeDtypeStruct((width, ff), BF),
                   jax.ShapeDtypeStruct((1, ff), F32)],
        compiler_params=params(),
        name="mlp",
    )(sec, back, vec, up, down)


def attn_bwd_kernel(unroll, hg_ref, mid_ref, back_ref, att_ref, qkv_ref, probs_ref, vec, up, w_out,
                    mg_ref, qg_ref, og_ref, sums_ref, cs_ref, acc, ag_ref):
    step = pl.program_id(0)
    rows, width = mid_ref.shape
    per = rows // 64

    @pl.when(step == 0)
    def _():
        acc[...] = jnp.zeros_like(acc)
        sums_ref[...] = jnp.zeros_like(sums_ref)
        cs_ref[...] = jnp.zeros_like(cs_ref)

    sg = dot_rt(hg_ref[...], up[...])
    center, inv = norm_stats(mid_ref[...])
    n = center * inv
    e = sg * vec[6:7]
    sums_ref[0:1] += jnp.sum(sg * n, axis=0, keepdims=True)
    sums_ref[1:2] += jnp.sum(sg, axis=0, keepdims=True)
    norm_grad = inv * (e - jnp.mean(e, axis=-1, keepdims=True) - n * jnp.mean(e * n, axis=-1, keepdims=True))
    mg = back_ref[...].astype(F32) + norm_grad
    mg_ref[...] = mg
    sums_ref[2:3] += jnp.sum(mg, axis=0, keepdims=True)
    low = mg.astype(BF)
    ag_ref[...] = dot_rt(low, w_out[...]).astype(BF)
    acc[...] += dot_lt(att_ref[...], low)
    og_ref[...] = acc[...].astype(BF)
    left = lax.broadcasted_iota(jnp.int32, (64, 128), 1) < HEAD

    def images(group, carry):
        work = []
        for u in range(unroll):
            i = group * unroll + u
            at = pl.ds(pl.multiple_of(i * 64, 64), 64)
            work += [(i, at, pair_cols(width, p), p) for p in range(HEADS // 2)]
        dps = []
        for i, at, c, p in work:
            da = split_heads(ag_ref[at, c[0]], left)
            qg_ref[at, c[2]] = dot(probs_ref[i, p], da).astype(BF)
            dps.append(dot_rt(qkv_ref[at, c[2]], da))
        dss = []
        for (i, at, c, p), dp in zip(work, dps):
            pr = probs_ref[i, p].astype(F32)
            t = dp * pr
            dss.append((t - pr * jnp.sum(t, axis=0, keepdims=True)).astype(BF))
        for (i, at, c, p), ds in zip(work, dss):
            qg_ref[at, c[1]] = (dot(ds, split_heads(qkv_ref[at, c[0]], left)) * 0.125).astype(BF)
            dq = dot_lt(ds, qkv_ref[at, c[1]])
            qg_ref[at, c[0]] = (jnp.where(left, dq[:64], dq[64:]) * 0.125).astype(BF)
        return carry

    lax.fori_loop(0, per // unroll, images, 0)
    cs_ref[...] += jnp.sum(qg_ref[...].astype(F32), axis=0, keepdims=True)


def attn_bwd(hg, mid, back, att, qkv, probs, vec, up, w_out, rows=256, unroll=2):
    total, width = mid.shape
    ff = hg.shape[1]
    per = rows // 64
    blk = lambda w: pl.BlockSpec((rows, w), lambda i: (i, 0))
    one = lambda s: pl.BlockSpec(s, lambda i: (0, 0))
    return pl.pallas_call(
        functools.partial(attn_bwd_kernel, unroll),
        grid=(total // rows,),
        in_specs=[blk(ff), blk(width), blk(width), blk(width), blk(3 * width),
                  pl.BlockSpec((per, HEADS // 2, 64, 128), lambda i: (i, 0, 0, 0)),
                  full(vec.shape), full(up.shape), full(w_out.shape)],
        out_specs=[blk(width), blk(3 * width), one((width, width)), one((8, width)), one((1, 3 * width))],
        out_shape=[jax.ShapeDtypeStruct((total, width), F32), jax.ShapeDtypeStruct((total, 3 * width), BF),
                   jax.ShapeDtypeStruct((width, width), BF), jax.ShapeDtypeStruct((8, width), F32),
                   jax.ShapeDtypeStruct((1, 3 * width), F32)],
        scratch_shapes=[pltpu.VMEM((width, width), F32), pltpu.VMEM((rows, width), BF)],
        compiler_params=params(),
        name="attn_bwd",
    )(hg, mid, back, att, qkv, probs, vec, up, w_out)


def in_grad_kernel(x_ref, qg_ref, o_ref, n_ref):
    @pl.when(pl.program_id(0) == 0)
    def _():
        for r in range(0, x_ref.shape[0], 256):
            center, inv = norm_stats(x_ref[r:r + 256].astype(F32))
            n_ref[r:r + 256] = (center * inv).astype(BF)

    o_ref[...] = dot_lt(n_ref[...], qg_ref[...]).astype(BF)


def in_grad(x, qg, f=768):
    total, width = x.shape
    cols = qg.shape[1]
    return pl.pallas_call(
        in_grad_kernel,
        grid=(cols // f,),
        in_specs=[full(x.shape), pl.BlockSpec((total, f), lambda i: (0, i))],
        out_specs=pl.BlockSpec((width, f), lambda i: (0, i)),
        out_shape=jax.ShapeDtypeStruct((width, cols), BF),
        scratch_shapes=[pltpu.VMEM((total, width), BF)],
        compiler_params=params(),
        name="in_grad",
    )(x, qg)


def tokens_grad_kernel(x_ref, qg_ref, mg_ref, vec, w_in, o_ref):
    center, inv = norm_stats(x_ref[...].astype(F32))
    n = center * inv
    e = dot_rt(qg_ref[...], w_in[...]) * vec[0:1]
    grad = inv * (e - jnp.mean(e, axis=-1, keepdims=True) - n * jnp.mean(e * n, axis=-1, keepdims=True))
    o_ref[...] = (mg_ref[...] + grad).astype(BF)


def tokens_grad(x, qg, mg, vec, w_in, rows=256):
    total, width = x.shape
    blk = lambda w: pl.BlockSpec((rows, w), lambda i: (i, 0))
    return pl.pallas_call(
        tokens_grad_kernel,
        grid=(total // rows,),
        in_specs=[blk(width), blk(3 * width), blk(width), full(vec.shape), full(w_in.shape)],
        out_specs=blk(width),
        out_shape=jax.ShapeDtypeStruct((total, width), BF),
        compiler_params=params(),
        name="tokens_grad",
    )(x, qg, mg, vec, w_in)


def mixed_kernel(counts, act_ref, mid_ref, vec, down, o_ref):
    step = pl.program_id(0)
    per = o_ref.shape[0] // 64
    r = mid_ref[...] + dot(act_ref[...], down[...]) + vec[8:9]
    pos = lax.broadcasted_iota(jnp.int32, (64, o_ref.shape[1]), 0)
    for i in range(per):
        o_ref[i * 64:(i + 1) * 64] = jnp.where(pos <= counts[step * per + i], r[i * 64:(i + 1) * 64], 0.0).astype(BF)


def mixed_out(counts, act, mid, vec, down, rows=256):
    total, width = mid.shape
    ff = act.shape[1]
    blk = lambda w: pl.BlockSpec((rows, w), lambda i: (i, 0))
    return pl.pallas_call(
        mixed_kernel,
        grid=(total // rows,),
        in_specs=[pl.BlockSpec(memory_space=pltpu.SMEM), blk(ff), blk(width), full(vec.shape), full(down.shape)],
        out_specs=blk(width),
        out_shape=jax.ShapeDtypeStruct((total, width), BF),
        compiler_params=params(),
        name="mixed",
    )(counts, act, mid, vec, down)


def gather(v, axis=0):
    return lax.all_gather(v, "fsdp", axis=axis, tiled=True)


def both(shard):
    return lax.psum(shard.astype(BF), "rep").astype(F32)


def local(tokens, counts, cotangent, first_gain, first_shift, in_proj, query_bias, value_bias, out_proj, out_bias,
          second_gain, second_shift, up_proj, hidden_bias, down_proj, down_bias):
    images, rows, width = tokens.shape
    own = first_gain.shape[0]
    x = tokens.reshape(images * rows, width)
    cot = cotangent.reshape(images * rows, width)
    pack = jnp.concatenate([first_gain, first_shift, query_bias, jnp.zeros_like(query_bias), value_bias, out_bias,
                            second_gain, second_shift, down_bias, hidden_bias]).reshape(13, own)
    whole = lax.all_gather(pack, "fsdp", axis=0)
    vec = jnp.concatenate([whole[:, :9].transpose(1, 0, 2).reshape(9, width), whole[:, 9:].reshape(4, width),
                           jnp.zeros((3, width), BF)]).astype(F32)
    w_in = gather(in_proj)
    outup = gather(jnp.concatenate([out_proj, up_proj], axis=1))
    w_out, up = outup[:, :width], outup[:, width:]
    down = gather(down_proj)
    qkv, probs, att, mid, sec, back, db = attn_fwd(counts, x, cot, vec, w_in, w_out)
    act, hg, dg, ug, hb = mlp(sec, back, vec, up, down)
    scatter = lambda v: lax.psum_scatter(v, "fsdp", scatter_dimension=0, tiled=True)
    dg = scatter(dg)
    ug = scatter(ug)
    mg, qg, og, sums, cs = attn_bwd(hg, mid, back, att, qkv, probs, vec, up, w_out)
    ig = in_grad(x, qg)
    iog = scatter(jnp.concatenate([ig, og], axis=1))
    tg = tokens_grad(x, qg, mg, vec, w_in)
    mix = mixed_out(counts, act, mid, vec, down)
    sums = lax.psum(jnp.concatenate([db, sums[:3], cs.reshape(3, width), hb.reshape(4, width)]), ("fsdp", "rep"))
    iog, ug, dg = both(iog), both(ug), both(dg)
    cs = sums[4:7].reshape(1, 3 * width)
    ig, og = iog[:, :3 * width], iog[:, 3 * width:]
    w_own = in_proj.astype(F32)
    gain = first_gain.astype(F32).reshape(own, 1)
    shift = first_shift.astype(F32).reshape(own, 1)
    gain_grad = jnp.sum(ig * w_own, axis=1)
    shift_grad = jnp.sum(cs * w_own, axis=1)
    in_proj_grad = gain * ig + shift * cs
    me = lax.axis_index("fsdp")
    mine = lax.dynamic_slice_in_dim(sums[:7], me * own, own, 1)
    hidden_grad = lax.dynamic_slice_in_dim(sums[7:].reshape(-1), me * (4 * own), 4 * own, 0)
    return (mix.reshape(tokens.shape), tg.reshape(tokens.shape), gain_grad, shift_grad, in_proj_grad, mine[4], mine[6],
            og, mine[3], mine[1], mine[2], ug, hidden_grad, dg, mine[0])


def solution(mesh):
    rows = P(("fsdp", "rep"), None, None)
    v, m = P("fsdp"), P("fsdp", None)
    in_specs = (rows, P(("fsdp", "rep")), rows, v, v, m, v, v, m, v, v, v, m, v, m, v)
    out_specs = (rows, rows, v, v, m, v, v, m, v, v, v, m, v, m, v)
    return jax.shard_map(local, mesh=mesh, in_specs=in_specs, out_specs=out_specs, check_vma=False)
```

```python
import functools
import jax
import jax.numpy as jnp
from jax import lax
from jax.experimental import pallas as pl
from jax.experimental.pallas import tpu as pltpu
from jax.sharding import PartitionSpec as P

HEADS = 12
HEAD = 64
EPS = 1e-06
BF = jnp.bfloat16
F32 = jnp.float32
VMEM = 60 << 20


def dot(a, b):
    return jnp.dot(a, b, preferred_element_type=F32)


def dot_rt(a, b):
    return lax.dot_general(a, b, (((1,), (1,)), ((), ())), preferred_element_type=F32)


def dot_lt(a, b):
    return lax.dot_general(a, b, (((0,), (0,)), ((), ())), preferred_element_type=F32)


def norm_stats(v):
    center = v - jnp.mean(v, axis=-1, keepdims=True)
    inv = lax.rsqrt(jnp.mean(center * center, axis=-1, keepdims=True) + EPS)
    return center, inv


def params(**kw):
    return pltpu.CompilerParams(vmem_limit_bytes=VMEM, **kw)


def full(shape):
    zeros = (0,) * len(shape)
    return pl.BlockSpec(shape, lambda *_: zeros, pipeline_mode=pl.Buffered(buffer_count=1))


def split_heads(pair, left):
    zero = jnp.zeros_like(pair)
    return jnp.concatenate([jnp.where(left, pair, zero), jnp.where(left, zero, pair)], axis=0)


def cost(flops, nbytes):
    return pl.CostEstimate(flops=int(flops), bytes_accessed=int(nbytes), transcendentals=0)


GROUPS = 16


def position(hier):
    if not hier:
        return 0, 0, 0
    me = lax.axis_index("fsdp")
    return me // 4, (me // 2) % 2, me % 2


def owner(hier, pos, k, other_x, other_c):
    if not hier:
        return (k * 2 + other_x) * 2 + other_c
    z, x, c = pos
    z = lax.rem(z + k, 4)
    x = 1 - x if other_x else x
    c = 1 - c if other_c else c
    return (z * 2 + x) * 2 + c


def piece_copies(hier, mine, other, w_ref, sems, cols):
    pos = position(hier)
    out = []
    for c, ref in enumerate((mine, other)):
        for x in range(2):
            for k in range(4):
                slot = owner(hier, pos, (4 - k) % 4, x, c)
                out.append(pltpu.make_async_copy(ref.at[x * 4 + k, :, cols], w_ref.at[slot], sems.at[len(out)]))
    return out


def whole_of(w_ref, cols=None):
    w = w_ref[...] if cols is None else w_ref[:, :, cols]
    return w.reshape(w.shape[0] * w.shape[1], w.shape[2])


def pair_cols(width, p):
    return [slice(j * width + p * 128, j * width + (p + 1) * 128) for j in range(3)]


def attn_fwd_kernel(unroll, hier, counts, x_ref, cot_ref, mine, other,
                    qkv_ref, probs_ref, att_ref, mid_ref, sec_ref, back_ref, db_ref, vec, w_ref, sems):
    step = pl.program_id(0)
    rows, width = x_ref.shape

    @pl.when(step == 0)
    def _():
        copies = piece_copies(hier, mine, other, w_ref, sems, slice(None))
        for copy in copies:
            copy.start()
        for copy in copies:
            copy.wait()
        vec[...] = whole_of(w_ref, slice(4 * width, 4 * width + 128)).astype(F32).T[:16]

    per = rows // 64
    x = x_ref[...].astype(F32)
    center, inv = norm_stats(x)
    first = (center * inv * vec[0:1] + vec[1:2]).astype(BF)
    for j in range(3):
        cols = slice(j * width, (j + 1) * width)
        qkv_ref[:, cols] = (dot(first, whole_of(w_ref, cols)) + vec[2 + j:3 + j]).astype(BF)
    left = lax.broadcasted_iota(jnp.int32, (64, 128), 1) < HEAD
    row = lax.broadcasted_iota(jnp.int32, (64, 128), 0)
    pos = lax.broadcasted_iota(jnp.int32, (64, width), 0)

    def images(group, total):
        work = []
        for u in range(unroll):
            i = group * unroll + u
            count = counts[step * per + i]
            at = pl.ds(pl.multiple_of(i * 64, 64), 64)
            work += [(i, at, row <= count, pair_cols(width, p), p) for p in range(HEADS // 2)]
            back = jnp.where(pos <= count, cot_ref[at, :].astype(F32), 0.0)
            back_ref[at, :] = back.astype(BF)
            total = total + jnp.sum(back, axis=0, keepdims=True)
        scores = [dot_rt(qkv_ref[at, c[1]], split_heads(qkv_ref[at, c[0]], left)) for i, at, usable, c, p in work]
        lows = []
        for (i, at, usable, c, p), s in zip(work, scores):
            s = jnp.where(usable, s * 0.125, -1000000000.0)
            e = jnp.exp(s - jnp.max(s, axis=0, keepdims=True))
            low = (e * (1.0 / jnp.sum(e, axis=0, keepdims=True))).astype(BF)
            probs_ref[i, p] = low
            lows.append(low)
        for (i, at, usable, c, p), low in zip(work, lows):
            o = dot_lt(low, qkv_ref[at, c[2]])
            att_ref[at, c[0]] = jnp.where(left, o[:64], o[64:]).astype(BF)
        return total

    total = lax.fori_loop(0, per // unroll, images, jnp.zeros((1, width), F32))

    @pl.when(step == 0)
    def _():
        db_ref[...] = total

    @pl.when(step > 0)
    def _():
        db_ref[...] += total

    mid = x + dot(att_ref[...], whole_of(w_ref, slice(3 * width, 4 * width))) + vec[5:6]
    mid_ref[...] = mid
    center, inv = norm_stats(mid)
    sec_ref[...] = (center * inv * vec[6:7] + vec[7:8]).astype(BF)


ANY = pl.BlockSpec(memory_space=pl.ANY)


def attn_fwd(hier, counts, x, cot, mine, other, rows=512, unroll=4):
    total, width = x.shape
    per = rows // 64
    blk = lambda w: pl.BlockSpec((rows, w), lambda i: (i, 0))
    return pl.pallas_call(
        functools.partial(attn_fwd_kernel, unroll, hier),
        grid=(total // rows,),
        in_specs=[pl.BlockSpec(memory_space=pltpu.SMEM), blk(width), blk(width), ANY, ANY],
        out_specs=[blk(3 * width), pl.BlockSpec((per, HEADS // 2, 64, 128), lambda i: (i, 0, 0, 0)),
                   blk(width), blk(width), blk(width), blk(width), pl.BlockSpec((1, width), lambda i: (0, 0)),
                   pl.BlockSpec((16, width), lambda i: (0, 0))],
        out_shape=[jax.ShapeDtypeStruct((total, 3 * width), BF),
                   jax.ShapeDtypeStruct((total // 64, HEADS // 2, 64, 128), BF),
                   jax.ShapeDtypeStruct((total, width), BF),
                   jax.ShapeDtypeStruct((total, width), F32),
                   jax.ShapeDtypeStruct((total, width), BF),
                   jax.ShapeDtypeStruct((total, width), BF),
                   jax.ShapeDtypeStruct((1, width), F32),
                   jax.ShapeDtypeStruct((16, width), F32)],
        scratch_shapes=[pltpu.VMEM((GROUPS,) + mine.shape[1:], BF), pltpu.SemaphoreType.DMA((GROUPS,))],
        compiler_params=params(),
        cost_estimate=cost(8 * total * width * width * 1.5, 20 * total * width),
        name="attn_fwd",
    )(counts, x, cot, mine, other)


def gelu_parts(h):
    cdf = 0.5 + 0.5 * lax.erf(h * 0.7071067811865476)
    pdf = jnp.exp(h * h * -0.5) * 0.3989422804014327
    return (h * cdf).astype(BF), cdf + h * pdf


def whole_rows(packed):
    owners, rows, four = packed.shape
    width = four // 4
    return jnp.concatenate([packed[o, :, j * width:(j + 1) * width] for o in range(owners) for j in range(4)], axis=0)


def mlp_kernel(chunk, sec_ref, back_ref, bias_ref, up, down, act_ref, hg_ref, dg_ref, ug_ref, hb_ref):
    rows = sec_ref.shape[0]
    bias = bias_ref[...]
    down = whole_rows(down)
    sums = jnp.zeros((8, hb_ref.shape[1]), F32)
    for r in range(rows // chunk):
        at = slice(r * chunk, (r + 1) * chunk)
        act, slope = gelu_parts(dot(sec_ref[at], up[...]) + bias)
        act_ref[at] = act
        hg = (dot_rt(back_ref[at], down) * slope).astype(BF)
        hg_ref[at] = hg
        sums = sums + jnp.sum(hg.astype(F32).reshape(chunk // 8, 8, -1), axis=0)
    hb_ref[...] = jnp.sum(sums, axis=0, keepdims=True)
    dg_ref[...] = dot_lt(act_ref[...], back_ref[...]).astype(BF)
    ug_ref[...] = dot_lt(sec_ref[...], hg_ref[...]).astype(BF)


def mlp(sec, back, bias, updown, chunk=256):
    total, width = sec.shape
    ff = bias.shape[1]
    f = width
    col = lambda r: pl.BlockSpec((r, f), lambda i: (0, i))
    row = pl.BlockSpec((f, width), lambda i: (i, 0))
    packed = updown.reshape(GROUPS, width // GROUPS, 2 * ff)
    return pl.pallas_call(
        functools.partial(mlp_kernel, chunk),
        grid=(ff // f,),
        in_specs=[full(sec.shape), full(back.shape), col(1), col(width),
                  pl.BlockSpec((GROUPS * f // ff, width // GROUPS, ff), lambda i: (i, 0, 1))],
        out_specs=[col(total), col(total), row, col(width), col(1)],
        out_shape=[jax.ShapeDtypeStruct((total, ff), BF), jax.ShapeDtypeStruct((total, ff), BF),
                   jax.ShapeDtypeStruct((ff, width), BF), jax.ShapeDtypeStruct((width, ff), BF),
                   jax.ShapeDtypeStruct((1, ff), F32)],
        compiler_params=params(),
        cost_estimate=cost(8 * total * width * ff, 12 * total * width),
        name="mlp",
    )(sec, back, bias, updown, packed)


def attn_bwd_kernel(unroll, hier, hg_ref, mid_ref, back_ref, att_ref, qkv_ref, probs_ref, vec, up, mine, other,
                    mg_ref, qg_ref, og_ref, sums_ref, acc, ag_ref, w_out, sems):
    step = pl.program_id(0)
    rows, width = mid_ref.shape
    per = rows // 64

    @pl.when(step == 0)
    def _():
        copies = piece_copies(hier, mine, other, w_out, sems, slice(3 * width, 4 * width))
        for copy in copies:
            copy.start()
        acc[...] = jnp.zeros_like(acc)
        sums_ref[...] = jnp.zeros_like(sums_ref)
        for copy in copies:
            copy.wait()

    sg = dot_rt(hg_ref[...], up[...])
    center, inv = norm_stats(mid_ref[...])
    n = center * inv
    e = sg * vec[6:7]
    sums_ref[0:1] += jnp.sum(sg * n, axis=0, keepdims=True)
    sums_ref[1:2] += jnp.sum(sg, axis=0, keepdims=True)
    norm_grad = inv * (e - jnp.mean(e, axis=-1, keepdims=True) - n * jnp.mean(e * n, axis=-1, keepdims=True))
    mg = back_ref[...].astype(F32) + norm_grad
    mg_ref[...] = mg
    sums_ref[2:3] += jnp.sum(mg, axis=0, keepdims=True)
    low = mg.astype(BF)
    ag_ref[...] = dot_rt(low, whole_of(w_out)).astype(BF)
    acc[...] += dot_lt(att_ref[...], low)

    @pl.when(step == pl.num_programs(0) - 1)
    def _():
        og_ref[...] = acc[...].astype(BF)

    left = lax.broadcasted_iota(jnp.int32, (64, 128), 1) < HEAD

    def images(group, carry):
        work = []
        for u in range(unroll):
            i = group * unroll + u
            at = pl.ds(pl.multiple_of(i * 64, 64), 64)
            work += [(i, at, pair_cols(width, p), p) for p in range(HEADS // 2)]
        dps = []
        for i, at, c, p in work:
            da = split_heads(ag_ref[at, c[0]], left)
            qg_ref[at, c[2]] = dot(probs_ref[i, p], da).astype(BF)
            dps.append(dot_rt(qkv_ref[at, c[2]], da))
        dss = []
        for (i, at, c, p), dp in zip(work, dps):
            pr = probs_ref[i, p].astype(F32)
            t = dp * pr
            dss.append((t - pr * jnp.sum(t, axis=0, keepdims=True)).astype(BF))
        for (i, at, c, p), ds in zip(work, dss):
            qg_ref[at, c[1]] = (dot(ds, split_heads(qkv_ref[at, c[0]], left)) * 0.125).astype(BF)
            dq = dot_lt(ds, qkv_ref[at, c[1]])
            qg_ref[at, c[0]] = (jnp.where(left, dq[:64], dq[64:]) * 0.125).astype(BF)
        return carry

    lax.fori_loop(0, per // unroll, images, 0)


def attn_bwd(hier, hg, mid, back, att, qkv, probs, vec, updown, mine, other, rows=256, unroll=2):
    total, width = mid.shape
    ff = hg.shape[1]
    per = rows // 64
    blk = lambda w: pl.BlockSpec((rows, w), lambda i: (i, 0))
    one = lambda s: pl.BlockSpec(s, lambda i: (0, 0))
    return pl.pallas_call(
        functools.partial(attn_bwd_kernel, unroll, hier),
        grid=(total // rows,),
        in_specs=[blk(ff), blk(width), blk(width), blk(width), blk(3 * width),
                  pl.BlockSpec((per, HEADS // 2, 64, 128), lambda i: (i, 0, 0, 0)),
                  full(vec.shape), full((width, ff)), ANY, ANY],
        out_specs=[blk(width), blk(3 * width), one((width, width)), one((8, width))],
        out_shape=[jax.ShapeDtypeStruct((total, width), F32), jax.ShapeDtypeStruct((total, 3 * width), BF),
                   jax.ShapeDtypeStruct((width, width), BF), jax.ShapeDtypeStruct((8, width), F32)],
        scratch_shapes=[pltpu.VMEM((width, width), F32), pltpu.VMEM((rows, width), BF),
                        pltpu.VMEM((GROUPS, width // GROUPS, width), BF), pltpu.SemaphoreType.DMA((GROUPS,))],
        compiler_params=params(),
        cost_estimate=cost(2 * total * width * (ff + 6 * width), 24 * total * width),
        name="attn_bwd",
    )(hg, mid, back, att, qkv, probs, vec, updown, mine, other)


def in_grad_kernel(hier, x_ref, qg_hbm, og_ref, db_ref, sums_ref, hid_ref, mine, other,
                   near_ref, far_ref, n_ref, qg_ref, w_ref, block, sems, qg_sems):
    total, width = x_ref.shape
    pos = position(hier)
    weights = piece_copies(hier, mine, other, w_ref, sems, slice(None))
    loads = [pltpu.make_async_copy(qg_hbm.at[:, j * width:(j + 1) * width], qg_ref.at[j], qg_sems.at[j]) for j in range(3)]
    for copy in loads + weights:
        copy.start()

    def place(cols):
        for far, ref in enumerate((near_ref, far_ref)):
            for x in range(2):
                for k in range(4):
                    ref[x, k, :, cols] = block[owner(hier, pos, k, x, far), :, :cols.stop - cols.start]

    for r in range(0, total, 256):
        center, inv = norm_stats(x_ref[r:r + 256].astype(F32))
        n_ref[r:r + 256] = (center * inv).astype(BF)
    for copy in weights:
        copy.wait()
    vec = whole_of(w_ref, slice(4 * width, 4 * width + 128)).astype(F32)
    gain, shift = vec[:, 0:1], vec[:, 1:2]
    gain_grad = jnp.zeros((width, 1), F32)
    shift_grad = jnp.zeros((width, 1), F32)
    colsums = []
    for j in range(3):
        loads[j].wait()
        cols = slice(j * width, (j + 1) * width)
        m = dot_lt(n_ref[...], qg_ref[j])
        cs = jnp.sum(qg_ref[j].astype(F32), axis=0, keepdims=True)
        colsums.append(cs)
        w = whole_of(w_ref, cols).astype(F32)
        gain_grad = gain_grad + jnp.sum(w * m, axis=1, keepdims=True)
        shift_grad = shift_grad + jnp.sum(w * cs, axis=1, keepdims=True)
        block[...] = (gain * m + shift * cs).astype(BF).reshape(block.shape)
        place(cols)
    block[...] = og_ref[...].reshape(block.shape)
    place(slice(3 * width, 4 * width))
    rows = jnp.concatenate([db_ref[...], sums_ref[0:3], colsums[0], colsums[2], hid_ref[...], jnp.zeros((118, width), F32)])
    lane = lax.broadcasted_iota(jnp.int32, (width, 128), 1)
    tail = jnp.where(lane == 10, gain_grad, jnp.where(lane == 11, shift_grad, rows.T))
    block[:, :, :128] = tail.astype(BF).reshape(block.shape[0], block.shape[1], 128)
    place(slice(4 * width, 4 * width + 128))


def in_grad(hier, x, qg, og, db, sums, hid, mine, other):
    total, width = x.shape
    rows = width // GROUPS
    wide = 4 * width + 128
    vm = pl.BlockSpec(memory_space=pltpu.VMEM)
    return pl.pallas_call(
        functools.partial(in_grad_kernel, hier),
        in_specs=[vm, ANY, vm, vm, vm, vm, ANY, ANY],
        out_specs=[vm, vm],
        out_shape=[jax.ShapeDtypeStruct((2, 4, rows, wide), BF)] * 2,
        scratch_shapes=[pltpu.VMEM((total, width), BF), pltpu.VMEM((3, total, width), BF), pltpu.VMEM((GROUPS, rows, wide), BF),
                        pltpu.VMEM((GROUPS, rows, width), BF), pltpu.SemaphoreType.DMA((GROUPS,)), pltpu.SemaphoreType.DMA((3,))],
        compiler_params=params(),
        cost_estimate=cost(6 * total * width * width, 8 * total * width),
        name="in_grad",
    )(x, qg, og, db, sums, hid, mine, other)


def tokens_grad_kernel(hier, x_ref, qg_ref, mg_ref, vec, mine, other, o_ref, w_ref, sems):
    @pl.when(pl.program_id(0) == 0)
    def _():
        copies = piece_copies(hier, mine, other, w_ref, sems, slice(0, w_ref.shape[2]))
        for copy in copies:
            copy.start()
        for copy in copies:
            copy.wait()

    center, inv = norm_stats(x_ref[...].astype(F32))
    n = center * inv
    e = dot_rt(qg_ref[...], whole_of(w_ref)) * vec[0:1]
    grad = inv * (e - jnp.mean(e, axis=-1, keepdims=True) - n * jnp.mean(e * n, axis=-1, keepdims=True))
    o_ref[...] = (mg_ref[...] + grad).astype(BF)


def tokens_grad(hier, x, qg, mg, vec, mine, other, rows=256):
    total, width = x.shape
    blk = lambda w: pl.BlockSpec((rows, w), lambda i: (i, 0))
    return pl.pallas_call(
        functools.partial(tokens_grad_kernel, hier),
        grid=(total // rows,),
        in_specs=[blk(width), blk(3 * width), blk(width), full(vec.shape), ANY, ANY],
        out_specs=blk(width),
        out_shape=jax.ShapeDtypeStruct((total, width), BF),
        scratch_shapes=[pltpu.VMEM((GROUPS, width // GROUPS, 3 * width), BF), pltpu.SemaphoreType.DMA((GROUPS,))],
        compiler_params=params(),
        cost_estimate=cost(6 * total * width * width, 14 * total * width),
        name="tokens_grad",
    )(x, qg, mg, vec, mine, other)


def mixed_kernel(counts, act_ref, mid_ref, vec, down, o_ref, d_ref):
    step = pl.program_id(0)
    per = o_ref.shape[0] // 64

    @pl.when(step == 0)
    def _():
        d_ref[...] = whole_rows(down)

    r = mid_ref[...] + dot(act_ref[...], d_ref[...]) + vec[8:9]
    pos = lax.broadcasted_iota(jnp.int32, (64, o_ref.shape[1]), 0)
    for i in range(per):
        o_ref[i * 64:(i + 1) * 64] = jnp.where(pos <= counts[step * per + i], r[i * 64:(i + 1) * 64], 0.0).astype(BF)


def mixed_out(counts, act, mid, vec, updown, rows=256):
    total, width = mid.shape
    ff = act.shape[1]
    blk = lambda w: pl.BlockSpec((rows, w), lambda i: (i, 0))
    packed = updown.reshape(GROUPS, width // GROUPS, 2 * ff)
    return pl.pallas_call(
        mixed_kernel,
        grid=(total // rows,),
        in_specs=[pl.BlockSpec(memory_space=pltpu.SMEM), blk(ff), blk(width), full(vec.shape),
                  pl.BlockSpec((GROUPS, width // GROUPS, ff), lambda i: (0, 0, 1), pipeline_mode=pl.Buffered(buffer_count=1))],
        out_specs=blk(width),
        out_shape=jax.ShapeDtypeStruct((total, width), BF),
        scratch_shapes=[pltpu.VMEM((ff, width), BF)],
        compiler_params=params(),
        cost_estimate=cost(2 * total * width * ff, 14 * total * width),
        name="mixed",
    )(counts, act, mid, vec, packed)


CORE = [(i, i ^ 1) for i in range(16)]
ACROSS = [(i, i ^ 2) for i in range(16)]
ALONG = [[(i, ((i // 4 + k) % 4) * 4 + i % 4) for i in range(16)] for k in range(4)]
SWAP = [(0, 1), (1, 0)]


def permute(v, pairs):
    return lax.ppermute(v, "fsdp", pairs)


def gather_pieces(hier, shard):
    if not hier:
        whole = lax.all_gather(shard, "fsdp", axis=0, tiled=True)
        whole = whole.reshape(4, 2, 2, whole.shape[0] // GROUPS, whole.shape[1])
        order = jnp.concatenate([whole[:1], whole[3:0:-1]], axis=0).transpose(2, 1, 0, 3, 4)
        return order[0].reshape((8,) + order.shape[3:]), order[1].reshape((8,) + order.shape[3:])
    along = [shard] + [permute(shard, ALONG[k]) for k in (1, 2, 3)]
    mine = jnp.stack(along + [permute(v, ACROSS) for v in along])
    return mine, permute(mine, CORE)


def add_low(a, b):
    return (a.astype(F32) + b.astype(F32)).astype(BF)


def over_rep(shard):
    low = shard.astype(BF)
    return low.astype(F32) + lax.ppermute(low, "rep", SWAP).astype(F32)


def scatter_pieces(hier, near, far):
    if not hier:
        blocks = jnp.stack([near, far]).transpose(2, 1, 0, 3, 4)
        blocks = blocks.reshape(-1, blocks.shape[-1])
        return lax.psum_scatter(blocks, "fsdp", scatter_dimension=0, tiled=True).astype(F32)
    got = permute(far, CORE)
    there = permute(add_low(near[1], got[1]), ACROSS)
    here = add_low(near[0], got[0])
    parts = [add_low(here[k], there[k]) for k in range(4)]
    total = parts[0].astype(F32)
    for k in (1, 2, 3):
        total = total + permute(parts[k], ALONG[k]).astype(F32)
    return total


def local(hier, tokens, counts, cotangent, first_gain, first_shift, in_proj, query_bias, value_bias, out_proj, out_bias,
          second_gain, second_shift, up_proj, hidden_bias, down_proj, down_bias):
    images, rows, width = tokens.shape
    own = first_gain.shape[0]
    ff = 4 * width
    x = tokens.reshape(images * rows, width)
    cot = cotangent.reshape(images * rows, width)
    columns = jnp.concatenate([first_gain, first_shift, query_bias, jnp.zeros_like(query_bias), value_bias, out_bias,
                               second_gain, second_shift, down_bias, hidden_bias]).reshape(13, own).T
    pack = jnp.concatenate([in_proj, out_proj, columns, jnp.zeros((own, 115), BF)], axis=1)
    mine, other = gather_pieces(hier, pack)
    updown = jnp.concatenate([up_proj] + [down_proj[j * own:(j + 1) * own] for j in range(4)], axis=1)
    updown = lax.all_gather(updown, "fsdp", axis=0, tiled=True)
    qkv, probs, att, mid, sec, back, db, vec = attn_fwd(hier, counts, x, cot, mine, other)
    owners = width // own
    bias = vec[9:13].reshape(4, owners, own).transpose(1, 0, 2).reshape(1, ff)
    if not hier:
        updown = regroup(updown, own)
    act, hg, dg, ug, hb = mlp(sec, back, bias, updown)
    scatter = lambda v: lax.psum_scatter(v, "fsdp", scatter_dimension=0, tiled=True)
    dg = scatter(dg)
    ug = scatter(ug)
    mg, qg, og, sums = attn_bwd(hier, hg, mid, back, att, qkv, probs, vec, updown, mine, other)
    hid = hb.reshape(owners, 4, own).transpose(1, 0, 2).reshape(4, width)
    near, far = in_grad(hier, x, qg, og, db, sums, hid, mine, other)
    tg = tokens_grad(hier, x, qg, mg, vec, mine, other)
    mix = mixed_out(counts, act, mid, vec, updown)
    wide = over_rep(scatter_pieces(hier, near, far))
    ug, dg = over_rep(ug), over_rep(dg)
    cols = wide[:, 4 * width:].T
    return (mix.reshape(tokens.shape), tg.reshape(tokens.shape), cols[10], cols[11], wide[:, :3 * width], cols[4], cols[5],
            wide[:, 3 * width:4 * width], cols[3], cols[1], cols[2], ug, cols[6:10].reshape(4 * own), dg, cols[0])


def regroup(updown, own):
    width = updown.shape[0]
    ff = 4 * width
    part = width // GROUPS
    down = updown[:, ff:].reshape(width // own, own, 4, width).transpose(0, 2, 1, 3).reshape(GROUPS, 4, part, width)
    return jnp.concatenate([updown[:, :ff], down.transpose(0, 2, 1, 3).reshape(width, ff)], axis=1)


def solution(mesh):
    rows = P(("fsdp", "rep"), None, None)
    v, m = P("fsdp"), P("fsdp", None)
    in_specs = (rows, P(("fsdp", "rep")), rows, v, v, m, v, v, m, v, v, v, m, v, m, v)
    out_specs = (rows, rows, v, v, m, v, v, m, v, v, v, m, v, m, v)
    hier = mesh.shape["fsdp"] == GROUPS and mesh.shape["rep"] == 2
    return jax.shard_map(functools.partial(local, hier), mesh=mesh, in_specs=in_specs, out_specs=out_specs, check_vma=False)
```

```python
import functools
import jax
import jax.numpy as jnp
from jax import lax
from jax.experimental import pallas as pl
from jax.experimental.pallas import tpu as pltpu
from jax.sharding import PartitionSpec as P

HEADS = 12
HEAD = 64
EPS = 1e-06
BF = jnp.bfloat16
F32 = jnp.float32
VMEM = 60 << 20


def dot(a, b):
    return jnp.dot(a, b, preferred_element_type=F32)


def dot_rt(a, b):
    return lax.dot_general(a, b, (((1,), (1,)), ((), ())), preferred_element_type=F32)


def dot_lt(a, b):
    return lax.dot_general(a, b, (((0,), (0,)), ((), ())), preferred_element_type=F32)


def norm_stats(v):
    center = v - jnp.mean(v, axis=-1, keepdims=True)
    inv = lax.rsqrt(jnp.mean(center * center, axis=-1, keepdims=True) + EPS)
    return center, inv


def params(**kw):
    return pltpu.CompilerParams(vmem_limit_bytes=VMEM, **kw)


def full(shape):
    zeros = (0,) * len(shape)
    return pl.BlockSpec(shape, lambda *_: zeros, pipeline_mode=pl.Buffered(buffer_count=1))


def columns_of(rows, block, width):
    return pl.BlockSpec((rows, width), lambda *_: (0, block), pipeline_mode=pl.Buffered(buffer_count=1))


def pack_mlp_kernel(up, down, o_ref):
    rows, ff = up.shape
    width = ff // 4
    o_ref[:, :ff] = up[...]
    for j in range(4):
        o_ref[:, ff + j * width:ff + (j + 1) * width] = down[j * rows:(j + 1) * rows]


def pack_mlp(up, down):
    rows, ff = up.shape
    vm = pl.BlockSpec(memory_space=pltpu.VMEM)
    return pl.pallas_call(
        pack_mlp_kernel,
        in_specs=[vm, vm],
        out_specs=vm,
        out_shape=jax.ShapeDtypeStruct((rows, 2 * ff), BF),
        compiler_params=params(),
        name="pack_mlp",
    )(up, down)


def split_heads(pair, left):
    zero = jnp.zeros_like(pair)
    return jnp.concatenate([jnp.where(left, pair, zero), jnp.where(left, zero, pair)], axis=0)


def cost(flops, nbytes):
    return pl.CostEstimate(flops=int(flops), bytes_accessed=int(nbytes), transcendentals=0)


GROUPS = 16


def position(hier):
    if not hier:
        return 0, 0, 0
    me = lax.axis_index("fsdp")
    return me // 4, (me // 2) % 2, me % 2


def owner(hier, pos, k, other_x, other_c):
    if not hier:
        return (k * 2 + other_x) * 2 + other_c
    z, x, c = pos
    z = lax.rem(z + k, 4)
    x = 1 - x if other_x else x
    c = 1 - c if other_c else c
    return (z * 2 + x) * 2 + c


def rows_of(slot, rows):
    return pl.ds(pl.multiple_of(slot * rows, rows), rows)


def piece_copies(hier, mine, other, w_ref, sems, cols):
    pos = position(hier)
    out = []
    for c, ref in enumerate((mine, other)):
        for x in range(2):
            for k in range(4):
                slot = owner(hier, pos, (4 - k) % 4, x, c)
                out.append(pltpu.make_async_copy(ref.at[x * 4 + k, :, cols], w_ref.at[rows_of(slot, ref.shape[1])], sems.at[len(out)]))
    return out


def run_copies(copies):
    for copy in copies:
        copy.start()
    for copy in copies:
        copy.wait()


def pack_kernel(*refs):
    *vectors, hidden, in_proj, out_proj, o_ref = refs
    rows = o_ref.shape[0]
    wide = in_proj.shape[1] + out_proj.shape[1]
    o_ref[:, :in_proj.shape[1]] = in_proj[...]
    o_ref[:, in_proj.shape[1]:wide] = out_proj[...]
    lines = [v[...].astype(F32).reshape(1, rows) for v in vectors]
    lines.insert(3, jnp.zeros((1, rows), F32))
    hidden = hidden[...].astype(F32).reshape(1, 4 * rows)
    lines += [hidden[:, j * rows:(j + 1) * rows] for j in range(4)] + [jnp.zeros((115, rows), F32)]
    o_ref[:, wide:] = jnp.concatenate(lines, axis=0).T.astype(BF)


def pack(vectors, hidden, in_proj, out_proj):
    rows = in_proj.shape[0]
    vm = pl.BlockSpec(memory_space=pltpu.VMEM)
    return pl.pallas_call(
        pack_kernel,
        in_specs=[vm] * (len(vectors) + 3),
        out_specs=vm,
        out_shape=jax.ShapeDtypeStruct((rows, in_proj.shape[1] + out_proj.shape[1] + 128), BF),
        compiler_params=params(),
        name="pack",
    )(*vectors, hidden, in_proj, out_proj)


def pair_cols(width, p):
    return [slice(j * width + p * 128, j * width + (p + 1) * 128) for j in range(3)]


def attn_fwd_kernel(chunk, hier, counts, x_ref, cot_ref, mine, other,
                    qkv_ref, probs_ref, att_ref, mid_ref, sec_ref, back_ref, db_ref, vec, w_ref, sems):
    step = pl.program_id(0)
    rows, width = x_ref.shape
    per = rows // 64

    @pl.when(step == 0)
    def _():
        run_copies(piece_copies(hier, mine, other, w_ref, sems, slice(None)))
        vec[...] = w_ref[:, 4 * width:].astype(F32).T[:16]
        db_ref[...] = jnp.zeros_like(db_ref)

    left = lax.broadcasted_iota(jnp.int32, (64, 128), 1) < HEAD
    row = lax.broadcasted_iota(jnp.int32, (64, 128), 0)
    pos = lax.broadcasted_iota(jnp.int32, (64, width), 0)

    def project(at):
        center, inv = norm_stats(x_ref[at].astype(F32))
        first = (center * inv * vec[0:1] + vec[1:2]).astype(BF)
        for j in range(3):
            cols = slice(j * width, (j + 1) * width)
            qkv_ref[at, cols] = (dot(first, w_ref[:, cols]) + vec[2 + j:3 + j]).astype(BF)

    def attend(at):
        work = []
        for i in range(at.start // 64, at.stop // 64):
            here = slice(i * 64, (i + 1) * 64)
            work += [(i, here, row <= counts[step * per + i], pair_cols(width, p), p) for p in range(HEADS // 2)]
        scores = [dot_rt(qkv_ref[here, c[1]], split_heads(qkv_ref[here, c[0]], left)) for i, here, usable, c, p in work]
        lows = []
        for (i, here, usable, c, p), s in zip(work, scores):
            s = jnp.where(usable, s * 0.125, -1000000000.0)
            e = jnp.exp(s - jnp.max(s, axis=0, keepdims=True))
            low = (e * (1.0 / jnp.sum(e, axis=0, keepdims=True))).astype(BF)
            probs_ref[i, p] = low
            lows.append(low)
        for (i, here, usable, c, p), low in zip(work, lows):
            o = dot_lt(low, qkv_ref[here, c[2]])
            att_ref[here, c[0]] = jnp.where(left, o[:64], o[64:]).astype(BF)

    def output(at):
        mid = x_ref[at].astype(F32) + dot(att_ref[at], w_ref[:, 3 * width:4 * width]) + vec[5:6]
        mid_ref[at] = mid
        center, inv = norm_stats(mid)
        sec_ref[at] = (center * inv * vec[6:7] + vec[7:8]).astype(BF)

    chunks = [slice(r, r + chunk) for r in range(0, rows, chunk)]
    project(chunks[0])
    for c, at in enumerate(chunks):
        if c + 1 < len(chunks):
            project(chunks[c + 1])
        attend(at)
        output(at)
    total = jnp.zeros((1, width), F32)
    for i in range(per):
        at = slice(i * 64, (i + 1) * 64)
        back = jnp.where(pos <= counts[step * per + i], cot_ref[at].astype(F32), 0.0)
        back_ref[at] = back.astype(BF)
        total = total + jnp.sum(back, axis=0, keepdims=True)
    db_ref[...] += total


ANY = pl.BlockSpec(memory_space=pl.ANY)


def attn_fwd(hier, counts, x, cot, mine, other, rows=512, chunk=256):
    total, width = x.shape
    per = rows // 64
    blk = lambda w: pl.BlockSpec((rows, w), lambda i: (i, 0))
    return pl.pallas_call(
        functools.partial(attn_fwd_kernel, chunk, hier),
        grid=(total // rows,),
        in_specs=[pl.BlockSpec(memory_space=pltpu.SMEM), blk(width), blk(width), ANY, ANY],
        out_specs=[blk(3 * width), pl.BlockSpec((per, HEADS // 2, 64, 128), lambda i: (i, 0, 0, 0)),
                   blk(width), blk(width), blk(width), blk(width), pl.BlockSpec((1, width), lambda i: (0, 0)),
                   pl.BlockSpec((16, width), lambda i: (0, 0))],
        out_shape=[jax.ShapeDtypeStruct((total, 3 * width), BF),
                   jax.ShapeDtypeStruct((total // 64, HEADS // 2, 64, 128), BF),
                   jax.ShapeDtypeStruct((total, width), BF),
                   jax.ShapeDtypeStruct((total, width), F32),
                   jax.ShapeDtypeStruct((total, width), BF),
                   jax.ShapeDtypeStruct((total, width), BF),
                   jax.ShapeDtypeStruct((1, width), F32),
                   jax.ShapeDtypeStruct((16, width), F32)],
        scratch_shapes=[pltpu.VMEM((width, mine.shape[2]), BF), pltpu.SemaphoreType.DMA((GROUPS,))],
        compiler_params=params(),
        cost_estimate=cost(8 * total * width * width * 1.5, 20 * total * width),
        name="attn_fwd",
    )(counts, x, cot, mine, other)


def gelu_parts(h):
    cdf = 0.5 + 0.5 * lax.erf(h * 0.7071067811865476)
    pdf = jnp.exp(h * h * -0.5) * 0.3989422804014327
    return (h * cdf).astype(BF), cdf + h * pdf


def whole_rows(packed):
    owners, rows, four = packed.shape
    width = four // 4
    return jnp.concatenate([packed[o, :, j * width:(j + 1) * width] for o in range(owners) for j in range(4)], axis=0)


def mlp_kernel(chunk, sec_ref, back_ref, bias_ref, up, down, act_ref, hg_ref, hb_ref, g_hbm, ug_ref, dg_ref, g_sems):
    step = pl.program_id(0)
    last = pl.num_programs(0) - 1
    rows, width = sec_ref.shape
    owners, part, ff = dg_ref.shape
    down = whole_rows(down)
    sums = jnp.zeros((8, width), F32)
    for r in range(rows // chunk):
        at = slice(r * chunk, (r + 1) * chunk)
        act, slope = gelu_parts(dot(sec_ref[at], up[...]) + bias_ref[...])
        act_ref[at] = act
        hg = (dot_rt(back_ref[at], down) * slope).astype(BF)
        hg_ref[at] = hg
        sums = sums + jnp.sum(hg.astype(F32).reshape(chunk // 8, 8, -1), axis=0)
    hb_ref[...] = jnp.sum(sums, axis=0, keepdims=True)

    def outputs(s):
        at = pl.ds(pl.multiple_of(s * width, width), width)
        return (pltpu.make_async_copy(dg_ref, g_hbm.at[pl.ds(s * owners, owners), :, ff:], g_sems.at[0]),
                pltpu.make_async_copy(ug_ref, g_hbm.at[:, :, at], g_sems.at[1]))

    @pl.when(step > 0)
    def _():
        for copy in outputs(step - 1):
            copy.wait()

    dg = dot_lt(act_ref[...], back_ref[...]).astype(BF)
    for o in range(owners):
        for j in range(4):
            dg_ref[o, :, j * width:(j + 1) * width] = dg[(o * 4 + j) * part:(o * 4 + j + 1) * part]
    outputs(step)[0].start()
    ug_ref[...] = dot_lt(sec_ref[...], hg_ref[...]).astype(BF).reshape(ug_ref.shape)
    outputs(step)[1].start()

    @pl.when(step == last)
    def _():
        for copy in outputs(step):
            copy.wait()


def mlp(sec, back, bias, updown, chunk=256):
    total, width = sec.shape
    ff = bias.shape[1]
    f = width
    part = width // GROUPS
    owners = GROUPS * f // ff
    col = lambda r: pl.BlockSpec((r, f), lambda i: (0, i))
    return pl.pallas_call(
        functools.partial(mlp_kernel, chunk),
        grid=(ff // f,),
        in_specs=[full(sec.shape), full(back.shape), col(1), col(width),
                  pl.BlockSpec((owners, part, ff), lambda i: (i, 0, 1))],
        out_specs=[col(total), col(total), col(1), ANY],
        out_shape=[jax.ShapeDtypeStruct((total, ff), BF), jax.ShapeDtypeStruct((total, ff), BF),
                   jax.ShapeDtypeStruct((1, ff), F32), jax.ShapeDtypeStruct((GROUPS, part, 2 * ff), BF)],
        scratch_shapes=[pltpu.VMEM((GROUPS, part, f), BF), pltpu.VMEM((owners, part, ff), BF), pltpu.SemaphoreType.DMA((2,))],
        compiler_params=params(),
        cost_estimate=cost(8 * total * width * ff, 12 * total * width),
        name="mlp",
    )(sec, back, bias, updown, updown.reshape(GROUPS, part, 2 * ff))


def attn_bwd_kernel(chunk, hier, hg_ref, mid_ref, back_ref, att_ref, qkv_ref, probs_ref, vec, up, mine, other,
                    mg_ref, qg_ref, og_ref, sums_ref, acc, ag_ref, w_out, sems):
    step = pl.program_id(0)
    rows, width = mid_ref.shape

    @pl.when(step == 0)
    def _():
        copies = piece_copies(hier, mine, other, w_out, sems, slice(3 * width, 4 * width))
        for copy in copies:
            copy.start()
        acc[...] = jnp.zeros_like(acc)
        sums_ref[...] = jnp.zeros_like(sums_ref)
        for copy in copies:
            copy.wait()

    left = lax.broadcasted_iota(jnp.int32, (64, 128), 1) < HEAD

    def through_norm(at):
        sg = dot_rt(hg_ref[at], up[...])
        center, inv = norm_stats(mid_ref[at])
        n = center * inv
        e = sg * vec[6:7]
        sums_ref[0:1] += jnp.sum(sg * n, axis=0, keepdims=True)
        sums_ref[1:2] += jnp.sum(sg, axis=0, keepdims=True)
        norm_grad = inv * (e - jnp.mean(e, axis=-1, keepdims=True) - n * jnp.mean(e * n, axis=-1, keepdims=True))
        mg = back_ref[at].astype(F32) + norm_grad
        mg_ref[at] = mg
        sums_ref[2:3] += jnp.sum(mg, axis=0, keepdims=True)
        low = mg.astype(BF)
        ag_ref[at] = dot_rt(low, w_out[...]).astype(BF)
        return low

    def attend(at):
        work = []
        for i in range(at.start // 64, at.stop // 64):
            work += [(i, slice(i * 64, (i + 1) * 64), pair_cols(width, p), p) for p in range(HEADS // 2)]
        dps = []
        for i, here, c, p in work:
            da = split_heads(ag_ref[here, c[0]], left)
            qg_ref[here, c[2]] = dot(probs_ref[i, p], da).astype(BF)
            dps.append(dot_rt(qkv_ref[here, c[2]], da))
        dss = []
        for (i, here, c, p), dp in zip(work, dps):
            pr = probs_ref[i, p].astype(F32)
            t = dp * pr
            dss.append((t - pr * jnp.sum(t, axis=0, keepdims=True)).astype(BF))
        for (i, here, c, p), ds in zip(work, dss):
            qg_ref[here, c[1]] = (dot(ds, split_heads(qkv_ref[here, c[0]], left)) * 0.125).astype(BF)
            dq = dot_lt(ds, qkv_ref[here, c[1]])
            qg_ref[here, c[0]] = (jnp.where(left, dq[:64], dq[64:]) * 0.125).astype(BF)

    chunks = [slice(r, r + chunk) for r in range(0, rows, chunk)]
    lows = [through_norm(chunks[0])]
    for c, at in enumerate(chunks):
        if c + 1 < len(chunks):
            lows.append(through_norm(chunks[c + 1]))
        attend(at)
    acc[...] += dot_lt(att_ref[...], jnp.concatenate(lows, axis=0))

    @pl.when(step == pl.num_programs(0) - 1)
    def _():
        og_ref[...] = acc[...].astype(BF)


def attn_bwd(hier, hg, mid, back, att, qkv, probs, vec, updown, mine, other, rows=512, chunk=256):
    total, width = mid.shape
    ff = hg.shape[1]
    per = rows // 64
    blk = lambda w: pl.BlockSpec((rows, w), lambda i: (i, 0))
    one = lambda s: pl.BlockSpec(s, lambda i: (0, 0))
    return pl.pallas_call(
        functools.partial(attn_bwd_kernel, chunk, hier),
        grid=(total // rows,),
        in_specs=[blk(ff), blk(width), blk(width), blk(width), blk(3 * width),
                  pl.BlockSpec((per, HEADS // 2, 64, 128), lambda i: (i, 0, 0, 0)),
                  full(vec.shape), columns_of(width, 0, ff), ANY, ANY],
        out_specs=[blk(width), blk(3 * width), one((width, width)), one((8, width))],
        out_shape=[jax.ShapeDtypeStruct((total, width), F32), jax.ShapeDtypeStruct((total, 3 * width), BF),
                   jax.ShapeDtypeStruct((width, width), BF), jax.ShapeDtypeStruct((8, width), F32)],
        scratch_shapes=[pltpu.VMEM((width, width), F32), pltpu.VMEM((rows, width), BF),
                        pltpu.VMEM((width, width), BF), pltpu.SemaphoreType.DMA((GROUPS,))],
        compiler_params=params(),
        cost_estimate=cost(2 * total * width * (ff + 6 * width), 24 * total * width),
        name="attn_bwd",
    )(hg, mid, back, att, qkv, probs, vec, updown, mine, other)


def in_grad_kernel(hier, x_ref, qg_hbm, og_ref, db_ref, sums_ref, hid_ref, mine, other,
                   near_ref, far_ref, n_ref, qg_ref, w_ref, block, sems, qg_sems):
    total, width = x_ref.shape
    pos = position(hier)
    weights = piece_copies(hier, mine, other, w_ref, sems, slice(None))
    loads = [pltpu.make_async_copy(qg_hbm.at[:, j * width:(j + 1) * width], qg_ref.at[j], qg_sems.at[j]) for j in range(3)]
    for copy in loads + weights:
        copy.start()

    def place(cols):
        for far, ref in enumerate((near_ref, far_ref)):
            for x in range(2):
                for k in range(4):
                    ref[x, k, :, cols] = block[owner(hier, pos, k, x, far), :, :cols.stop - cols.start]

    for r in range(0, total, 256):
        center, inv = norm_stats(x_ref[r:r + 256].astype(F32))
        n_ref[r:r + 256] = (center * inv).astype(BF)
    for copy in weights:
        copy.wait()
    vec = w_ref[:, 4 * width:].astype(F32)
    gain, shift = vec[:, 0:1], vec[:, 1:2]
    gain_grad = jnp.zeros((width, 1), F32)
    shift_grad = jnp.zeros((width, 1), F32)
    colsums = []
    for j in range(3):
        loads[j].wait()
        cols = slice(j * width, (j + 1) * width)
        m = dot_lt(n_ref[...], qg_ref[j])
        cs = jnp.sum(qg_ref[j].astype(F32), axis=0, keepdims=True)
        colsums.append(cs)
        w = w_ref[:, cols].astype(F32)
        gain_grad = gain_grad + jnp.sum(w * m, axis=1, keepdims=True)
        shift_grad = shift_grad + jnp.sum(w * cs, axis=1, keepdims=True)
        block[...] = (gain * m + shift * cs).astype(BF).reshape(block.shape)
        place(cols)
    block[...] = og_ref[...].reshape(block.shape)
    place(slice(3 * width, 4 * width))
    rows = jnp.concatenate([db_ref[...], sums_ref[0:3], colsums[0], colsums[2], jnp.zeros((6, width), F32), hid_ref[...],
                            jnp.zeros((112, width), F32)])
    lane = lax.broadcasted_iota(jnp.int32, (width, 128), 1)
    tail = jnp.where(lane == 10, gain_grad, jnp.where(lane == 11, shift_grad, rows.T))
    block[:, :, :128] = tail.astype(BF).reshape(block.shape[0], block.shape[1], 128)
    place(slice(4 * width, 4 * width + 128))


def in_grad(hier, x, qg, og, db, sums, hid, mine, other):
    total, width = x.shape
    rows = width // GROUPS
    wide = 4 * width + 128
    vm = pl.BlockSpec(memory_space=pltpu.VMEM)
    return pl.pallas_call(
        functools.partial(in_grad_kernel, hier),
        in_specs=[vm, ANY, vm, vm, vm, vm, ANY, ANY],
        out_specs=[vm, vm],
        out_shape=[jax.ShapeDtypeStruct((2, 4, rows, wide), BF)] * 2,
        scratch_shapes=[pltpu.VMEM((total, width), BF), pltpu.VMEM((3, total, width), BF), pltpu.VMEM((width, wide), BF),
                        pltpu.VMEM((GROUPS, rows, width), BF), pltpu.SemaphoreType.DMA((GROUPS,)), pltpu.SemaphoreType.DMA((3,))],
        compiler_params=params(),
        cost_estimate=cost(6 * total * width * width, 8 * total * width),
        name="in_grad",
    )(x, qg, og, db, sums, hid, mine, other)


def tokens_grad_kernel(hier, x_ref, qg_ref, mg_ref, vec, mine, other, tie, old, o_ref, w_ref, sems):
    @pl.when(pl.program_id(0) == 0)
    def _():
        run_copies(piece_copies(hier, mine, other, w_ref, sems, slice(0, w_ref.shape[1])))

    center, inv = norm_stats(x_ref[...].astype(F32))
    n = center * inv
    e = dot_rt(qg_ref[...], w_ref[...]) * vec[0:1]
    grad = inv * (e - jnp.mean(e, axis=-1, keepdims=True) - n * jnp.mean(e * n, axis=-1, keepdims=True))
    o_ref[...] = (mg_ref[...] + grad).astype(BF)


def part_of(total, rows, part, parts, width):
    first = part * (total // rows // parts)
    return pl.BlockSpec((rows, width), lambda i: (first + i, 0))


def tokens_grad(hier, part, parts, x, qg, mg, vec, mine, other, tie, old, rows=256):
    total, width = x.shape
    blk = lambda w: part_of(total, rows, part, parts, w)
    return pl.pallas_call(
        functools.partial(tokens_grad_kernel, hier),
        grid=(total // rows // parts,),
        in_specs=[blk(width), blk(3 * width), blk(width), full(vec.shape), ANY, ANY, ANY, ANY],
        out_specs=blk(width),
        out_shape=jax.ShapeDtypeStruct((total, width), BF),
        scratch_shapes=[pltpu.VMEM((width, 3 * width), BF), pltpu.SemaphoreType.DMA((GROUPS,))],
        input_output_aliases={7: 0} if part else {},
        compiler_params=params(),
        cost_estimate=cost(6 * total * width * width // parts, 14 * total * width // parts),
        name="tokens_grad",
    )(x, qg, mg, vec, mine, other, tie, old)


def mixed_kernel(first, counts, act_ref, mid_ref, vec, down, tie, old, o_ref):
    step = pl.program_id(0)
    per = o_ref.shape[0] // 64
    r = mid_ref[...] + dot(act_ref[...], whole_rows(down)) + vec[8:9]
    pos = lax.broadcasted_iota(jnp.int32, (64, o_ref.shape[1]), 0)
    for i in range(per):
        count = counts[(first + step) * per + i]
        o_ref[i * 64:(i + 1) * 64] = jnp.where(pos <= count, r[i * 64:(i + 1) * 64], 0.0).astype(BF)


def mixed_out(part, parts, counts, act, mid, vec, updown, tie, old, rows=256):
    total, width = mid.shape
    ff = act.shape[1]
    blk = lambda w: part_of(total, rows, part, parts, w)
    packed = updown.reshape(GROUPS, width // GROUPS, 2 * ff)
    return pl.pallas_call(
        functools.partial(mixed_kernel, part * (total // rows // parts)),
        grid=(total // rows // parts,),
        in_specs=[pl.BlockSpec(memory_space=pltpu.SMEM), blk(ff), blk(width), full(vec.shape),
                  pl.BlockSpec((GROUPS, width // GROUPS, ff), lambda i: (0, 0, 1), pipeline_mode=pl.Buffered(buffer_count=1)), ANY, ANY],
        out_specs=blk(width),
        out_shape=jax.ShapeDtypeStruct((total, width), BF),
        input_output_aliases={6: 0} if part else {},
        compiler_params=params(),
        cost_estimate=cost(2 * total * width * ff // parts, 14 * total * width // parts),
        name="mixed",
    )(counts, act, mid, vec, packed, tie, old)


def core_sum_kernel(near, got, tie, here, there):
    total = near[...].astype(F32) + got[...].astype(F32)
    here[0] = total[0, 0].astype(BF)
    there[0] = total[1, 0].astype(BF)


def core_sum(near, got, tie):
    _, along, rows, wide = near.shape
    blk = pl.BlockSpec((2, 1, rows, wide), lambda i: (0, i, 0, 0))
    out = pl.BlockSpec((1, rows, wide), lambda i: (i, 0, 0))
    return pl.pallas_call(
        core_sum_kernel,
        grid=(along,),
        in_specs=[blk, blk, ANY],
        out_specs=[out, out],
        out_shape=[jax.ShapeDtypeStruct((along, rows, wide), BF)] * 2,
        compiler_params=params(),
        name="core_sum",
    )(near, got, tie)


def across_sum_kernel(here, there, tie, *outs):
    for k, o_ref in enumerate(outs):
        o_ref[...] = (here[k].astype(F32) + there[k].astype(F32)).astype(BF)


def across_sum(here, there, tie):
    along, rows, wide = here.shape
    vm = pl.BlockSpec(memory_space=pltpu.VMEM)
    return pl.pallas_call(
        across_sum_kernel,
        in_specs=[vm, vm, ANY],
        out_specs=[vm] * along,
        out_shape=[jax.ShapeDtypeStruct((rows, wide), BF)] * along,
        compiler_params=params(),
        name="across_sum",
    )(here, there, tie)


def along_sum_kernel(a, b, c, d, tie, o_ref):
    total = (a[...].astype(F32) + b[...].astype(F32)) + (c[...].astype(F32) + d[...].astype(F32))
    o_ref[...] = total.astype(BF)


def along_sum(a, b, c, d, tie):
    vm = pl.BlockSpec(memory_space=pltpu.VMEM)
    return pl.pallas_call(
        along_sum_kernel,
        in_specs=[vm] * 4 + [ANY],
        out_specs=vm,
        out_shape=jax.ShapeDtypeStruct(a.shape, BF),
        compiler_params=params(),
        name="along_sum",
    )(a, b, c, d, tie)


def finish_kernel(a_ref, b_ref, in_ref, out_ref, *vectors):
    rows = a_ref.shape[0]
    total = a_ref[...].astype(F32) + b_ref[...].astype(F32)
    wide = in_ref.shape[1] + out_ref.shape[1]
    in_ref[...] = total[:, :in_ref.shape[1]]
    out_ref[...] = total[:, in_ref.shape[1]:wide]
    lines = total[:, wide:].T
    for i, v in enumerate(vectors[:-1]):
        v[...] = lines[i:i + 1].reshape(rows)
    vectors[-1][...] = lines[12:16]


def finish(a, b, width):
    rows = a.shape[0]
    vm = pl.BlockSpec(memory_space=pltpu.VMEM)
    return pl.pallas_call(
        finish_kernel,
        in_specs=[vm, vm],
        out_specs=[vm] * 15,
        out_shape=[jax.ShapeDtypeStruct((rows, 3 * width), F32), jax.ShapeDtypeStruct((rows, width), F32)]
        + [jax.ShapeDtypeStruct((rows,), F32)] * 12 + [jax.ShapeDtypeStruct((4, rows), F32)],
        compiler_params=params(),
        name="finish",
    )(a, b)


CORE = [(i, i ^ 1) for i in range(16)]
ACROSS = [(i, i ^ 2) for i in range(16)]
ALONG = [[(i, ((i // 4 + k) % 4) * 4 + i % 4) for i in range(16)] for k in range(4)]
SWAP = [(0, 1), (1, 0)]


def permute(v, pairs):
    return lax.ppermute(v, "fsdp", pairs)


def gather_along(shard):
    return [shard] + [permute(shard, ALONG[k]) for k in (1, 3, 2)]


def gather_across(along):
    along = [along[0], along[1], along[3], along[2]]
    mine = jnp.stack(along + [permute(v, ACROSS) for v in along])
    return mine, permute(mine, CORE)


def gather_whole(shard):
    whole = lax.all_gather(shard, "fsdp", axis=0, tiled=True)
    whole = whole.reshape(4, 2, 2, whole.shape[0] // GROUPS, whole.shape[1])
    order = jnp.concatenate([whole[:1], whole[3:0:-1]], axis=0).transpose(2, 1, 0, 3, 4)
    return order[0].reshape((8,) + order.shape[3:]), order[1].reshape((8,) + order.shape[3:])


def regroup(updown, own):
    width = updown.shape[0]
    ff = 4 * width
    down = updown[:, ff:].reshape(width // own, own, 4, width).transpose(0, 2, 1, 3).reshape(GROUPS, 4, width // GROUPS, width)
    return jnp.concatenate([updown[:, :ff], down.transpose(0, 2, 1, 3).reshape(width, ff)], axis=1)


def over_rep(shard):
    low = shard.astype(BF)
    return low, lax.ppermute(low, "rep", SWAP)


def local(hier, tokens, counts, cotangent, first_gain, first_shift, in_proj, query_bias, value_bias, out_proj, out_bias,
          second_gain, second_shift, up_proj, hidden_bias, down_proj, down_bias):
    images, rows, width = tokens.shape
    own = first_gain.shape[0]
    ff = 4 * width
    x = tokens.reshape(images * rows, width)
    cot = cotangent.reshape(images * rows, width)
    vectors = (first_gain, first_shift, query_bias, value_bias, out_bias, second_gain, second_shift, down_bias)
    if hier:
        packed = pack(vectors, hidden_bias, in_proj, out_proj)
        mine, other = gather_across(gather_along(packed))
        updown = lax.all_gather(pack_mlp(up_proj, down_proj), "fsdp", axis=0, tiled=True)
    else:
        columns = jnp.concatenate(vectors[:3] + (jnp.zeros_like(query_bias),) + vectors[3:] + (hidden_bias,)).reshape(13, own).T
        packed = jnp.concatenate([in_proj, out_proj, columns, jnp.zeros((own, 115), BF)], axis=1)
        mine, other = gather_whole(packed)
        updown = jnp.concatenate([up_proj] + [down_proj[j * own:(j + 1) * own] for j in range(4)], axis=1)
        updown = regroup(lax.all_gather(updown, "fsdp", axis=0, tiled=True), own)
    qkv, probs, att, mid, sec, back, db, vec = attn_fwd(hier, counts, x, cot, mine, other)
    owners = width // own
    bias = vec[9:13].reshape(4, owners, own).transpose(1, 0, 2).reshape(1, ff)
    act, hg, hb, grads = mlp(sec, back, bias, updown)
    if not hier:
        dg = grads[:, :, ff:].reshape(GROUPS, width // GROUPS, 4, width).transpose(0, 2, 1, 3).reshape(owners, 4, own, width)
        grads = jnp.concatenate([grads[:, :, :ff].reshape(width, ff), dg.transpose(0, 2, 1, 3).reshape(width, ff)], axis=1)
    mlp_grads = lax.psum_scatter(grads.reshape(width, 2 * ff), "fsdp", scatter_dimension=0, tiled=True)
    mg, qg, og, sums = attn_bwd(hier, hg, mid, back, att, qkv, probs, vec, updown, mine, other)
    hid = hb.reshape(owners, 4, own).transpose(1, 0, 2).reshape(4, width)
    near, far = in_grad(hier, x, qg, og, db, sums, hid, mine, other)
    tok = lambda part, tie, old: tokens_grad(hier, part, 2, x, qg, mg, vec, mine, other, tie, old)
    mix = lambda part, tie, old: mixed_out(part, 2, counts, act, mid, vec, updown, tie, old)
    if hier:
        got = permute(far, CORE)
        mixed = mix(0, far, far)
        here, send = core_sum(near, got, mixed)
        there = permute(send, ACROSS)
        mixed = mix(1, send, mixed)
        toks = tok(0, mixed, mixed)
        parts = across_sum(here, there, toks)
        moved = [permute(parts[k], ALONG[k]) for k in (1, 2, 3)]
        toks = tok(1, parts[3], toks)
        low = along_sum(parts[0], *moved, toks)
    else:
        mixed = mix(1, far, mix(0, far, far))
        toks = tok(1, far, tok(0, far, far))
        blocks = jnp.stack([near, far]).transpose(2, 1, 0, 3, 4).reshape(width, near.shape[-1])
        low = lax.psum_scatter(blocks, "fsdp", scatter_dimension=0, tiled=True)
    a, b = over_rep(low)
    if hier:
        grad_in, grad_out, *lines, hidden = finish(a, b, width)
    else:
        wide = a.astype(F32) + b.astype(F32)
        grad_in, grad_out, lines = wide[:, :3 * width], wide[:, 3 * width:4 * width], wide[:, 4 * width:].T
        hidden = lines[12:16]
    a, b = over_rep(mlp_grads)
    mlp_grads = a.astype(F32) + b.astype(F32)
    grad_up = mlp_grads[:, :ff]
    grad_down = jnp.concatenate([mlp_grads[:, ff + j * width:ff + (j + 1) * width] for j in range(4)], axis=0)
    return (mixed.reshape(tokens.shape), toks.reshape(tokens.shape), lines[10], lines[11], grad_in, lines[4], lines[5],
            grad_out, lines[3], lines[1], lines[2], grad_up, hidden.reshape(4 * own), grad_down, lines[0])


def solution(mesh):
    rows = P(("fsdp", "rep"), None, None)
    v, m = P("fsdp"), P("fsdp", None)
    in_specs = (rows, P(("fsdp", "rep")), rows, v, v, m, v, v, m, v, v, v, m, v, m, v)
    out_specs = (rows, rows, v, v, m, v, v, m, v, v, v, m, v, m, v)
    hier = mesh.shape["fsdp"] == GROUPS and mesh.shape["rep"] == 2
    return jax.shard_map(functools.partial(local, hier), mesh=mesh, in_specs=in_specs, out_specs=out_specs, check_vma=False)
```

```python
import functools
import jax
import jax.numpy as jnp
from jax import lax
from jax.experimental import pallas as pl
from jax.experimental.pallas import tpu as pltpu
from jax.sharding import PartitionSpec as P

HEADS = 12
HEAD = 64
EPS = 1e-06
BF = jnp.bfloat16
F32 = jnp.float32
VMEM = 60 << 20


def dot(a, b):
    return jnp.dot(a, b, preferred_element_type=F32)


def dot_rt(a, b):
    return lax.dot_general(a, b, (((1,), (1,)), ((), ())), preferred_element_type=F32)


def dot_lt(a, b):
    return lax.dot_general(a, b, (((0,), (0,)), ((), ())), preferred_element_type=F32)


def norm_stats(v):
    center = v - jnp.mean(v, axis=-1, keepdims=True)
    inv = lax.rsqrt(jnp.mean(center * center, axis=-1, keepdims=True) + EPS)
    return center, inv


def params(**kw):
    return pltpu.CompilerParams(vmem_limit_bytes=VMEM, **kw)


def full(shape):
    zeros = (0,) * len(shape)
    return pl.BlockSpec(shape, lambda *_: zeros, pipeline_mode=pl.Buffered(buffer_count=1))


def columns_of(rows, block, width):
    return pl.BlockSpec((rows, width), lambda *_: (0, block), pipeline_mode=pl.Buffered(buffer_count=1))


def pack_mlp_kernel(up, down, o_ref):
    rows, ff = up.shape
    width = ff // 4
    o_ref[:, :ff] = up[...]
    for j in range(4):
        o_ref[:, ff + j * width:ff + (j + 1) * width] = down[j * rows:(j + 1) * rows]


def pack_mlp(up, down):
    rows, ff = up.shape
    vm = pl.BlockSpec(memory_space=pltpu.VMEM)
    return pl.pallas_call(
        pack_mlp_kernel,
        in_specs=[vm, vm],
        out_specs=vm,
        out_shape=jax.ShapeDtypeStruct((rows, 2 * ff), BF),
        compiler_params=params(),
        name="pack_mlp",
    )(up, down)


def split_heads(pair, left):
    zero = jnp.zeros_like(pair)
    return jnp.concatenate([jnp.where(left, pair, zero), jnp.where(left, zero, pair)], axis=0)


def cost(flops, nbytes):
    return pl.CostEstimate(flops=int(flops), bytes_accessed=int(nbytes), transcendentals=0)


GROUPS = 16


def position(hier):
    if not hier:
        return 0, 0, 0
    me = lax.axis_index("fsdp")
    return me // 4, (me // 2) % 2, me % 2


def owner(hier, pos, k, other_x, other_c):
    if not hier:
        return (k * 2 + other_x) * 2 + other_c
    z, x, c = pos
    z = lax.rem(z + k, 4)
    x = 1 - x if other_x else x
    c = 1 - c if other_c else c
    return (z * 2 + x) * 2 + c


def rows_of(slot, rows):
    return pl.ds(pl.multiple_of(slot * rows, rows), rows)


def piece_copies(hier, mine, other, w_ref, sems, cols):
    pos = position(hier)
    out = []
    for c, ref in enumerate((mine, other)):
        for x in range(2):
            for k in range(4):
                slot = owner(hier, pos, (4 - k) % 4, x, c)
                out.append(pltpu.make_async_copy(ref.at[x * 4 + k, :, cols], w_ref.at[rows_of(slot, ref.shape[1])], sems.at[len(out)]))
    return out


def run_copies(copies):
    for copy in copies:
        copy.start()
    for copy in copies:
        copy.wait()


def pack_kernel(*refs):
    *vectors, hidden, in_proj, out_proj, o_ref = refs
    rows = o_ref.shape[0]
    wide = in_proj.shape[1] + out_proj.shape[1]
    o_ref[:, :in_proj.shape[1]] = in_proj[...]
    o_ref[:, in_proj.shape[1]:wide] = out_proj[...]
    lines = [v[...].astype(F32).reshape(1, rows) for v in vectors]
    lines.insert(3, jnp.zeros((1, rows), F32))
    hidden = hidden[...].astype(F32).reshape(1, 4 * rows)
    lines += [hidden[:, j * rows:(j + 1) * rows] for j in range(4)] + [jnp.zeros((115, rows), F32)]
    o_ref[:, wide:] = jnp.concatenate(lines, axis=0).T.astype(BF)


def pack(vectors, hidden, in_proj, out_proj):
    rows = in_proj.shape[0]
    vm = pl.BlockSpec(memory_space=pltpu.VMEM)
    return pl.pallas_call(
        pack_kernel,
        in_specs=[vm] * (len(vectors) + 3),
        out_specs=vm,
        out_shape=jax.ShapeDtypeStruct((rows, in_proj.shape[1] + out_proj.shape[1] + 128), BF),
        compiler_params=params(),
        name="pack",
    )(*vectors, hidden, in_proj, out_proj)


def pair_cols(width, p):
    return [slice(j * width + p * 128, j * width + (p + 1) * 128) for j in range(3)]


def attn_fwd_kernel(chunk, hier, counts, x_ref, cot_ref, mine, other,
                    qkv_ref, probs_ref, att_ref, mid_ref, sec_ref, back_ref, db_ref, vec, w_ref, sems):
    step = pl.program_id(0)
    rows, width = x_ref.shape
    per = rows // 64

    @pl.when(step == 0)
    def _():
        run_copies(piece_copies(hier, mine, other, w_ref, sems, slice(None)))
        vec[...] = w_ref[:, 4 * width:].astype(F32).T[:16]
        db_ref[...] = jnp.zeros_like(db_ref)

    left = lax.broadcasted_iota(jnp.int32, (64, 128), 1) < HEAD
    row = lax.broadcasted_iota(jnp.int32, (64, 128), 0)
    pos = lax.broadcasted_iota(jnp.int32, (64, width), 0)

    def project(at):
        center, inv = norm_stats(x_ref[at].astype(F32))
        first = (center * inv * vec[0:1] + vec[1:2]).astype(BF)
        for j in range(3):
            cols = slice(j * width, (j + 1) * width)
            qkv_ref[at, cols] = (dot(first, w_ref[:, cols]) + vec[2 + j:3 + j]).astype(BF)

    def attend(at):
        work = []
        for i in range(at.start // 64, at.stop // 64):
            here = slice(i * 64, (i + 1) * 64)
            work += [(i, here, row <= counts[step * per + i], pair_cols(width, p), p) for p in range(HEADS // 2)]
        scores = [dot_rt(qkv_ref[here, c[1]], split_heads(qkv_ref[here, c[0]], left)) for i, here, usable, c, p in work]
        lows = []
        for (i, here, usable, c, p), s in zip(work, scores):
            s = jnp.where(usable, s * 0.125, -1000000000.0)
            e = jnp.exp(s - jnp.max(s, axis=0, keepdims=True))
            low = (e * (1.0 / jnp.sum(e, axis=0, keepdims=True))).astype(BF)
            probs_ref[i, p] = low
            lows.append(low)
        for (i, here, usable, c, p), low in zip(work, lows):
            o = dot_lt(low, qkv_ref[here, c[2]])
            att_ref[here, c[0]] = jnp.where(left, o[:64], o[64:]).astype(BF)

    def output(at):
        mid = x_ref[at].astype(F32) + dot(att_ref[at], w_ref[:, 3 * width:4 * width]) + vec[5:6]
        mid_ref[at] = mid
        center, inv = norm_stats(mid)
        sec_ref[at] = (center * inv * vec[6:7] + vec[7:8]).astype(BF)

    chunks = [slice(r, r + chunk) for r in range(0, rows, chunk)]
    project(chunks[0])
    for c, at in enumerate(chunks):
        if c + 1 < len(chunks):
            project(chunks[c + 1])
        attend(at)
        output(at)
    total = jnp.zeros((1, width), F32)
    for i in range(per):
        at = slice(i * 64, (i + 1) * 64)
        back = jnp.where(pos <= counts[step * per + i], cot_ref[at].astype(F32), 0.0)
        back_ref[at] = back.astype(BF)
        total = total + jnp.sum(back, axis=0, keepdims=True)
    db_ref[...] += total


ANY = pl.BlockSpec(memory_space=pl.ANY)


def attn_fwd(hier, counts, x, cot, mine, other, rows=512, chunk=256):
    total, width = x.shape
    per = rows // 64
    blk = lambda w: pl.BlockSpec((rows, w), lambda i: (i, 0))
    return pl.pallas_call(
        functools.partial(attn_fwd_kernel, chunk, hier),
        grid=(total // rows,),
        in_specs=[pl.BlockSpec(memory_space=pltpu.SMEM), blk(width), blk(width), ANY, ANY],
        out_specs=[blk(3 * width), pl.BlockSpec((per, HEADS // 2, 64, 128), lambda i: (i, 0, 0, 0)),
                   blk(width), blk(width), blk(width), blk(width), pl.BlockSpec((1, width), lambda i: (0, 0)),
                   pl.BlockSpec((16, width), lambda i: (0, 0))],
        out_shape=[jax.ShapeDtypeStruct((total, 3 * width), BF),
                   jax.ShapeDtypeStruct((total // 64, HEADS // 2, 64, 128), BF),
                   jax.ShapeDtypeStruct((total, width), BF),
                   jax.ShapeDtypeStruct((total, width), F32),
                   jax.ShapeDtypeStruct((total, width), BF),
                   jax.ShapeDtypeStruct((total, width), BF),
                   jax.ShapeDtypeStruct((1, width), F32),
                   jax.ShapeDtypeStruct((16, width), F32)],
        scratch_shapes=[pltpu.VMEM((width, mine.shape[2]), BF), pltpu.SemaphoreType.DMA((GROUPS,))],
        compiler_params=params(),
        cost_estimate=cost(8 * total * width * width * 1.5, 20 * total * width),
        name="attn_fwd",
    )(counts, x, cot, mine, other)


def gelu_parts(h):
    cdf = 0.5 + 0.5 * lax.erf(h * 0.7071067811865476)
    pdf = jnp.exp(h * h * -0.5) * 0.3989422804014327
    return (h * cdf).astype(BF), cdf + h * pdf


def whole_rows(packed):
    owners, rows, four = packed.shape
    width = four // 4
    return jnp.concatenate([packed[o, :, j * width:(j + 1) * width] for o in range(owners) for j in range(4)], axis=0)


def mlp_kernel(chunk, sec_ref, back_ref, bias_ref, up, down, act_ref, hg_ref, hb_ref, g_hbm, ug_ref, dg_ref, g_sems):
    step = pl.program_id(0)
    last = pl.num_programs(0) - 1
    rows, width = sec_ref.shape
    owners, part, ff = dg_ref.shape
    down = whole_rows(down)
    sums = jnp.zeros((8, width), F32)
    for r in range(rows // chunk):
        at = slice(r * chunk, (r + 1) * chunk)
        act, slope = gelu_parts(dot(sec_ref[at], up[...]) + bias_ref[...])
        act_ref[at] = act
        hg = (dot_rt(back_ref[at], down) * slope).astype(BF)
        hg_ref[at] = hg
        sums = sums + jnp.sum(hg.astype(F32).reshape(chunk // 8, 8, -1), axis=0)
    column = jnp.sum(jnp.concatenate([sums, jnp.zeros((120, width), F32)], axis=0).T, axis=1, keepdims=True)
    lane = lax.broadcasted_iota(jnp.int32, (part, 128), 1)
    for o in range(owners):
        rows_j = [column[(o * 4 + j) * part:(o * 4 + j + 1) * part] for j in range(4)]
        hb_ref[o * part:(o + 1) * part] = sum(jnp.where(lane == 12 + j, rows_j[j], 0.0) for j in range(4))

    def outputs(s):
        at = pl.ds(pl.multiple_of(s * width, width), width)
        return (pltpu.make_async_copy(dg_ref, g_hbm.at[pl.ds(s * owners, owners), :, ff:], g_sems.at[0]),
                pltpu.make_async_copy(ug_ref, g_hbm.at[:, :, at], g_sems.at[1]))

    @pl.when(step > 0)
    def _():
        for copy in outputs(step - 1):
            copy.wait()

    dg = dot_lt(act_ref[...], back_ref[...]).astype(BF)
    for o in range(owners):
        for j in range(4):
            dg_ref[o, :, j * width:(j + 1) * width] = dg[(o * 4 + j) * part:(o * 4 + j + 1) * part]
    outputs(step)[0].start()
    ug_ref[...] = dot_lt(sec_ref[...], hg_ref[...]).astype(BF).reshape(ug_ref.shape)
    outputs(step)[1].start()

    @pl.when(step == last)
    def _():
        for copy in outputs(step):
            copy.wait()


def mlp(sec, back, bias, updown, chunk=256):
    total, width = sec.shape
    ff = bias.shape[1]
    f = width
    part = width // GROUPS
    owners = GROUPS * f // ff
    col = lambda r: pl.BlockSpec((r, f), lambda i: (0, i))
    return pl.pallas_call(
        functools.partial(mlp_kernel, chunk),
        grid=(ff // f,),
        in_specs=[full(sec.shape), full(back.shape), col(1), col(width),
                  pl.BlockSpec((owners, part, ff), lambda i: (i, 0, 1))],
        out_specs=[col(total), col(total), pl.BlockSpec((owners * part, 128), lambda i: (i, 0)), ANY],
        out_shape=[jax.ShapeDtypeStruct((total, ff), BF), jax.ShapeDtypeStruct((total, ff), BF),
                   jax.ShapeDtypeStruct((width, 128), F32), jax.ShapeDtypeStruct((GROUPS, part, 2 * ff), BF)],
        scratch_shapes=[pltpu.VMEM((GROUPS, part, f), BF), pltpu.VMEM((owners, part, ff), BF), pltpu.SemaphoreType.DMA((2,))],
        compiler_params=params(),
        cost_estimate=cost(8 * total * width * ff, 12 * total * width),
        name="mlp",
    )(sec, back, bias, updown, updown.reshape(GROUPS, part, 2 * ff))


def attn_bwd_kernel(hier, hg_ref, mid_ref, back_ref, att_ref, qkv_ref, probs_ref, x_ref, vec, up, db_ref, hid_ref, mine, other,
                    mg_ref, qg_ref, near_hbm, far_hbm, out_acc, in_acc, sums, cs, ag_ref, low_ref, payload, w_ref, sems, out_sems):
    step = pl.program_id(0)
    steps = pl.num_programs(0) - 1
    rows, width = mid_ref.shape

    @pl.when(step == 0)
    def _():
        copies = piece_copies(hier, mine, other, w_ref, sems, slice(None))
        for copy in copies:
            copy.start()
        for ref in (out_acc, in_acc, sums, cs, ag_ref, low_ref):
            ref[...] = jnp.zeros_like(ref)
        for copy in copies:
            copy.wait()

    left = lax.broadcasted_iota(jnp.int32, (64, 128), 1) < HEAD
    center, inv = norm_stats(x_ref[...].astype(F32))
    first = (center * inv).astype(BF)
    work = []
    for i in range(rows // 64):
        work += [(i, slice(i * 64, (i + 1) * 64), pair_cols(width, p), p) for p in range(HEADS // 2)]
    dps = []
    for i, here, c, p in work:
        da = split_heads(ag_ref[here, c[0]], left)
        qg_ref[here, c[2]] = dot(probs_ref[i, p], da).astype(BF)
        dps.append(dot_rt(qkv_ref[here, c[2]], da))
    dss = []
    for (i, here, c, p), dp in zip(work, dps):
        pr = probs_ref[i, p].astype(F32)
        t = dp * pr
        dss.append((t - pr * jnp.sum(t, axis=0, keepdims=True)).astype(BF))
    for (i, here, c, p), ds in zip(work, dss):
        qg_ref[here, c[1]] = (dot(ds, split_heads(qkv_ref[here, c[0]], left)) * 0.125).astype(BF)
        dq = dot_lt(ds, qkv_ref[here, c[1]])
        qg_ref[here, c[0]] = (jnp.where(left, dq[:64], dq[64:]) * 0.125).astype(BF)

    sg = dot_rt(hg_ref[...], up[...])
    out_acc[...] += dot_lt(att_ref[...], low_ref[...])
    center, inv = norm_stats(mid_ref[...])
    n = center * inv
    e = sg * vec[6:7]
    for j in range(3):
        cols = slice(j * width, (j + 1) * width)
        in_acc[:, cols] += dot_lt(first, qg_ref[:, cols])
        cs[:, cols] += jnp.sum(qg_ref[:, cols].astype(F32), axis=0, keepdims=True)
    norm_grad = inv * (e - jnp.mean(e, axis=-1, keepdims=True) - n * jnp.mean(e * n, axis=-1, keepdims=True))
    mg = back_ref[...].astype(F32) + norm_grad
    mg_ref[...] = mg
    once = jnp.where(step < steps, 1.0, 0.0)
    sums[0:1] += once * jnp.sum(sg * n, axis=0, keepdims=True)
    sums[1:2] += once * jnp.sum(sg, axis=0, keepdims=True)
    sums[2:3] += once * jnp.sum(mg, axis=0, keepdims=True)
    low = mg.astype(BF)
    low_ref[...] = low
    ag_ref[...] = dot_rt(low, w_ref[:, 3 * width:4 * width]).astype(BF)

    @pl.when(step == steps)
    def _():
        pos = position(hier)
        sent = []

        def send(cols):
            for away, ref in enumerate((near_hbm, far_hbm)):
                for x in range(2):
                    for k in range(4):
                        copy = pltpu.make_async_copy(payload.at[owner(hier, pos, k, x, away), :, cols], ref.at[x, k, :, cols],
                                                     out_sems.at[len(sent)])
                        copy.start()
                        sent.append(copy)

        def hold(cols, value):
            payload[:, :, cols] = value.astype(BF).reshape(payload.shape[0], payload.shape[1], cols.stop - cols.start)
            send(cols)

        hold(slice(3 * width, 4 * width), out_acc[...])
        tail = w_ref[:, 4 * width:].astype(F32)
        gain, shift = tail[:, 0:1], tail[:, 1:2]
        gain_grad = jnp.zeros((width, 1), F32)
        shift_grad = jnp.zeros((width, 1), F32)
        for j in range(3):
            cols = slice(j * width, (j + 1) * width)
            w = w_ref[:, cols].astype(F32)
            hold(cols, gain * in_acc[:, cols] + shift * cs[:, cols])
            gain_grad = gain_grad + jnp.sum(w * in_acc[:, cols], axis=1, keepdims=True)
            shift_grad = shift_grad + jnp.sum(w * cs[:, cols], axis=1, keepdims=True)
        lines = jnp.concatenate([db_ref[...], sums[0:3], cs[:, :width], cs[:, 2 * width:], jnp.zeros((122, width), F32)], axis=0)
        lane = lax.broadcasted_iota(jnp.int32, (width, 128), 1)
        last = jnp.where(lane == 10, gain_grad, jnp.where(lane == 11, shift_grad, jnp.where(lane < 10, lines.T, hid_ref[...])))
        hold(slice(4 * width, 4 * width + 256), jnp.concatenate([last, jnp.zeros_like(last)], axis=1))
        for copy in sent:
            copy.wait()


def attn_bwd(hier, hg, mid, back, att, qkv, probs, x, vec, updown, db, hid, mine, other, rows=256):
    total, width = mid.shape
    ff = hg.shape[1]
    per = rows // 64
    wide = 4 * width + 256
    part = width // GROUPS
    steps = total // rows
    now = lambda w: pl.BlockSpec((rows, w), lambda i: (jnp.minimum(i, steps - 1), 0))
    ago = lambda w: pl.BlockSpec((rows, w), lambda i: (jnp.maximum(i - 1, 0), 0))
    return pl.pallas_call(
        functools.partial(attn_bwd_kernel, hier),
        grid=(steps + 1,),
        in_specs=[now(ff), now(width), now(width), ago(width), ago(3 * width),
                  pl.BlockSpec((per, HEADS // 2, 64, 128), lambda i: (jnp.maximum(i - 1, 0), 0, 0, 0)), ago(width),
                  full(vec.shape), columns_of(width, 0, ff), full(db.shape), full(hid.shape), ANY, ANY],
        out_specs=[now(width), ago(3 * width), ANY, ANY],
        out_shape=[jax.ShapeDtypeStruct((total, width), F32), jax.ShapeDtypeStruct((total, 3 * width), BF),
                   jax.ShapeDtypeStruct((2, 4, part, wide), BF), jax.ShapeDtypeStruct((2, 4, part, wide), BF)],
        scratch_shapes=[pltpu.VMEM((width, width), F32), pltpu.VMEM((width, 3 * width), F32), pltpu.VMEM((8, width), F32),
                        pltpu.VMEM((1, 3 * width), F32), pltpu.VMEM((rows, width), BF), pltpu.VMEM((rows, width), BF),
                        pltpu.VMEM((GROUPS, part, wide), BF), pltpu.VMEM((width, mine.shape[2]), BF), pltpu.SemaphoreType.DMA((GROUPS,)),
                        pltpu.SemaphoreType.DMA((5 * GROUPS,))],
        compiler_params=params(),
        cost_estimate=cost(2 * total * width * (ff + 9 * width), 28 * total * width),
        name="attn_bwd",
    )(hg, mid, back, att, qkv, probs, x, vec, updown, db, hid, mine, other)


def tokens_grad_kernel(hier, x_ref, qg_ref, mg_ref, vec, mine, other, tie, old, o_ref, w_ref, sems):
    @pl.when(pl.program_id(0) == 0)
    def _():
        run_copies(piece_copies(hier, mine, other, w_ref, sems, slice(0, w_ref.shape[1])))

    center, inv = norm_stats(x_ref[...].astype(F32))
    n = center * inv
    e = dot_rt(qg_ref[...], w_ref[...]) * vec[0:1]
    grad = inv * (e - jnp.mean(e, axis=-1, keepdims=True) - n * jnp.mean(e * n, axis=-1, keepdims=True))
    o_ref[...] = (mg_ref[...] + grad).astype(BF)


def part_of(total, rows, part, parts, width):
    first = part * (total // rows // parts)
    return pl.BlockSpec((rows, width), lambda i: (first + i, 0))


def tokens_grad(hier, part, parts, x, qg, mg, vec, mine, other, tie, old, rows=256):
    total, width = x.shape
    blk = lambda w: part_of(total, rows, part, parts, w)
    return pl.pallas_call(
        functools.partial(tokens_grad_kernel, hier),
        grid=(total // rows // parts,),
        in_specs=[blk(width), blk(3 * width), blk(width), full(vec.shape), ANY, ANY, ANY, ANY],
        out_specs=blk(width),
        out_shape=jax.ShapeDtypeStruct((total, width), BF),
        scratch_shapes=[pltpu.VMEM((width, 3 * width), BF), pltpu.SemaphoreType.DMA((GROUPS,))],
        input_output_aliases={7: 0} if part else {},
        compiler_params=params(),
        cost_estimate=cost(6 * total * width * width // parts, 14 * total * width // parts),
        name="tokens_grad",
    )(x, qg, mg, vec, mine, other, tie, old)


def mixed_kernel(first, counts, act_ref, mid_ref, vec, down, tie, old, o_ref):
    step = pl.program_id(0)
    per = o_ref.shape[0] // 64
    r = mid_ref[...] + dot(act_ref[...], whole_rows(down)) + vec[8:9]
    pos = lax.broadcasted_iota(jnp.int32, (64, o_ref.shape[1]), 0)
    for i in range(per):
        count = counts[(first + step) * per + i]
        o_ref[i * 64:(i + 1) * 64] = jnp.where(pos <= count, r[i * 64:(i + 1) * 64], 0.0).astype(BF)


def mixed_out(part, parts, counts, act, mid, vec, updown, tie, old, rows=256):
    total, width = mid.shape
    ff = act.shape[1]
    blk = lambda w: part_of(total, rows, part, parts, w)
    packed = updown.reshape(GROUPS, width // GROUPS, 2 * ff)
    return pl.pallas_call(
        functools.partial(mixed_kernel, part * (total // rows // parts)),
        grid=(total // rows // parts,),
        in_specs=[pl.BlockSpec(memory_space=pltpu.SMEM), blk(ff), blk(width), full(vec.shape),
                  pl.BlockSpec((GROUPS, width // GROUPS, ff), lambda i: (0, 0, 1), pipeline_mode=pl.Buffered(buffer_count=1)), ANY, ANY],
        out_specs=blk(width),
        out_shape=jax.ShapeDtypeStruct((total, width), BF),
        input_output_aliases={6: 0} if part else {},
        compiler_params=params(),
        cost_estimate=cost(2 * total * width * ff // parts, 14 * total * width // parts),
        name="mixed",
    )(counts, act, mid, vec, packed, tie, old)


FIRST = 896
SECOND = 768


def add(a, b):
    return (a.astype(F32) + b.astype(F32)).astype(BF)


def core_sum_kernel(near, got, tie, x_keep, x_send, y_keep, y_send):
    rep = lax.axis_index("rep")
    first = slice(0, 2 * FIRST)
    x_keep[0] = add(near[0, 0, :, first], got[0, 0, :, first])
    x_send[0] = add(near[1, 0, :, first], got[1, 0, :, first])
    for x in range(2):
        for ref, half in ((y_keep, rep), (y_send, 1 - rep)):
            at = pl.ds(pl.multiple_of(2 * FIRST + half * SECOND, 128), SECOND)
            ref[x, 0] = add(near[x, 0, :, at], got[x, 0, :, at])


def core_sum(near, got, tie):
    _, along, rows, wide = near.shape
    blk = pl.BlockSpec((2, 1, rows, wide), lambda i: (0, i, 0, 0))
    one = pl.BlockSpec((1, rows, 2 * FIRST), lambda i: (i, 0, 0))
    two = pl.BlockSpec((2, 1, rows, SECOND), lambda i: (0, i, 0, 0))
    return pl.pallas_call(
        core_sum_kernel,
        grid=(along,),
        in_specs=[blk, blk, ANY],
        out_specs=[one, one, two, two],
        out_shape=[jax.ShapeDtypeStruct((along, rows, 2 * FIRST), BF)] * 2 + [jax.ShapeDtypeStruct((2, along, rows, SECOND), BF)] * 2,
        compiler_params=params(),
        name="core_sum",
    )(near, got, tie)


def across_sum_kernel(x_keep, x_got, y_keep, y_got, tie, first_keep, first_send, second_keep, second_send):
    rep = lax.axis_index("rep")
    for ref, half in ((first_keep, rep), (first_send, 1 - rep)):
        at = pl.ds(pl.multiple_of(half * FIRST, 128), FIRST)
        ref[...] = add(x_keep[:, :, at], x_got[:, :, at])
    second_keep[...] = add(y_keep[0], y_got[0])
    second_send[...] = add(y_keep[1], y_got[1])


def across_sum(x_keep, x_got, y_keep, y_got, tie):
    along, rows, _ = x_keep.shape
    vm = pl.BlockSpec(memory_space=pltpu.VMEM)
    return pl.pallas_call(
        across_sum_kernel,
        in_specs=[vm] * 4 + [ANY],
        out_specs=[vm] * 4,
        out_shape=[jax.ShapeDtypeStruct((along, rows, FIRST), BF)] * 2 + [jax.ShapeDtypeStruct((along, rows, SECOND), BF)] * 2,
        compiler_params=params(),
        name="across_sum",
    )(x_keep, x_got, y_keep, y_got, tie)


def plane_sum_kernel(first_keep, first_got, second_keep, second_got, tie, *outs):
    for k, o_ref in enumerate(outs):
        o_ref[:, :FIRST] = add(first_keep[k], first_got[k])
        o_ref[:, FIRST:] = add(second_keep[k], second_got[k])


def plane_sum(first_keep, first_got, second_keep, second_got, tie):
    along, rows, _ = first_keep.shape
    vm = pl.BlockSpec(memory_space=pltpu.VMEM)
    return pl.pallas_call(
        plane_sum_kernel,
        in_specs=[vm] * 4 + [ANY],
        out_specs=[vm] * along,
        out_shape=[jax.ShapeDtypeStruct((rows, FIRST + SECOND), BF)] * along,
        compiler_params=params(),
        name="plane_sum",
    )(first_keep, first_got, second_keep, second_got, tie)


def along_sum_kernel(a, b, c, d, tie, o_ref):
    total = (a[...].astype(F32) + b[...].astype(F32)) + (c[...].astype(F32) + d[...].astype(F32))
    o_ref[...] = total.astype(BF)


def along_sum(a, b, c, d, tie):
    vm = pl.BlockSpec(memory_space=pltpu.VMEM)
    return pl.pallas_call(
        along_sum_kernel,
        in_specs=[vm] * 4 + [ANY],
        out_specs=vm,
        out_shape=jax.ShapeDtypeStruct(a.shape, BF),
        compiler_params=params(),
        name="along_sum",
    )(a, b, c, d, tie)


def finish_kernel(a_ref, b_ref, in_ref, out_ref, *vectors):
    rows = a_ref.shape[0]
    front = lax.axis_index("rep") == 0
    a, b = a_ref[...].astype(F32), b_ref[...].astype(F32)
    low, high = jnp.where(front, a, b), jnp.where(front, b, a)
    total = jnp.concatenate([low[:, :FIRST], high[:, :FIRST], low[:, FIRST:], high[:, FIRST:]], axis=1)
    wide = in_ref.shape[1] + out_ref.shape[1]
    in_ref[...] = total[:, :in_ref.shape[1]]
    out_ref[...] = total[:, in_ref.shape[1]:wide]
    lines = total[:, wide:wide + 128].T
    for i, v in enumerate(vectors[:-1]):
        v[...] = lines[i:i + 1].reshape(rows)
    vectors[-1][...] = lines[12:16]


def finish(a, b, width):
    rows = a.shape[0]
    vm = pl.BlockSpec(memory_space=pltpu.VMEM)
    return pl.pallas_call(
        finish_kernel,
        in_specs=[vm, vm],
        out_specs=[vm] * 15,
        out_shape=[jax.ShapeDtypeStruct((rows, 3 * width), F32), jax.ShapeDtypeStruct((rows, width), F32)]
        + [jax.ShapeDtypeStruct((rows,), F32)] * 12 + [jax.ShapeDtypeStruct((4, rows), F32)],
        compiler_params=params(),
        name="finish",
    )(a, b)


CORE = [(i, i ^ 1) for i in range(16)]
ACROSS = [(i, i ^ 2) for i in range(16)]
ALONG = [[(i, ((i // 4 + k) % 4) * 4 + i % 4) for i in range(16)] for k in range(4)]
SWAP = [(0, 1), (1, 0)]


def permute(v, pairs):
    return lax.ppermute(v, "fsdp", pairs)


def gather_along(shard):
    return [shard] + [permute(shard, ALONG[k]) for k in (1, 3, 2)]


def gather_across(along):
    along = [along[0], along[1], along[3], along[2]]
    mine = jnp.stack(along + [permute(v, ACROSS) for v in along])
    return mine, permute(mine, CORE)


def gather_whole(shard):
    whole = lax.all_gather(shard, "fsdp", axis=0, tiled=True)
    whole = whole.reshape(4, 2, 2, whole.shape[0] // GROUPS, whole.shape[1])
    order = jnp.concatenate([whole[:1], whole[3:0:-1]], axis=0).transpose(2, 1, 0, 3, 4)
    return order[0].reshape((8,) + order.shape[3:]), order[1].reshape((8,) + order.shape[3:])


def regroup(updown, own):
    width = updown.shape[0]
    ff = 4 * width
    down = updown[:, ff:].reshape(width // own, own, 4, width).transpose(0, 2, 1, 3).reshape(GROUPS, 4, width // GROUPS, width)
    return jnp.concatenate([updown[:, :ff], down.transpose(0, 2, 1, 3).reshape(width, ff)], axis=1)


def over_rep(shard):
    low = shard.astype(BF)
    return low, lax.ppermute(low, "rep", SWAP)


def after(value, other):
    return lax.optimization_barrier((value, other))[0]


def local(hier, tokens, counts, cotangent, first_gain, first_shift, in_proj, query_bias, value_bias, out_proj, out_bias,
          second_gain, second_shift, up_proj, hidden_bias, down_proj, down_bias):
    images, rows, width = tokens.shape
    own = first_gain.shape[0]
    ff = 4 * width
    x = tokens.reshape(images * rows, width)
    cot = cotangent.reshape(images * rows, width)
    vectors = (first_gain, first_shift, query_bias, value_bias, out_bias, second_gain, second_shift, down_bias)
    if hier:
        packed = pack(vectors, hidden_bias, in_proj, out_proj)
        mine, other = gather_across(gather_along(packed))
        updown = lax.all_gather(pack_mlp(up_proj, down_proj), "fsdp", axis=0, tiled=True)
    else:
        columns = jnp.concatenate(vectors[:3] + (jnp.zeros_like(query_bias),) + vectors[3:] + (hidden_bias,)).reshape(13, own).T
        packed = jnp.concatenate([in_proj, out_proj, columns, jnp.zeros((own, 115), BF)], axis=1)
        mine, other = gather_whole(packed)
        updown = jnp.concatenate([up_proj] + [down_proj[j * own:(j + 1) * own] for j in range(4)], axis=1)
        updown = regroup(lax.all_gather(updown, "fsdp", axis=0, tiled=True), own)
    qkv, probs, att, mid, sec, back, db, vec = attn_fwd(hier, counts, x, cot, mine, other)
    owners = width // own
    bias = vec[9:13].reshape(4, owners, own).transpose(1, 0, 2).reshape(1, ff)
    act, hg, hid, grads = mlp(sec, back, bias, updown)
    if not hier:
        sums = hid[:, 12:16].reshape(GROUPS, width // GROUPS, 4).transpose(0, 2, 1).reshape(owners, 4, own).transpose(0, 2, 1)
        hid = hid.at[:, 12:16].set(sums.reshape(width, 4))
        dg = grads[:, :, ff:].reshape(GROUPS, width // GROUPS, 4, width).transpose(0, 2, 1, 3).reshape(owners, 4, own, width)
        grads = jnp.concatenate([grads[:, :, :ff].reshape(width, ff), dg.transpose(0, 2, 1, 3).reshape(width, ff)], axis=1)
    mlp_grads = lax.psum_scatter(grads.reshape(width, 2 * ff), "fsdp", scatter_dimension=0, tiled=True)
    mg, qg, near, far = attn_bwd(hier, hg, mid, back, att, qkv, probs, x, vec, updown, db, hid, mine, other)
    tok = lambda part, tie, old: tokens_grad(hier, part, 2, x, qg, mg, vec, mine, other, tie, old)
    mix = lambda part, tie, old: mixed_out(part, 2, counts, act, mid, vec, updown, tie, old)
    if hier:
        got = permute(far, CORE)
        mixed = mix(0, far, far)
        x_keep, x_send, y_keep, y_send = core_sum(near, got, mixed)
        x_got, y_got = permute(x_send, ACROSS), lax.ppermute(y_send, "rep", SWAP)
        mixed = mix(1, x_send, mixed)
        first_keep, first_send, second_keep, second_send = across_sum(x_keep, x_got, y_keep, y_got, mixed)
        first_got, second_got = lax.ppermute(first_send, "rep", SWAP), permute(second_send, ACROSS)
        toks = tok(0, first_send, mixed)
        parts = plane_sum(first_keep, first_got, second_keep, second_got, toks)
        moved = [permute(parts[k], ALONG[k]) for k in (1, 2, 3)]
        mlp_grads = after(mlp_grads, parts[3])
        toks = tok(1, parts[3], toks)
        low = along_sum(parts[0], *moved, toks)
        grad_in, grad_out, *lines, hidden = finish(low, lax.ppermute(low, "rep", SWAP), width)
    else:
        mixed = mix(1, far, mix(0, far, far))
        toks = tok(1, far, tok(0, far, far))
        blocks = jnp.stack([near, far]).transpose(2, 1, 0, 3, 4).reshape(width, near.shape[-1])
        a, b = over_rep(lax.psum_scatter(blocks, "fsdp", scatter_dimension=0, tiled=True))
        wide = a.astype(F32) + b.astype(F32)
        grad_in, grad_out, lines = wide[:, :3 * width], wide[:, 3 * width:4 * width], wide[:, 4 * width:].T
        hidden = lines[12:16]
    a, b = over_rep(mlp_grads)
    mlp_grads = a.astype(F32) + b.astype(F32)
    grad_up = mlp_grads[:, :ff]
    grad_down = jnp.concatenate([mlp_grads[:, ff + j * width:ff + (j + 1) * width] for j in range(4)], axis=0)
    return (mixed.reshape(tokens.shape), toks.reshape(tokens.shape), lines[10], lines[11], grad_in, lines[4], lines[5],
            grad_out, lines[3], lines[1], lines[2], grad_up, hidden.reshape(4 * own), grad_down, lines[0])


def solution(mesh):
    rows = P(("fsdp", "rep"), None, None)
    v, m = P("fsdp"), P("fsdp", None)
    in_specs = (rows, P(("fsdp", "rep")), rows, v, v, m, v, v, m, v, v, v, m, v, m, v)
    out_specs = (rows, rows, v, v, m, v, v, m, v, v, v, m, v, m, v)
    hier = mesh.shape["fsdp"] == GROUPS and mesh.shape["rep"] == 2
    return jax.shard_map(functools.partial(local, hier), mesh=mesh, in_specs=in_specs, out_specs=out_specs, check_vma=False)
```

```python
import functools
import jax
import jax.numpy as jnp
from jax import lax
from jax.experimental import pallas as pl
from jax.experimental.pallas import tpu as pltpu
from jax.sharding import PartitionSpec as P

HEADS = 12
HEAD = 64
EPS = 1e-06
BF = jnp.bfloat16
F32 = jnp.float32
VMEM = 63 << 20


def dot(a, b):
    return jnp.dot(a, b, preferred_element_type=F32)


def dot_rt(a, b):
    return lax.dot_general(a, b, (((1,), (1,)), ((), ())), preferred_element_type=F32)


def dot_lt(a, b):
    return lax.dot_general(a, b, (((0,), (0,)), ((), ())), preferred_element_type=F32)


def norm_stats(v):
    center = v - jnp.mean(v, axis=-1, keepdims=True)
    inv = lax.rsqrt(jnp.mean(center * center, axis=-1, keepdims=True) + EPS)
    return center, inv


def params(**kw):
    return pltpu.CompilerParams(vmem_limit_bytes=VMEM, **kw)


def full(shape):
    zeros = (0,) * len(shape)
    return pl.BlockSpec(shape, lambda *_: zeros, pipeline_mode=pl.Buffered(buffer_count=1))


def columns_of(rows, block, width):
    return pl.BlockSpec((rows, width), lambda *_: (0, block), pipeline_mode=pl.Buffered(buffer_count=1))


def pack_mlp_kernel(up, down, o_ref):
    rows, ff = up.shape
    width = ff // 4
    o_ref[:, :ff] = up[...]
    for j in range(4):
        o_ref[:, ff + j * width:ff + (j + 1) * width] = down[j * rows:(j + 1) * rows]


def pack_mlp(up, down):
    rows, ff = up.shape
    vm = pl.BlockSpec(memory_space=pltpu.VMEM)
    return pl.pallas_call(
        pack_mlp_kernel,
        in_specs=[vm, vm],
        out_specs=vm,
        out_shape=jax.ShapeDtypeStruct((rows, 2 * ff), BF),
        compiler_params=params(),
        name="pack_mlp",
    )(up, down)


def split_heads(pair, left):
    zero = jnp.zeros_like(pair)
    return jnp.concatenate([jnp.where(left, pair, zero), jnp.where(left, zero, pair)], axis=0)


def cost(flops, nbytes):
    return pl.CostEstimate(flops=int(flops), bytes_accessed=int(nbytes), transcendentals=0)


GROUPS = 16


def position(hier):
    if not hier:
        return 0, 0, 0
    me = lax.axis_index("fsdp")
    return me // 4, (me // 2) % 2, me % 2


def owner(hier, pos, k, other_x, other_c):
    if not hier:
        return (k * 2 + other_x) * 2 + other_c
    z, x, c = pos
    z = lax.rem(z + k, 4)
    x = 1 - x if other_x else x
    c = 1 - c if other_c else c
    return (z * 2 + x) * 2 + c


def rows_of(slot, rows):
    return pl.ds(pl.multiple_of(slot * rows, rows), rows)


def piece_copies(hier, mine, other, w_ref, sems, cols):
    pos = position(hier)
    out = []
    for c, ref in enumerate((mine, other)):
        for x in range(2):
            for k in range(4):
                slot = owner(hier, pos, (4 - k) % 4, x, c)
                out.append(pltpu.make_async_copy(ref.at[x * 4 + k, :, cols], w_ref.at[rows_of(slot, ref.shape[1])], sems.at[len(out)]))
    return out


def run_copies(copies):
    for copy in copies:
        copy.start()
    for copy in copies:
        copy.wait()


def pack_kernel(*refs):
    *vectors, hidden, in_proj, out_proj, o_ref, half_ref = refs
    rows = o_ref.shape[0]
    wide = in_proj.shape[1] + out_proj.shape[1]
    o_ref[:, :in_proj.shape[1]] = in_proj[...]
    o_ref[:, in_proj.shape[1]:wide] = out_proj[...]
    lines = [v[...].astype(F32).reshape(1, rows) for v in vectors]
    lines.insert(3, jnp.zeros((1, rows), F32))
    hidden = hidden[...].astype(F32).reshape(1, 4 * rows)
    lines += [hidden[:, j * rows:(j + 1) * rows] for j in range(4)] + [jnp.zeros((115, rows), F32)]
    o_ref[:, wide:wide + 128] = jnp.concatenate(lines, axis=0).T.astype(BF)
    o_ref[:, wide + 128:] = jnp.zeros((rows, 128), BF)
    some = half_ref.shape[1]
    half_ref[...] = o_ref[:, pl.ds(pl.multiple_of(lax.axis_index("rep") * some, 128), some)]


def pack(vectors, hidden, in_proj, out_proj):
    rows = in_proj.shape[0]
    wide = in_proj.shape[1] + out_proj.shape[1] + 256
    vm = pl.BlockSpec(memory_space=pltpu.VMEM)
    return pl.pallas_call(
        pack_kernel,
        in_specs=[vm] * (len(vectors) + 3),
        out_specs=[vm, vm],
        out_shape=[jax.ShapeDtypeStruct((rows, wide), BF), jax.ShapeDtypeStruct((rows, wide // 2), BF)],
        compiler_params=params(),
        name="pack",
    )(*vectors, hidden, in_proj, out_proj)


def assemble_kernel(own, across, *refs):
    *halves, o_ref = refs
    some = o_ref.shape[2] // 2
    rep = lax.axis_index("rep")
    here = pl.ds(pl.multiple_of(rep * some, 128), some)
    there = pl.ds(pl.multiple_of((1 - rep) * some, 128), some)
    o_ref[0] = own[...]
    o_ref[4] = across[...]
    for i in range(6):
        to = i + 1 if i < 3 else i + 2
        o_ref[to, :, here] = halves[2 * i][...]
        o_ref[to, :, there] = halves[2 * i + 1][...]


def assemble(own, across, halves):
    vm = pl.BlockSpec(memory_space=pltpu.VMEM)
    return pl.pallas_call(
        assemble_kernel,
        in_specs=[vm] * 14,
        out_specs=vm,
        out_shape=jax.ShapeDtypeStruct((8,) + own.shape, BF),
        compiler_params=params(),
        name="assemble",
    )(own, across, *halves)


def pair_cols(width, p):
    return [slice(j * width + p * 128, j * width + (p + 1) * 128) for j in range(3)]


def attn_fwd_kernel(chunk, hier, counts, x_ref, cot_ref, mine, other,
                    qkv_ref, probs_ref, att_ref, mid_ref, sec_ref, back_ref, db_ref, vec, w_ref, sems):
    step = pl.program_id(0)
    rows, width = x_ref.shape
    per = rows // 64

    @pl.when(step == 0)
    def _():
        run_copies(piece_copies(hier, mine, other, w_ref, sems, slice(None)))
        vec[...] = w_ref[:, 4 * width:4 * width + 128].astype(F32).T[:16]
        db_ref[...] = jnp.zeros_like(db_ref)

    left = lax.broadcasted_iota(jnp.int32, (64, 128), 1) < HEAD
    row = lax.broadcasted_iota(jnp.int32, (64, 128), 0)
    pos = lax.broadcasted_iota(jnp.int32, (64, width), 0)

    def project(at):
        center, inv = norm_stats(x_ref[at].astype(F32))
        first = (center * inv * vec[0:1] + vec[1:2]).astype(BF)
        for j in range(3):
            cols = slice(j * width, (j + 1) * width)
            qkv_ref[at, cols] = (dot(first, w_ref[:, cols]) + vec[2 + j:3 + j]).astype(BF)

    def attend(at):
        work = []
        for i in range(at.start // 64, at.stop // 64):
            here = slice(i * 64, (i + 1) * 64)
            work += [(i, here, row <= counts[step * per + i], pair_cols(width, p), p) for p in range(HEADS // 2)]
        scores = [dot_rt(qkv_ref[here, c[1]], split_heads(qkv_ref[here, c[0]], left)) for i, here, usable, c, p in work]
        lows = []
        for (i, here, usable, c, p), s in zip(work, scores):
            s = jnp.where(usable, s * 0.125, -1000000000.0)
            e = jnp.exp(s - jnp.max(s, axis=0, keepdims=True))
            low = (e * (1.0 / jnp.sum(e, axis=0, keepdims=True))).astype(BF)
            probs_ref[i, p] = low
            lows.append(low)
        for (i, here, usable, c, p), low in zip(work, lows):
            o = dot_lt(low, qkv_ref[here, c[2]])
            att_ref[here, c[0]] = jnp.where(left, o[:64], o[64:]).astype(BF)

    def output(at):
        mid = x_ref[at].astype(F32) + dot(att_ref[at], w_ref[:, 3 * width:4 * width]) + vec[5:6]
        mid_ref[at] = mid
        center, inv = norm_stats(mid)
        sec_ref[at] = (center * inv * vec[6:7] + vec[7:8]).astype(BF)

    chunks = [slice(r, r + chunk) for r in range(0, rows, chunk)]
    project(chunks[0])
    for c, at in enumerate(chunks):
        if c + 1 < len(chunks):
            project(chunks[c + 1])
        attend(at)
        output(at)
    total = jnp.zeros((1, width), F32)
    for i in range(per):
        at = slice(i * 64, (i + 1) * 64)
        back = jnp.where(pos <= counts[step * per + i], cot_ref[at].astype(F32), 0.0)
        back_ref[at] = back.astype(BF)
        total = total + jnp.sum(back, axis=0, keepdims=True)
    db_ref[...] += total


ANY = pl.BlockSpec(memory_space=pl.ANY)


def attn_fwd(hier, counts, x, cot, mine, other, rows=512, chunk=256):
    total, width = x.shape
    per = rows // 64
    blk = lambda w: pl.BlockSpec((rows, w), lambda i: (i, 0))
    return pl.pallas_call(
        functools.partial(attn_fwd_kernel, chunk, hier),
        grid=(total // rows,),
        in_specs=[pl.BlockSpec(memory_space=pltpu.SMEM), blk(width), blk(width), ANY, ANY],
        out_specs=[blk(3 * width), pl.BlockSpec((per, HEADS // 2, 64, 128), lambda i: (i, 0, 0, 0)),
                   blk(width), blk(width), blk(width), blk(width), pl.BlockSpec((1, width), lambda i: (0, 0)),
                   pl.BlockSpec((16, width), lambda i: (0, 0))],
        out_shape=[jax.ShapeDtypeStruct((total, 3 * width), BF),
                   jax.ShapeDtypeStruct((total // 64, HEADS // 2, 64, 128), BF),
                   jax.ShapeDtypeStruct((total, width), BF),
                   jax.ShapeDtypeStruct((total, width), F32),
                   jax.ShapeDtypeStruct((total, width), BF),
                   jax.ShapeDtypeStruct((total, width), BF),
                   jax.ShapeDtypeStruct((1, width), F32),
                   jax.ShapeDtypeStruct((16, width), F32)],
        scratch_shapes=[pltpu.VMEM((width, mine.shape[2]), BF), pltpu.SemaphoreType.DMA((GROUPS,))],
        compiler_params=params(),
        cost_estimate=cost(8 * total * width * width * 1.5, 20 * total * width),
        name="attn_fwd",
    )(counts, x, cot, mine, other)


def gelu_parts(h):
    cdf = 0.5 + 0.5 * lax.erf(h * 0.7071067811865476)
    pdf = jnp.exp(h * h * -0.5) * 0.3989422804014327
    return (h * cdf).astype(BF), cdf + h * pdf


def whole_rows(packed):
    owners, rows, four = packed.shape
    width = four // 4
    return jnp.concatenate([packed[o, :, j * width:(j + 1) * width] for o in range(owners) for j in range(4)], axis=0)


def mlp_kernel(chunk, sec_ref, back_ref, bias_ref, up, down, act_hbm, hg_hbm, hb_ref, g_hbm,
               act_ref, hg_ref, ug_ref, dg_ref, a_sems, g_sems):
    step = pl.program_id(0)
    last = pl.num_programs(0) - 1
    rows, width = sec_ref.shape
    owners, part, ff = dg_ref.shape
    slot = lax.rem(step, 2)

    def blocks(s, which):
        at = pl.ds(pl.multiple_of(s * width, width), width)
        return (pltpu.make_async_copy(act_ref.at[which], act_hbm.at[:, at], a_sems.at[which, 0]),
                pltpu.make_async_copy(hg_ref.at[which], hg_hbm.at[:, at], a_sems.at[which, 1]))

    def outputs(s):
        at = pl.ds(pl.multiple_of(s * width, width), width)
        return (pltpu.make_async_copy(dg_ref, g_hbm.at[pl.ds(s * owners, owners), :, ff:], g_sems.at[0]),
                pltpu.make_async_copy(ug_ref, g_hbm.at[:, :, at], g_sems.at[1]))

    @pl.when(step > 1)
    def _():
        for copy in blocks(step - 2, slot):
            copy.wait()

    @pl.when(step > 0)
    def _():
        for copy in outputs(step - 1):
            copy.wait()

    down = whole_rows(down)
    sums = jnp.zeros((8, width), F32)
    for r in range(rows // chunk):
        at = slice(r * chunk, (r + 1) * chunk)
        act, slope = gelu_parts(dot(sec_ref[at], up[...]) + bias_ref[...])
        act_ref[slot, at] = act
        hg = (dot_rt(back_ref[at], down) * slope).astype(BF)
        hg_ref[slot, at] = hg
        sums = sums + jnp.sum(hg.astype(F32).reshape(chunk // 8, 8, -1), axis=0)
    for copy in blocks(step, slot):
        copy.start()
    column = jnp.sum(jnp.concatenate([sums, jnp.zeros((120, width), F32)], axis=0).T, axis=1, keepdims=True)
    lane = lax.broadcasted_iota(jnp.int32, (part, 128), 1)
    for o in range(owners):
        rows_j = [column[(o * 4 + j) * part:(o * 4 + j + 1) * part] for j in range(4)]
        hb_ref[o * part:(o + 1) * part] = sum(jnp.where(lane == 12 + j, rows_j[j], 0.0) for j in range(4))
    dg = dot_lt(act_ref[slot], back_ref[...]).astype(BF)
    for o in range(owners):
        for j in range(4):
            dg_ref[o, :, j * width:(j + 1) * width] = dg[(o * 4 + j) * part:(o * 4 + j + 1) * part]
    outputs(step)[0].start()
    ug_ref[...] = dot_lt(sec_ref[...], hg_ref[slot]).astype(BF).reshape(ug_ref.shape)
    outputs(step)[1].start()

    @pl.when(step == last)
    def _():
        for copy in blocks(step - 1, 1 - slot) + blocks(step, slot) + outputs(step):
            copy.wait()


def mlp(sec, back, bias, updown, chunk=256):
    total, width = sec.shape
    ff = bias.shape[1]
    f = width
    part = width // GROUPS
    owners = GROUPS * f // ff
    col = lambda r: pl.BlockSpec((r, f), lambda i: (0, i))
    return pl.pallas_call(
        functools.partial(mlp_kernel, chunk),
        grid=(ff // f,),
        in_specs=[full(sec.shape), full(back.shape), col(1), col(width),
                  pl.BlockSpec((owners, part, ff), lambda i: (i, 0, 1))],
        out_specs=[ANY, ANY, pl.BlockSpec((owners * part, 128), lambda i: (i, 0)), ANY],
        out_shape=[jax.ShapeDtypeStruct((total, ff), BF), jax.ShapeDtypeStruct((total, ff), BF),
                   jax.ShapeDtypeStruct((width, 128), F32), jax.ShapeDtypeStruct((GROUPS, part, 2 * ff), BF)],
        scratch_shapes=[pltpu.VMEM((2, total, f), BF), pltpu.VMEM((2, total, f), BF), pltpu.VMEM((GROUPS, part, f), BF),
                        pltpu.VMEM((owners, part, ff), BF), pltpu.SemaphoreType.DMA((2, 2)), pltpu.SemaphoreType.DMA((2,))],
        compiler_params=params(),
        cost_estimate=cost(8 * total * width * ff, 12 * total * width),
        name="mlp",
    )(sec, back, bias, updown, updown.reshape(GROUPS, part, 2 * ff))


def attn_bwd_kernel(hier, hg_ref, mid_ref, back_ref, att_ref, qkv_ref, probs_ref, x_ref, vec, up, db_ref, hid_ref, mine, other,
                    mg_ref, qg_ref, near_hbm, far_hbm, out_acc, in_acc, sums, cs, ag_ref, low_ref, payload, w_ref, sems, out_sems):
    step = pl.program_id(0)
    steps = pl.num_programs(0) - 1
    rows, width = mid_ref.shape

    @pl.when(step == 0)
    def _():
        for copy in piece_copies(hier, mine, other, w_ref, sems, slice(None)):
            copy.start()
        for ref in (out_acc, in_acc, sums, cs):
            ref[...] = jnp.zeros_like(ref)

    left = lax.broadcasted_iota(jnp.int32, (64, 128), 1) < HEAD

    def body(here_too, before_too):
        if before_too:
            center, inv = norm_stats(x_ref[...].astype(F32))
            first = (center * inv).astype(BF)
            work = []
            for i in range(rows // 64):
                work += [(i, slice(i * 64, (i + 1) * 64), pair_cols(width, p), p) for p in range(HEADS // 2)]
            dps = []
            for i, here, c, p in work:
                da = split_heads(ag_ref[here, c[0]], left)
                qg_ref[here, c[2]] = dot(probs_ref[i, p], da).astype(BF)
                dps.append(dot_rt(qkv_ref[here, c[2]], da))
            dss = []
            for (i, here, c, p), dp in zip(work, dps):
                pr = probs_ref[i, p].astype(F32)
                t = dp * pr
                dss.append((t - pr * jnp.sum(t, axis=0, keepdims=True)).astype(BF))
            for (i, here, c, p), ds in zip(work, dss):
                qg_ref[here, c[1]] = (dot(ds, split_heads(qkv_ref[here, c[0]], left)) * 0.125).astype(BF)
                dq = dot_lt(ds, qkv_ref[here, c[1]])
                qg_ref[here, c[0]] = (jnp.where(left, dq[:64], dq[64:]) * 0.125).astype(BF)
        if here_too:
            sg = dot_rt(hg_ref[...], up[...])
        if before_too:
            out_acc[...] += dot_lt(att_ref[...], low_ref[...])
        if here_too:
            center, inv = norm_stats(mid_ref[...])
            n = center * inv
            e = sg * vec[6:7]
        if before_too:
            for j in range(3):
                cols = slice(j * width, (j + 1) * width)
                in_acc[:, cols] += dot_lt(first, qg_ref[:, cols])
                cs[:, cols] += jnp.sum(qg_ref[:, cols].astype(F32), axis=0, keepdims=True)
        if here_too:
            norm_grad = inv * (e - jnp.mean(e, axis=-1, keepdims=True) - n * jnp.mean(e * n, axis=-1, keepdims=True))
            mg = back_ref[...].astype(F32) + norm_grad
            mg_ref[...] = mg
            sums[0:1] += jnp.sum(sg * n, axis=0, keepdims=True)
            sums[1:2] += jnp.sum(sg, axis=0, keepdims=True)
            sums[2:3] += jnp.sum(mg, axis=0, keepdims=True)
            low = mg.astype(BF)
            low_ref[...] = low
            if not before_too:
                for copy in piece_copies(hier, mine, other, w_ref, sems, slice(None)):
                    copy.wait()
            ag_ref[...] = dot_rt(low, w_ref[:, 3 * width:4 * width]).astype(BF)

    @pl.when(step == 0)
    def _():
        body(True, False)

    @pl.when((step > 0) & (step < steps))
    def _():
        body(True, True)

    @pl.when(step == steps)
    def _():
        body(False, True)

    @pl.when(step == steps)
    def _():
        pos = position(hier)
        sent = []

        def send(cols):
            for away, ref in enumerate((near_hbm, far_hbm)):
                for x in range(2):
                    for k in range(4):
                        copy = pltpu.make_async_copy(payload.at[owner(hier, pos, k, x, away), :, cols], ref.at[x, k, :, cols],
                                                     out_sems.at[len(sent)])
                        copy.start()
                        sent.append(copy)

        def hold(cols, value):
            payload[:, :, cols] = value.astype(BF).reshape(payload.shape[0], payload.shape[1], cols.stop - cols.start)
            send(cols)

        hold(slice(3 * width, 4 * width), out_acc[...])
        tail = w_ref[:, 4 * width:4 * width + 128].astype(F32)
        gain, shift = tail[:, 0:1], tail[:, 1:2]
        gain_grad = jnp.zeros((width, 1), F32)
        shift_grad = jnp.zeros((width, 1), F32)
        for j in range(3):
            cols = slice(j * width, (j + 1) * width)
            w = w_ref[:, cols].astype(F32)
            hold(cols, gain * in_acc[:, cols] + shift * cs[:, cols])
            gain_grad = gain_grad + jnp.sum(w * in_acc[:, cols], axis=1, keepdims=True)
            shift_grad = shift_grad + jnp.sum(w * cs[:, cols], axis=1, keepdims=True)
        lines = jnp.concatenate([db_ref[...], sums[0:3], cs[:, :width], cs[:, 2 * width:], jnp.zeros((122, width), F32)], axis=0)
        lane = lax.broadcasted_iota(jnp.int32, (width, 128), 1)
        last = jnp.where(lane == 10, gain_grad, jnp.where(lane == 11, shift_grad, jnp.where(lane < 10, lines.T, hid_ref[...])))
        hold(slice(4 * width, 4 * width + 256), jnp.concatenate([last, jnp.zeros_like(last)], axis=1))
        for copy in sent:
            copy.wait()


def attn_bwd(hier, hg, mid, back, att, qkv, probs, x, vec, updown, db, hid, mine, other, rows=256):
    total, width = mid.shape
    ff = hg.shape[1]
    per = rows // 64
    wide = 4 * width + 256
    part = width // GROUPS
    steps = total // rows
    now = lambda w: pl.BlockSpec((rows, w), lambda i: (jnp.minimum(i, steps - 1), 0))
    ago = lambda w: pl.BlockSpec((rows, w), lambda i: (jnp.maximum(i - 1, 0), 0))
    return pl.pallas_call(
        functools.partial(attn_bwd_kernel, hier),
        grid=(steps + 1,),
        in_specs=[now(ff), now(width), now(width), ago(width), ago(3 * width),
                  pl.BlockSpec((per, HEADS // 2, 64, 128), lambda i: (jnp.maximum(i - 1, 0), 0, 0, 0)), ago(width),
                  full(vec.shape), columns_of(width, 0, ff), full(db.shape), full(hid.shape), ANY, ANY],
        out_specs=[now(width), ago(3 * width), ANY, ANY],
        out_shape=[jax.ShapeDtypeStruct((total, width), F32), jax.ShapeDtypeStruct((total, 3 * width), BF),
                   jax.ShapeDtypeStruct((2, 4, part, wide), BF), jax.ShapeDtypeStruct((2, 4, part, wide), BF)],
        scratch_shapes=[pltpu.VMEM((width, width), F32), pltpu.VMEM((width, 3 * width), F32), pltpu.VMEM((8, width), F32),
                        pltpu.VMEM((1, 3 * width), F32), pltpu.VMEM((rows, width), BF), pltpu.VMEM((rows, width), BF),
                        pltpu.VMEM((GROUPS, part, wide), BF), pltpu.VMEM((width, mine.shape[2]), BF), pltpu.SemaphoreType.DMA((GROUPS,)),
                        pltpu.SemaphoreType.DMA((5 * GROUPS,))],
        compiler_params=params(),
        cost_estimate=cost(2 * total * width * (ff + 9 * width), 28 * total * width),
        name="attn_bwd",
    )(hg, mid, back, att, qkv, probs, x, vec, updown, db, hid, mine, other)


def tokens_grad_kernel(hier, x_ref, qg_ref, mg_ref, vec, mine, other, tie, old, o_ref, w_ref, sems):
    @pl.when(pl.program_id(0) == 0)
    def _():
        run_copies(piece_copies(hier, mine, other, w_ref, sems, slice(0, w_ref.shape[1])))

    center, inv = norm_stats(x_ref[...].astype(F32))
    n = center * inv
    e = dot_rt(qg_ref[...], w_ref[...]) * vec[0:1]
    grad = inv * (e - jnp.mean(e, axis=-1, keepdims=True) - n * jnp.mean(e * n, axis=-1, keepdims=True))
    o_ref[...] = (mg_ref[...] + grad).astype(BF)


def part_of(rows, first, width):
    return pl.BlockSpec((rows, width), lambda i: (first + i, 0))


def tokens_grad(hier, first, blocks, x, qg, mg, vec, mine, other, tie, old, rows=256):
    total, width = x.shape
    blk = lambda w: part_of(rows, first, w)
    return pl.pallas_call(
        functools.partial(tokens_grad_kernel, hier),
        grid=(blocks,),
        in_specs=[blk(width), blk(3 * width), blk(width), full(vec.shape), ANY, ANY, ANY, ANY],
        out_specs=blk(width),
        out_shape=jax.ShapeDtypeStruct((total, width), BF),
        scratch_shapes=[pltpu.VMEM((width, 3 * width), BF), pltpu.SemaphoreType.DMA((GROUPS,))],
        input_output_aliases={7: 0} if first else {},
        compiler_params=params(),
        cost_estimate=cost(6 * blocks * rows * width * width, 14 * blocks * rows * width),
        name="tokens_grad",
    )(x, qg, mg, vec, mine, other, tie, old)


def mixed_kernel(first, counts, act_ref, mid_ref, vec, down, tie, old, o_ref):
    step = pl.program_id(0)
    per = o_ref.shape[0] // 64
    r = mid_ref[...] + dot(act_ref[...], whole_rows(down)) + vec[8:9]
    pos = lax.broadcasted_iota(jnp.int32, (64, o_ref.shape[1]), 0)
    for i in range(per):
        count = counts[(first + step) * per + i]
        o_ref[i * 64:(i + 1) * 64] = jnp.where(pos <= count, r[i * 64:(i + 1) * 64], 0.0).astype(BF)


def mixed_out(first, blocks, counts, act, mid, vec, updown, tie, old, rows=256):
    total, width = mid.shape
    ff = act.shape[1]
    blk = lambda w: part_of(rows, first, w)
    packed = updown.reshape(GROUPS, width // GROUPS, 2 * ff)
    return pl.pallas_call(
        functools.partial(mixed_kernel, first),
        grid=(blocks,),
        in_specs=[pl.BlockSpec(memory_space=pltpu.SMEM), blk(ff), blk(width), full(vec.shape),
                  pl.BlockSpec((GROUPS, width // GROUPS, ff), lambda i: (0, 0, 1), pipeline_mode=pl.Buffered(buffer_count=1)), ANY, ANY],
        out_specs=blk(width),
        out_shape=jax.ShapeDtypeStruct((total, width), BF),
        input_output_aliases={6: 0} if first else {},
        compiler_params=params(),
        cost_estimate=cost(2 * blocks * rows * width * ff, 14 * blocks * rows * width),
        name="mixed",
    )(counts, act, mid, vec, packed, tie, old)


FIRST = 640
SECOND = 1024


def add(a, b):
    return (a.astype(F32) + b.astype(F32)).astype(BF)


def core_sum_kernel(near, got, x_keep, x_send, y_keep, y_send):
    rep = lax.axis_index("rep")
    first = slice(0, 2 * FIRST)
    x_keep[0] = add(near[0, 0, :, first], got[0, 0, :, first])
    x_send[0] = add(near[1, 0, :, first], got[1, 0, :, first])
    for x in range(2):
        for ref, half in ((y_keep, rep), (y_send, 1 - rep)):
            at = pl.ds(pl.multiple_of(2 * FIRST + half * SECOND, 128), SECOND)
            ref[x, 0] = add(near[x, 0, :, at], got[x, 0, :, at])


def core_sum(near, got):
    _, along, rows, wide = near.shape
    blk = pl.BlockSpec((2, 1, rows, wide), lambda i: (0, i, 0, 0))
    one = pl.BlockSpec((1, rows, 2 * FIRST), lambda i: (i, 0, 0))
    two = pl.BlockSpec((2, 1, rows, SECOND), lambda i: (0, i, 0, 0))
    return pl.pallas_call(
        core_sum_kernel,
        grid=(along,),
        in_specs=[blk, blk],
        out_specs=[one, one, two, two],
        out_shape=[jax.ShapeDtypeStruct((along, rows, 2 * FIRST), BF)] * 2 + [jax.ShapeDtypeStruct((2, along, rows, SECOND), BF)] * 2,
        compiler_params=params(),
        name="core_sum",
    )(near, got)


def across_sum_kernel(x_keep, x_got, y_keep, y_got, tie, first_keep, first_send, second_keep, second_send):
    rep = lax.axis_index("rep")
    for ref, half in ((first_keep, rep), (first_send, 1 - rep)):
        at = pl.ds(pl.multiple_of(half * FIRST, 128), FIRST)
        ref[...] = add(x_keep[:, :, at], x_got[:, :, at])
    second_keep[...] = add(y_keep[0], y_got[0])
    second_send[...] = add(y_keep[1], y_got[1])


def across_sum(x_keep, x_got, y_keep, y_got, tie):
    along, rows, _ = x_keep.shape
    vm = pl.BlockSpec(memory_space=pltpu.VMEM)
    return pl.pallas_call(
        across_sum_kernel,
        in_specs=[vm] * 4 + [ANY],
        out_specs=[vm] * 4,
        out_shape=[jax.ShapeDtypeStruct((along, rows, FIRST), BF)] * 2 + [jax.ShapeDtypeStruct((along, rows, SECOND), BF)] * 2,
        compiler_params=params(),
        name="across_sum",
    )(x_keep, x_got, y_keep, y_got, tie)


def plane_sum_kernel(first_keep, first_got, second_keep, second_got, tie, *outs):
    for k, o_ref in enumerate(outs):
        o_ref[:, :FIRST] = add(first_keep[k], first_got[k])
        o_ref[:, FIRST:] = add(second_keep[k], second_got[k])


def plane_sum(first_keep, first_got, second_keep, second_got, tie):
    along, rows, _ = first_keep.shape
    vm = pl.BlockSpec(memory_space=pltpu.VMEM)
    return pl.pallas_call(
        plane_sum_kernel,
        in_specs=[vm] * 4 + [ANY],
        out_specs=[vm] * along,
        out_shape=[jax.ShapeDtypeStruct((rows, FIRST + SECOND), BF)] * along,
        compiler_params=params(),
        name="plane_sum",
    )(first_keep, first_got, second_keep, second_got, tie)


def along_sum_kernel(a, b, c, d, tie, o_ref):
    total = (a[...].astype(F32) + b[...].astype(F32)) + (c[...].astype(F32) + d[...].astype(F32))
    o_ref[...] = total.astype(BF)


def along_sum(a, b, c, d, tie):
    vm = pl.BlockSpec(memory_space=pltpu.VMEM)
    return pl.pallas_call(
        along_sum_kernel,
        in_specs=[vm] * 4 + [ANY],
        out_specs=vm,
        out_shape=jax.ShapeDtypeStruct(a.shape, BF),
        compiler_params=params(),
        name="along_sum",
    )(a, b, c, d, tie)


def finish_kernel(a_ref, b_ref, tie, in_ref, out_ref, *vectors):
    rows = a_ref.shape[0]
    front = lax.axis_index("rep") == 0
    a, b = a_ref[...].astype(F32), b_ref[...].astype(F32)
    low, high = jnp.where(front, a, b), jnp.where(front, b, a)
    total = jnp.concatenate([low[:, :FIRST], high[:, :FIRST], low[:, FIRST:], high[:, FIRST:]], axis=1)
    wide = in_ref.shape[1] + out_ref.shape[1]
    in_ref[...] = total[:, :in_ref.shape[1]]
    out_ref[...] = total[:, in_ref.shape[1]:wide]
    lines = total[:, wide:wide + 128].T
    for i, v in enumerate(vectors[:-1]):
        v[...] = lines[i:i + 1].reshape(rows)
    hidden = jnp.concatenate([lines[12 + j:13 + j] for j in range(4)], axis=1)
    vectors[-1][...] = hidden.reshape(4 * rows)


def finish(a, b, tie, width):
    rows = a.shape[0]
    vm = pl.BlockSpec(memory_space=pltpu.VMEM)
    return pl.pallas_call(
        finish_kernel,
        in_specs=[vm, vm, ANY],
        out_specs=[vm] * 15,
        out_shape=[jax.ShapeDtypeStruct((rows, 3 * width), F32), jax.ShapeDtypeStruct((rows, width), F32)]
        + [jax.ShapeDtypeStruct((rows,), F32)] * 12 + [jax.ShapeDtypeStruct((4 * rows,), F32)],
        compiler_params=params(),
        name="finish",
    )(a, b, tie)


def finish_mlp_kernel(a_ref, b_ref, tie, up_ref, down_ref):
    rows, ff = up_ref.shape
    width = ff // 4
    total = a_ref[...].astype(F32) + b_ref[...].astype(F32)
    up_ref[...] = total[:, :ff]
    for j in range(4):
        down_ref[j * rows:(j + 1) * rows] = total[:, ff + j * width:ff + (j + 1) * width]


def finish_mlp(a, b, tie):
    rows, wide = a.shape
    vm = pl.BlockSpec(memory_space=pltpu.VMEM)
    return pl.pallas_call(
        finish_mlp_kernel,
        in_specs=[vm, vm, ANY],
        out_specs=[vm, vm],
        out_shape=[jax.ShapeDtypeStruct((rows, wide // 2), F32), jax.ShapeDtypeStruct((4 * rows, wide // 8), F32)],
        compiler_params=params(),
        name="finish_mlp",
    )(a, b, tie)


CORE = [(i, i ^ 1) for i in range(16)]
ACROSS = [(i, i ^ 2) for i in range(16)]
ALONG = [[(i, ((i // 4 + k) % 4) * 4 + i % 4) for i in range(16)] for k in range(4)]
SWAP = [(0, 1), (1, 0)]


def permute(v, pairs):
    return lax.ppermute(v, "fsdp", pairs)


def gather_pieces(whole, half):
    swap = lambda v: lax.ppermute(v, "rep", SWAP)
    across = permute(whole, ACROSS)
    along = {k: permute(half, ALONG[k]) for k in (1, 3, 2)}
    both = {k: permute(along[k], ACROSS) for k in (1, 3, 2)}
    halves = []
    for k in (1, 2, 3):
        halves += [along[k], swap(along[k])]
    for k in (1, 2, 3):
        halves += [both[k], swap(both[k])]
    mine = assemble(whole, across, halves)
    return mine, permute(mine, CORE)


def gather_whole(shard):
    whole = lax.all_gather(shard, "fsdp", axis=0, tiled=True)
    whole = whole.reshape(4, 2, 2, whole.shape[0] // GROUPS, whole.shape[1])
    order = jnp.concatenate([whole[:1], whole[3:0:-1]], axis=0).transpose(2, 1, 0, 3, 4)
    return order[0].reshape((8,) + order.shape[3:]), order[1].reshape((8,) + order.shape[3:])


def regroup(updown, own):
    width = updown.shape[0]
    ff = 4 * width
    down = updown[:, ff:].reshape(width // own, own, 4, width).transpose(0, 2, 1, 3).reshape(GROUPS, 4, width // GROUPS, width)
    return jnp.concatenate([updown[:, :ff], down.transpose(0, 2, 1, 3).reshape(width, ff)], axis=1)


def over_rep(shard):
    low = shard.astype(BF)
    return low, lax.ppermute(low, "rep", SWAP)


def after(value, other):
    return lax.optimization_barrier((value, other))[0]


def local(hier, tokens, counts, cotangent, first_gain, first_shift, in_proj, query_bias, value_bias, out_proj, out_bias,
          second_gain, second_shift, up_proj, hidden_bias, down_proj, down_bias):
    images, rows, width = tokens.shape
    own = first_gain.shape[0]
    ff = 4 * width
    x = tokens.reshape(images * rows, width)
    cot = cotangent.reshape(images * rows, width)
    vectors = (first_gain, first_shift, query_bias, value_bias, out_bias, second_gain, second_shift, down_bias)
    if hier:
        mine, other = gather_pieces(*pack(vectors, hidden_bias, in_proj, out_proj))
        updown = lax.all_gather(pack_mlp(up_proj, down_proj), "fsdp", axis=0, tiled=True)
    else:
        columns = jnp.concatenate(vectors[:3] + (jnp.zeros_like(query_bias),) + vectors[3:] + (hidden_bias,)).reshape(13, own).T
        packed = jnp.concatenate([in_proj, out_proj, columns, jnp.zeros((own, 243), BF)], axis=1)
        mine, other = gather_whole(packed)
        updown = jnp.concatenate([up_proj] + [down_proj[j * own:(j + 1) * own] for j in range(4)], axis=1)
        updown = regroup(lax.all_gather(updown, "fsdp", axis=0, tiled=True), own)
    qkv, probs, att, mid, sec, back, db, vec = attn_fwd(hier, counts, x, cot, mine, other)
    owners = width // own
    bias = vec[9:13].reshape(4, owners, own).transpose(1, 0, 2).reshape(1, ff)
    act, hg, hid, grads = mlp(sec, back, bias, updown)
    if not hier:
        sums = hid[:, 12:16].reshape(GROUPS, width // GROUPS, 4).transpose(0, 2, 1).reshape(owners, 4, own).transpose(0, 2, 1)
        hid = hid.at[:, 12:16].set(sums.reshape(width, 4))
        dg = grads[:, :, ff:].reshape(GROUPS, width // GROUPS, 4, width).transpose(0, 2, 1, 3).reshape(owners, 4, own, width)
        grads = jnp.concatenate([grads[:, :, :ff].reshape(width, ff), dg.transpose(0, 2, 1, 3).reshape(width, ff)], axis=1)
    mlp_grads = lax.psum_scatter(grads.reshape(width, 2 * ff), "fsdp", scatter_dimension=0, tiled=True)
    mg, qg, near, far = attn_bwd(hier, hg, mid, back, att, qkv, probs, x, vec, updown, db, hid, mine, other)
    blocks = images * rows // 256
    tok = lambda first, last, tie, old: tokens_grad(hier, first, last - first, x, qg, mg, vec, mine, other, tie, old)
    mix = lambda tie: mixed_out(0, blocks, counts, act, mid, vec, updown, tie, tie)
    if hier:
        got = permute(far, CORE)
        x_keep, x_send, y_keep, y_send = core_sum(near, got)
        x_got, y_got = permute(x_send, ACROSS), lax.ppermute(y_send, "rep", SWAP)
        mixed = mix(x_send)
        first_keep, first_send, second_keep, second_send = across_sum(x_keep, x_got, y_keep, y_got, mixed)
        first_got, second_got = lax.ppermute(first_send, "rep", SWAP), permute(second_send, ACROSS)
        toks = tok(0, blocks // 2, first_send, mixed)
        parts = plane_sum(first_keep, first_got, second_keep, second_got, toks)
        moved = [permute(parts[k], ALONG[k]) for k in (1, 2, 3)]
        toks = tok(blocks // 2, blocks, parts[3], toks)
        mlp_grads = after(mlp_grads, parts[3])
        mlp_got = lax.ppermute(mlp_grads, "rep", SWAP)
        low = along_sum(parts[0], *moved, toks)
        grad_up, grad_down = finish_mlp(mlp_grads, mlp_got, low)
        grad_in, grad_out, *lines, hidden = finish(low, lax.ppermute(low, "rep", SWAP), grad_up, width)
    else:
        mixed = mix(far)
        toks = tok(0, blocks, far, far)
        pieces = jnp.stack([near, far]).transpose(2, 1, 0, 3, 4).reshape(width, near.shape[-1])
        a, b = over_rep(lax.psum_scatter(pieces, "fsdp", scatter_dimension=0, tiled=True))
        wide = a.astype(F32) + b.astype(F32)
        grad_in, grad_out, lines = wide[:, :3 * width], wide[:, 3 * width:4 * width], wide[:, 4 * width:].T
        hidden = lines[12:16].reshape(4 * own)
        a, b = over_rep(mlp_grads)
        mlp_grads = a.astype(F32) + b.astype(F32)
        grad_up = mlp_grads[:, :ff]
        grad_down = jnp.concatenate([mlp_grads[:, ff + j * width:ff + (j + 1) * width] for j in range(4)], axis=0)
    return (mixed.reshape(tokens.shape), toks.reshape(tokens.shape), lines[10], lines[11], grad_in, lines[4], lines[5],
            grad_out, lines[3], lines[1], lines[2], grad_up, hidden, grad_down, lines[0])


def solution(mesh):
    rows = P(("fsdp", "rep"), None, None)
    v, m = P("fsdp"), P("fsdp", None)
    in_specs = (rows, P(("fsdp", "rep")), rows, v, v, m, v, v, m, v, v, v, m, v, m, v)
    out_specs = (rows, rows, v, v, m, v, v, m, v, v, v, m, v, m, v)
    hier = mesh.shape["fsdp"] == GROUPS and mesh.shape["rep"] == 2
    return jax.shard_map(functools.partial(local, hier), mesh=mesh, in_specs=in_specs, out_specs=out_specs, check_vma=False)
```

```python
import functools
import jax
import jax.numpy as jnp
from jax import lax
from jax.experimental import pallas as pl
from jax.experimental.pallas import tpu as pltpu
from jax.sharding import PartitionSpec as P

HEADS = 12
HEAD = 64
EPS = 1e-06
BF = jnp.bfloat16
F32 = jnp.float32
VMEM = 63 << 20


def dot(a, b):
    return jnp.dot(a, b, preferred_element_type=F32)


def dot_rt(a, b):
    return lax.dot_general(a, b, (((1,), (1,)), ((), ())), preferred_element_type=F32)


def dot_lt(a, b):
    return lax.dot_general(a, b, (((0,), (0,)), ((), ())), preferred_element_type=F32)


def norm_stats(v):
    center = v - jnp.mean(v, axis=-1, keepdims=True)
    inv = lax.rsqrt(jnp.mean(center * center, axis=-1, keepdims=True) + EPS)
    return center, inv


def params(**kw):
    return pltpu.CompilerParams(vmem_limit_bytes=VMEM, **kw)


def full(shape):
    zeros = (0,) * len(shape)
    return pl.BlockSpec(shape, lambda *_: zeros, pipeline_mode=pl.Buffered(buffer_count=1))


def columns_of(rows, block, width):
    return pl.BlockSpec((rows, width), lambda *_: (0, block), pipeline_mode=pl.Buffered(buffer_count=1))


def pack_mlp_kernel(up, down, o_ref):
    rows, ff = up.shape
    width = ff // 4
    o_ref[:, :ff] = up[...]
    for j in range(4):
        o_ref[:, ff + j * width:ff + (j + 1) * width] = down[j * rows:(j + 1) * rows]


def pack_mlp(up, down):
    rows, ff = up.shape
    vm = pl.BlockSpec(memory_space=pltpu.VMEM)
    return pl.pallas_call(
        pack_mlp_kernel,
        in_specs=[vm, vm],
        out_specs=vm,
        out_shape=jax.ShapeDtypeStruct((rows, 2 * ff), BF),
        compiler_params=params(),
        name="pack_mlp",
    )(up, down)


def split_heads(pair, left):
    zero = jnp.zeros_like(pair)
    return jnp.concatenate([jnp.where(left, pair, zero), jnp.where(left, zero, pair)], axis=0)


def cost(flops, nbytes):
    return pl.CostEstimate(flops=int(flops), bytes_accessed=int(nbytes), transcendentals=0)


GROUPS = 16


def position(hier):
    if not hier:
        return 0, 0, 0
    me = lax.axis_index("fsdp")
    return me // 4, (me // 2) % 2, me % 2


def owner(hier, pos, k, other_x, other_c):
    if not hier:
        return (k * 2 + other_x) * 2 + other_c
    z, x, c = pos
    z = lax.rem(z + k, 4)
    x = 1 - x if other_x else x
    c = 1 - c if other_c else c
    return (z * 2 + x) * 2 + c


def rows_of(slot, rows):
    return pl.ds(pl.multiple_of(slot * rows, rows), rows)


def piece_copies(hier, mine, other, w_ref, sems, cols):
    pos = position(hier)
    out = []
    for c, ref in enumerate((mine, other)):
        for x in range(2):
            for k in range(4):
                slot = owner(hier, pos, (4 - k) % 4, x, c)
                out.append(pltpu.make_async_copy(ref.at[x * 4 + k, :, cols], w_ref.at[rows_of(slot, ref.shape[1])], sems.at[len(out)]))
    return out


def run_copies(copies):
    for copy in copies:
        copy.start()
    for copy in copies:
        copy.wait()


def pack_kernel(*refs):
    *vectors, hidden, in_proj, out_proj, o_ref, half_ref = refs
    rows = o_ref.shape[0]
    wide = in_proj.shape[1] + out_proj.shape[1]
    o_ref[:, :in_proj.shape[1]] = in_proj[...]
    o_ref[:, in_proj.shape[1]:wide] = out_proj[...]
    lines = [v[...].astype(F32).reshape(1, rows) for v in vectors]
    lines.insert(3, jnp.zeros((1, rows), F32))
    hidden = hidden[...].astype(F32).reshape(1, 4 * rows)
    lines += [hidden[:, j * rows:(j + 1) * rows] for j in range(4)] + [jnp.zeros((115, rows), F32)]
    o_ref[:, wide:wide + 128] = jnp.concatenate(lines, axis=0).T.astype(BF)
    o_ref[:, wide + 128:] = jnp.zeros((rows, 128), BF)
    some = half_ref.shape[1]
    half_ref[...] = o_ref[:, pl.ds(pl.multiple_of(lax.axis_index("rep") * some, 128), some)]


def pack(vectors, hidden, in_proj, out_proj):
    rows = in_proj.shape[0]
    wide = in_proj.shape[1] + out_proj.shape[1] + 256
    vm = pl.BlockSpec(memory_space=pltpu.VMEM)
    return pl.pallas_call(
        pack_kernel,
        in_specs=[vm] * (len(vectors) + 3),
        out_specs=[vm, vm],
        out_shape=[jax.ShapeDtypeStruct((rows, wide), BF), jax.ShapeDtypeStruct((rows, wide // 2), BF)],
        compiler_params=params(),
        name="pack",
    )(*vectors, hidden, in_proj, out_proj)


def assemble_kernel(own, across, *refs):
    *halves, o_ref = refs
    some = o_ref.shape[2] // 2
    rep = lax.axis_index("rep")
    here = pl.ds(pl.multiple_of(rep * some, 128), some)
    there = pl.ds(pl.multiple_of((1 - rep) * some, 128), some)
    o_ref[0] = own[...]
    o_ref[4] = across[...]
    for i in range(6):
        to = i + 1 if i < 3 else i + 2
        o_ref[to, :, here] = halves[2 * i][...]
        o_ref[to, :, there] = halves[2 * i + 1][...]


def assemble(own, across, halves):
    vm = pl.BlockSpec(memory_space=pltpu.VMEM)
    return pl.pallas_call(
        assemble_kernel,
        in_specs=[vm] * 14,
        out_specs=vm,
        out_shape=jax.ShapeDtypeStruct((8,) + own.shape, BF),
        compiler_params=params(),
        name="assemble",
    )(own, across, *halves)


def pair_cols(width, p):
    return [slice(j * width + p * 128, j * width + (p + 1) * 128) for j in range(3)]


def attn_fwd_kernel(chunk, hier, counts, x_ref, cot_ref, mine, other,
                    qkv_ref, probs_ref, att_ref, mid_ref, sec_ref, back_ref, db_ref, vec, w_ref, sems):
    step = pl.program_id(0)
    rows, width = x_ref.shape
    per = rows // 64

    @pl.when(step == 0)
    def _():
        run_copies(piece_copies(hier, mine, other, w_ref, sems, slice(None)))
        vec[...] = w_ref[:, 4 * width:4 * width + 128].astype(F32).T[:16]
        db_ref[...] = jnp.zeros_like(db_ref)

    left = lax.broadcasted_iota(jnp.int32, (64, 128), 1) < HEAD
    row = lax.broadcasted_iota(jnp.int32, (64, 128), 0)
    pos = lax.broadcasted_iota(jnp.int32, (64, width), 0)

    def project(at):
        center, inv = norm_stats(x_ref[at].astype(F32))
        first = (center * inv * vec[0:1] + vec[1:2]).astype(BF)
        for j in range(3):
            cols = slice(j * width, (j + 1) * width)
            qkv_ref[at, cols] = (dot(first, w_ref[:, cols]) + vec[2 + j:3 + j]).astype(BF)

    def attend(at):
        work = []
        for i in range(at.start // 64, at.stop // 64):
            here = slice(i * 64, (i + 1) * 64)
            work += [(i, here, row <= counts[step * per + i], pair_cols(width, p), p) for p in range(HEADS // 2)]
        scores = [dot_rt(qkv_ref[here, c[1]], split_heads(qkv_ref[here, c[0]], left)) for i, here, usable, c, p in work]
        lows = []
        for (i, here, usable, c, p), s in zip(work, scores):
            s = jnp.where(usable, s * 0.125, -1000000000.0)
            e = jnp.exp(s - jnp.max(s, axis=0, keepdims=True))
            low = (e * (1.0 / jnp.sum(e, axis=0, keepdims=True))).astype(BF)
            probs_ref[i, p] = low
            lows.append(low)
        for (i, here, usable, c, p), low in zip(work, lows):
            o = dot_lt(low, qkv_ref[here, c[2]])
            att_ref[here, c[0]] = jnp.where(left, o[:64], o[64:]).astype(BF)

    def output(at):
        mid = x_ref[at].astype(F32) + dot(att_ref[at], w_ref[:, 3 * width:4 * width]) + vec[5:6]
        mid_ref[at] = mid
        center, inv = norm_stats(mid)
        sec_ref[at] = (center * inv * vec[6:7] + vec[7:8]).astype(BF)

    chunks = [slice(r, r + chunk) for r in range(0, rows, chunk)]
    project(chunks[0])
    for c, at in enumerate(chunks):
        if c + 1 < len(chunks):
            project(chunks[c + 1])
        attend(at)
        output(at)
    total = jnp.zeros((1, width), F32)
    for i in range(per):
        at = slice(i * 64, (i + 1) * 64)
        back = jnp.where(pos <= counts[step * per + i], cot_ref[at].astype(F32), 0.0)
        back_ref[at] = back.astype(BF)
        total = total + jnp.sum(back, axis=0, keepdims=True)
    db_ref[...] += total


ANY = pl.BlockSpec(memory_space=pl.ANY)


def attn_fwd(hier, counts, x, cot, mine, other, rows=512, chunk=256):
    total, width = x.shape
    per = rows // 64
    blk = lambda w: pl.BlockSpec((rows, w), lambda i: (i, 0))
    return pl.pallas_call(
        functools.partial(attn_fwd_kernel, chunk, hier),
        grid=(total // rows,),
        in_specs=[pl.BlockSpec(memory_space=pltpu.SMEM), blk(width), blk(width), ANY, ANY],
        out_specs=[blk(3 * width), pl.BlockSpec((per, HEADS // 2, 64, 128), lambda i: (i, 0, 0, 0)),
                   blk(width), blk(width), blk(width), blk(width), pl.BlockSpec((1, width), lambda i: (0, 0)),
                   pl.BlockSpec((16, width), lambda i: (0, 0))],
        out_shape=[jax.ShapeDtypeStruct((total, 3 * width), BF),
                   jax.ShapeDtypeStruct((total // 64, HEADS // 2, 64, 128), BF),
                   jax.ShapeDtypeStruct((total, width), BF),
                   jax.ShapeDtypeStruct((total, width), F32),
                   jax.ShapeDtypeStruct((total, width), BF),
                   jax.ShapeDtypeStruct((total, width), BF),
                   jax.ShapeDtypeStruct((1, width), F32),
                   jax.ShapeDtypeStruct((16, width), F32)],
        scratch_shapes=[pltpu.VMEM((width, mine.shape[2]), BF), pltpu.SemaphoreType.DMA((GROUPS,))],
        compiler_params=params(),
        cost_estimate=cost(8 * total * width * width * 1.5, 20 * total * width),
        name="attn_fwd",
    )(counts, x, cot, mine, other)


def gelu_parts(h):
    cdf = 0.5 + 0.5 * lax.erf(h * 0.7071067811865476)
    pdf = jnp.exp(h * h * -0.5) * 0.3989422804014327
    return (h * cdf).astype(BF), cdf + h * pdf


def whole_rows(packed):
    owners, rows, four = packed.shape
    width = four // 4
    return jnp.concatenate([packed[o, :, j * width:(j + 1) * width] for o in range(owners) for j in range(4)], axis=0)


def mlp_kernel(chunk, sec_ref, back_ref, bias_ref, up, down, act_hbm, hg_hbm, hb_ref, g_hbm,
               act_ref, hg_ref, ug_ref, dg_ref, a_sems, g_sems):
    step = pl.program_id(0)
    last = pl.num_programs(0) - 1
    rows, width = sec_ref.shape
    owners, part, ff = dg_ref.shape
    slot = lax.rem(step, 2)

    def blocks(s, which):
        at = pl.ds(pl.multiple_of(s * width, width), width)
        return (pltpu.make_async_copy(act_ref.at[which], act_hbm.at[:, at], a_sems.at[which, 0]),
                pltpu.make_async_copy(hg_ref.at[which], hg_hbm.at[:, at], a_sems.at[which, 1]))

    def outputs(s):
        at = pl.ds(pl.multiple_of(s * width, width), width)
        return (pltpu.make_async_copy(dg_ref, g_hbm.at[pl.ds(s * owners, owners), :, ff:], g_sems.at[0]),
                pltpu.make_async_copy(ug_ref, g_hbm.at[:, :, at], g_sems.at[1]))

    @pl.when(step > 1)
    def _():
        for copy in blocks(step - 2, slot):
            copy.wait()

    @pl.when(step > 0)
    def _():
        for copy in outputs(step - 1):
            copy.wait()

    down = whole_rows(down)
    sums = jnp.zeros((8, width), F32)
    for r in range(rows // chunk):
        at = slice(r * chunk, (r + 1) * chunk)
        act, slope = gelu_parts(dot(sec_ref[at], up[...]) + bias_ref[...])
        act_ref[slot, at] = act
        hg = (dot_rt(back_ref[at], down) * slope).astype(BF)
        hg_ref[slot, at] = hg
        sums = sums + jnp.sum(hg.astype(F32).reshape(chunk // 8, 8, -1), axis=0)
    for copy in blocks(step, slot):
        copy.start()
    column = jnp.sum(jnp.concatenate([sums, jnp.zeros((120, width), F32)], axis=0).T, axis=1, keepdims=True)
    lane = lax.broadcasted_iota(jnp.int32, (part, 128), 1)
    for o in range(owners):
        rows_j = [column[(o * 4 + j) * part:(o * 4 + j + 1) * part] for j in range(4)]
        hb_ref[o * part:(o + 1) * part] = sum(jnp.where(lane == 12 + j, rows_j[j], 0.0) for j in range(4))
    dg = dot_lt(act_ref[slot], back_ref[...]).astype(BF)
    for o in range(owners):
        for j in range(4):
            dg_ref[o, :, j * width:(j + 1) * width] = dg[(o * 4 + j) * part:(o * 4 + j + 1) * part]
    outputs(step)[0].start()
    ug_ref[...] = dot_lt(sec_ref[...], hg_ref[slot]).astype(BF).reshape(ug_ref.shape)
    outputs(step)[1].start()

    @pl.when(step == last)
    def _():
        for copy in blocks(step - 1, 1 - slot) + blocks(step, slot) + outputs(step):
            copy.wait()


def mlp(sec, back, bias, updown, chunk=256):
    total, width = sec.shape
    ff = bias.shape[1]
    f = width
    part = width // GROUPS
    owners = GROUPS * f // ff
    col = lambda r: pl.BlockSpec((r, f), lambda i: (0, i))
    return pl.pallas_call(
        functools.partial(mlp_kernel, chunk),
        grid=(ff // f,),
        in_specs=[full(sec.shape), full(back.shape), col(1), col(width),
                  pl.BlockSpec((owners, part, ff), lambda i: (i, 0, 1))],
        out_specs=[ANY, ANY, pl.BlockSpec((owners * part, 128), lambda i: (i, 0)), ANY],
        out_shape=[jax.ShapeDtypeStruct((total, ff), BF), jax.ShapeDtypeStruct((total, ff), BF),
                   jax.ShapeDtypeStruct((width, 128), F32), jax.ShapeDtypeStruct((GROUPS, part, 2 * ff), BF)],
        scratch_shapes=[pltpu.VMEM((2, total, f), BF), pltpu.VMEM((2, total, f), BF), pltpu.VMEM((GROUPS, part, f), BF),
                        pltpu.VMEM((owners, part, ff), BF), pltpu.SemaphoreType.DMA((2, 2)), pltpu.SemaphoreType.DMA((2,))],
        compiler_params=params(),
        cost_estimate=cost(8 * total * width * ff, 12 * total * width),
        name="mlp",
    )(sec, back, bias, updown, updown.reshape(GROUPS, part, 2 * ff))


def attn_bwd_kernel(hier, hg_ref, mid_ref, back_ref, att_ref, qkv_ref, probs_ref, x_ref, vec, up, db_ref, hid_ref, mine, other,
                    mg_ref, qg_ref, near_hbm, far_hbm, out_acc, in_acc, sums, cs, ag_ref, low_ref, payload, w_ref, sems, out_sems):
    step = pl.program_id(0)
    steps = pl.num_programs(0) - 1
    rows, width = mid_ref.shape

    @pl.when(step == 0)
    def _():
        for copy in piece_copies(hier, mine, other, w_ref, sems, slice(None)):
            copy.start()
        for ref in (out_acc, in_acc, sums, cs):
            ref[...] = jnp.zeros_like(ref)

    left = lax.broadcasted_iota(jnp.int32, (64, 128), 1) < HEAD

    def body(here_too, before_too):
        if before_too:
            center, inv = norm_stats(x_ref[...].astype(F32))
            first = (center * inv).astype(BF)
            work = []
            for i in range(rows // 64):
                work += [(i, slice(i * 64, (i + 1) * 64), pair_cols(width, p), p) for p in range(HEADS // 2)]
            dps = []
            for i, here, c, p in work:
                da = split_heads(ag_ref[here, c[0]], left)
                qg_ref[here, c[2]] = dot(probs_ref[i, p], da).astype(BF)
                dps.append(dot_rt(qkv_ref[here, c[2]], da))
            dss = []
            for (i, here, c, p), dp in zip(work, dps):
                pr = probs_ref[i, p].astype(F32)
                t = dp * pr
                dss.append((t - pr * jnp.sum(t, axis=0, keepdims=True)).astype(BF))
            for (i, here, c, p), ds in zip(work, dss):
                qg_ref[here, c[1]] = (dot(ds, split_heads(qkv_ref[here, c[0]], left)) * 0.125).astype(BF)
                dq = dot_lt(ds, qkv_ref[here, c[1]])
                qg_ref[here, c[0]] = (jnp.where(left, dq[:64], dq[64:]) * 0.125).astype(BF)
        if here_too:
            sg = dot_rt(hg_ref[...], up[...])
        if before_too:
            out_acc[...] += dot_lt(att_ref[...], low_ref[...])
        if here_too:
            center, inv = norm_stats(mid_ref[...])
            n = center * inv
            e = sg * vec[6:7]
        if before_too:
            for j in range(3):
                cols = slice(j * width, (j + 1) * width)
                in_acc[:, cols] += dot_lt(first, qg_ref[:, cols])
                cs[:, cols] += jnp.sum(qg_ref[:, cols].astype(F32), axis=0, keepdims=True)
        if here_too:
            norm_grad = inv * (e - jnp.mean(e, axis=-1, keepdims=True) - n * jnp.mean(e * n, axis=-1, keepdims=True))
            mg = back_ref[...].astype(F32) + norm_grad
            mg_ref[...] = mg
            sums[0:1] += jnp.sum(sg * n, axis=0, keepdims=True)
            sums[1:2] += jnp.sum(sg, axis=0, keepdims=True)
            sums[2:3] += jnp.sum(mg, axis=0, keepdims=True)
            low = mg.astype(BF)
            low_ref[...] = low
            if not before_too:
                for copy in piece_copies(hier, mine, other, w_ref, sems, slice(None)):
                    copy.wait()
            ag_ref[...] = dot_rt(low, w_ref[:, 3 * width:4 * width]).astype(BF)

    @pl.when(step == 0)
    def _():
        body(True, False)

    @pl.when((step > 0) & (step < steps))
    def _():
        body(True, True)

    @pl.when(step == steps)
    def _():
        body(False, True)

    @pl.when(step == steps)
    def _():
        pos = position(hier)
        sent = []

        def send(cols):
            for away, ref in enumerate((near_hbm, far_hbm)):
                for x in range(2):
                    for k in range(4):
                        copy = pltpu.make_async_copy(payload.at[owner(hier, pos, k, x, away), :, cols], ref.at[x, k, :, cols],
                                                     out_sems.at[len(sent)])
                        copy.start()
                        sent.append(copy)

        def hold(cols, value):
            payload[:, :, cols] = value.astype(BF).reshape(payload.shape[0], payload.shape[1], cols.stop - cols.start)
            send(cols)

        hold(slice(3 * width, 4 * width), out_acc[...])
        tail = w_ref[:, 4 * width:4 * width + 128].astype(F32)
        gain, shift = tail[:, 0:1], tail[:, 1:2]
        gain_grad = jnp.zeros((width, 1), F32)
        shift_grad = jnp.zeros((width, 1), F32)
        for j in range(3):
            cols = slice(j * width, (j + 1) * width)
            w = w_ref[:, cols].astype(F32)
            hold(cols, gain * in_acc[:, cols] + shift * cs[:, cols])
            gain_grad = gain_grad + jnp.sum(w * in_acc[:, cols], axis=1, keepdims=True)
            shift_grad = shift_grad + jnp.sum(w * cs[:, cols], axis=1, keepdims=True)
        lines = jnp.concatenate([db_ref[...], sums[0:3], cs[:, :width], cs[:, 2 * width:], jnp.zeros((122, width), F32)], axis=0)
        lane = lax.broadcasted_iota(jnp.int32, (width, 128), 1)
        last = jnp.where(lane == 10, gain_grad, jnp.where(lane == 11, shift_grad, jnp.where(lane < 10, lines.T, hid_ref[...])))
        hold(slice(4 * width, 4 * width + 256), jnp.concatenate([last, jnp.zeros_like(last)], axis=1))
        for copy in sent:
            copy.wait()


def attn_bwd(hier, hg, mid, back, att, qkv, probs, x, vec, updown, db, hid, mine, other, rows=256):
    total, width = mid.shape
    ff = hg.shape[1]
    per = rows // 64
    wide = 4 * width + 256
    part = width // GROUPS
    steps = total // rows
    now = lambda w: pl.BlockSpec((rows, w), lambda i: (jnp.minimum(i, steps - 1), 0))
    ago = lambda w: pl.BlockSpec((rows, w), lambda i: (jnp.maximum(i - 1, 0), 0))
    return pl.pallas_call(
        functools.partial(attn_bwd_kernel, hier),
        grid=(steps + 1,),
        in_specs=[now(ff), now(width), now(width), ago(width), ago(3 * width),
                  pl.BlockSpec((per, HEADS // 2, 64, 128), lambda i: (jnp.maximum(i - 1, 0), 0, 0, 0)), ago(width),
                  full(vec.shape), columns_of(width, 0, ff), full(db.shape), full(hid.shape), ANY, ANY],
        out_specs=[now(width), ago(3 * width), ANY, ANY],
        out_shape=[jax.ShapeDtypeStruct((total, width), F32), jax.ShapeDtypeStruct((total, 3 * width), BF),
                   jax.ShapeDtypeStruct((2, 4, part, wide), BF), jax.ShapeDtypeStruct((2, 4, part, wide), BF)],
        scratch_shapes=[pltpu.VMEM((width, width), F32), pltpu.VMEM((width, 3 * width), F32), pltpu.VMEM((8, width), F32),
                        pltpu.VMEM((1, 3 * width), F32), pltpu.VMEM((rows, width), BF), pltpu.VMEM((rows, width), BF),
                        pltpu.VMEM((GROUPS, part, wide), BF), pltpu.VMEM((width, mine.shape[2]), BF), pltpu.SemaphoreType.DMA((GROUPS,)),
                        pltpu.SemaphoreType.DMA((5 * GROUPS,))],
        compiler_params=params(),
        cost_estimate=cost(2 * total * width * (ff + 9 * width), 28 * total * width),
        name="attn_bwd",
    )(hg, mid, back, att, qkv, probs, x, vec, updown, db, hid, mine, other)


def tokens_grad_kernel(hier, x_ref, qg_ref, mg_ref, vec, mine, other, tie, old, o_ref, w_ref, sems):
    @pl.when(pl.program_id(0) == 0)
    def _():
        run_copies(piece_copies(hier, mine, other, w_ref, sems, slice(0, w_ref.shape[1])))

    center, inv = norm_stats(x_ref[...].astype(F32))
    n = center * inv
    e = dot_rt(qg_ref[...], w_ref[...]) * vec[0:1]
    grad = inv * (e - jnp.mean(e, axis=-1, keepdims=True) - n * jnp.mean(e * n, axis=-1, keepdims=True))
    o_ref[...] = (mg_ref[...] + grad).astype(BF)


def part_of(rows, first, width):
    return pl.BlockSpec((rows, width), lambda i: (first + i, 0))


def tokens_grad(hier, first, blocks, x, qg, mg, vec, mine, other, tie, old, rows=256):
    total, width = x.shape
    blk = lambda w: part_of(rows, first, w)
    return pl.pallas_call(
        functools.partial(tokens_grad_kernel, hier),
        grid=(blocks,),
        in_specs=[blk(width), blk(3 * width), blk(width), full(vec.shape), ANY, ANY, ANY, ANY],
        out_specs=blk(width),
        out_shape=jax.ShapeDtypeStruct((total, width), BF),
        scratch_shapes=[pltpu.VMEM((width, 3 * width), BF), pltpu.SemaphoreType.DMA((GROUPS,))],
        input_output_aliases={7: 0} if first else {},
        compiler_params=params(),
        cost_estimate=cost(6 * blocks * rows * width * width, 14 * blocks * rows * width),
        name="tokens_grad",
    )(x, qg, mg, vec, mine, other, tie, old)


def mixed_kernel(first, counts, act_ref, mid_ref, vec, down, tie, old, o_ref):
    step = pl.program_id(0)
    per = o_ref.shape[0] // 64
    r = mid_ref[...] + dot(act_ref[...], whole_rows(down)) + vec[8:9]
    pos = lax.broadcasted_iota(jnp.int32, (64, o_ref.shape[1]), 0)
    for i in range(per):
        count = counts[(first + step) * per + i]
        o_ref[i * 64:(i + 1) * 64] = jnp.where(pos <= count, r[i * 64:(i + 1) * 64], 0.0).astype(BF)


def mixed_out(first, blocks, counts, act, mid, vec, updown, tie, old, rows=256):
    total, width = mid.shape
    ff = act.shape[1]
    blk = lambda w: part_of(rows, first, w)
    packed = updown.reshape(GROUPS, width // GROUPS, 2 * ff)
    return pl.pallas_call(
        functools.partial(mixed_kernel, first),
        grid=(blocks,),
        in_specs=[pl.BlockSpec(memory_space=pltpu.SMEM), blk(ff), blk(width), full(vec.shape),
                  pl.BlockSpec((GROUPS, width // GROUPS, ff), lambda i: (0, 0, 1), pipeline_mode=pl.Buffered(buffer_count=1)), ANY, ANY],
        out_specs=blk(width),
        out_shape=jax.ShapeDtypeStruct((total, width), BF),
        input_output_aliases={6: 0} if first else {},
        compiler_params=params(),
        cost_estimate=cost(2 * blocks * rows * width * ff, 14 * blocks * rows * width),
        name="mixed",
    )(counts, act, mid, vec, packed, tie, old)


FIRST = 512
SECOND = 1152


def add(a, b):
    return (a.astype(F32) + b.astype(F32)).astype(BF)


def core_sum_kernel(near, got, x_keep, x_send, y_keep, y_send):
    rep = lax.axis_index("rep")
    first = slice(0, 2 * FIRST)
    x_keep[0] = add(near[0, 0, :, first], got[0, 0, :, first])
    x_send[0] = add(near[1, 0, :, first], got[1, 0, :, first])
    for x in range(2):
        for ref, half in ((y_keep, rep), (y_send, 1 - rep)):
            at = pl.ds(pl.multiple_of(2 * FIRST + half * SECOND, 128), SECOND)
            ref[x, 0] = add(near[x, 0, :, at], got[x, 0, :, at])


def core_sum(near, got):
    _, along, rows, wide = near.shape
    blk = pl.BlockSpec((2, 1, rows, wide), lambda i: (0, i, 0, 0))
    one = pl.BlockSpec((1, rows, 2 * FIRST), lambda i: (i, 0, 0))
    two = pl.BlockSpec((2, 1, rows, SECOND), lambda i: (0, i, 0, 0))
    return pl.pallas_call(
        core_sum_kernel,
        grid=(along,),
        in_specs=[blk, blk],
        out_specs=[one, one, two, two],
        out_shape=[jax.ShapeDtypeStruct((along, rows, 2 * FIRST), BF)] * 2 + [jax.ShapeDtypeStruct((2, along, rows, SECOND), BF)] * 2,
        compiler_params=params(),
        name="core_sum",
    )(near, got)


def across_sum_kernel(x_keep, x_got, y_keep, y_got, tie, first_keep, first_send, second_keep, second_send):
    rep = lax.axis_index("rep")
    for ref, half in ((first_keep, rep), (first_send, 1 - rep)):
        at = pl.ds(pl.multiple_of(half * FIRST, 128), FIRST)
        ref[...] = add(x_keep[:, :, at], x_got[:, :, at])
    second_keep[...] = add(y_keep[0], y_got[0])
    second_send[...] = add(y_keep[1], y_got[1])


def across_sum(x_keep, x_got, y_keep, y_got, tie):
    along, rows, _ = x_keep.shape
    vm = pl.BlockSpec(memory_space=pltpu.VMEM)
    return pl.pallas_call(
        across_sum_kernel,
        in_specs=[vm] * 4 + [ANY],
        out_specs=[vm] * 4,
        out_shape=[jax.ShapeDtypeStruct((along, rows, FIRST), BF)] * 2 + [jax.ShapeDtypeStruct((along, rows, SECOND), BF)] * 2,
        compiler_params=params(),
        name="across_sum",
    )(x_keep, x_got, y_keep, y_got, tie)


def plane_sum_kernel(first_keep, first_got, second_keep, second_got, tie, *outs):
    for k, o_ref in enumerate(outs):
        o_ref[:, :FIRST] = add(first_keep[k], first_got[k])
        o_ref[:, FIRST:] = add(second_keep[k], second_got[k])


def plane_sum(first_keep, first_got, second_keep, second_got, tie):
    along, rows, _ = first_keep.shape
    vm = pl.BlockSpec(memory_space=pltpu.VMEM)
    return pl.pallas_call(
        plane_sum_kernel,
        in_specs=[vm] * 4 + [ANY],
        out_specs=[vm] * along,
        out_shape=[jax.ShapeDtypeStruct((rows, FIRST + SECOND), BF)] * along,
        compiler_params=params(),
        name="plane_sum",
    )(first_keep, first_got, second_keep, second_got, tie)


def along_sum_kernel(a, b, c, d, tie, o_ref):
    total = (a[...].astype(F32) + b[...].astype(F32)) + (c[...].astype(F32) + d[...].astype(F32))
    o_ref[...] = total.astype(BF)


def along_sum(a, b, c, d, tie):
    vm = pl.BlockSpec(memory_space=pltpu.VMEM)
    return pl.pallas_call(
        along_sum_kernel,
        in_specs=[vm] * 4 + [ANY],
        out_specs=vm,
        out_shape=jax.ShapeDtypeStruct(a.shape, BF),
        compiler_params=params(),
        name="along_sum",
    )(a, b, c, d, tie)


def finish_kernel(a_ref, b_ref, tie, in_ref, out_ref, *vectors):
    rows = a_ref.shape[0]
    front = lax.axis_index("rep") == 0
    a, b = a_ref[...].astype(F32), b_ref[...].astype(F32)
    low, high = jnp.where(front, a, b), jnp.where(front, b, a)
    total = jnp.concatenate([low[:, :FIRST], high[:, :FIRST], low[:, FIRST:], high[:, FIRST:]], axis=1)
    wide = in_ref.shape[1] + out_ref.shape[1]
    in_ref[...] = total[:, :in_ref.shape[1]]
    out_ref[...] = total[:, in_ref.shape[1]:wide]
    lines = total[:, wide:wide + 128].T
    for i, v in enumerate(vectors[:-1]):
        v[...] = lines[i:i + 1].reshape(rows)
    hidden = jnp.concatenate([lines[12 + j:13 + j] for j in range(4)], axis=1)
    vectors[-1][...] = hidden.reshape(4 * rows)


def finish(a, b, tie, width):
    rows = a.shape[0]
    vm = pl.BlockSpec(memory_space=pltpu.VMEM)
    return pl.pallas_call(
        finish_kernel,
        in_specs=[vm, vm, ANY],
        out_specs=[vm] * 15,
        out_shape=[jax.ShapeDtypeStruct((rows, 3 * width), F32), jax.ShapeDtypeStruct((rows, width), F32)]
        + [jax.ShapeDtypeStruct((rows,), F32)] * 12 + [jax.ShapeDtypeStruct((4 * rows,), F32)],
        compiler_params=params(),
        name="finish",
    )(a, b, tie)


def finish_mlp_kernel(a_ref, b_ref, tie, up_ref, down_ref):
    rows, ff = up_ref.shape
    width = ff // 4
    total = a_ref[...].astype(F32) + b_ref[...].astype(F32)
    up_ref[...] = total[:, :ff]
    for j in range(4):
        down_ref[j * rows:(j + 1) * rows] = total[:, ff + j * width:ff + (j + 1) * width]


def finish_mlp(a, b, tie):
    rows, wide = a.shape
    vm = pl.BlockSpec(memory_space=pltpu.VMEM)
    return pl.pallas_call(
        finish_mlp_kernel,
        in_specs=[vm, vm, ANY],
        out_specs=[vm, vm],
        out_shape=[jax.ShapeDtypeStruct((rows, wide // 2), F32), jax.ShapeDtypeStruct((4 * rows, wide // 8), F32)],
        compiler_params=params(),
        name="finish_mlp",
    )(a, b, tie)


CORE = [(i, i ^ 1) for i in range(16)]
ACROSS = [(i, i ^ 2) for i in range(16)]
ALONG = [[(i, ((i // 4 + k) % 4) * 4 + i % 4) for i in range(16)] for k in range(4)]
SWAP = [(0, 1), (1, 0)]


def permute(v, pairs):
    return lax.ppermute(v, "fsdp", pairs)


def gather_pieces(whole, half):
    swap = lambda v: lax.ppermute(v, "rep", SWAP)
    across = permute(whole, ACROSS)
    along = {k: permute(half, ALONG[k]) for k in (1, 3, 2)}
    both = {k: permute(along[k], ACROSS) for k in (1, 3, 2)}
    halves = []
    for k in (1, 2, 3):
        halves += [along[k], swap(along[k])]
    for k in (1, 2, 3):
        halves += [both[k], swap(both[k])]
    mine = assemble(whole, across, halves)
    return mine, permute(mine, CORE)


def gather_whole(shard):
    whole = lax.all_gather(shard, "fsdp", axis=0, tiled=True)
    whole = whole.reshape(4, 2, 2, whole.shape[0] // GROUPS, whole.shape[1])
    order = jnp.concatenate([whole[:1], whole[3:0:-1]], axis=0).transpose(2, 1, 0, 3, 4)
    return order[0].reshape((8,) + order.shape[3:]), order[1].reshape((8,) + order.shape[3:])


def regroup(updown, own):
    width = updown.shape[0]
    ff = 4 * width
    down = updown[:, ff:].reshape(width // own, own, 4, width).transpose(0, 2, 1, 3).reshape(GROUPS, 4, width // GROUPS, width)
    return jnp.concatenate([updown[:, :ff], down.transpose(0, 2, 1, 3).reshape(width, ff)], axis=1)


def over_rep(shard):
    low = shard.astype(BF)
    return low, lax.ppermute(low, "rep", SWAP)


def after(value, other):
    return lax.optimization_barrier((value, other))[0]


def local(hier, tokens, counts, cotangent, first_gain, first_shift, in_proj, query_bias, value_bias, out_proj, out_bias,
          second_gain, second_shift, up_proj, hidden_bias, down_proj, down_bias):
    images, rows, width = tokens.shape
    own = first_gain.shape[0]
    ff = 4 * width
    x = tokens.reshape(images * rows, width)
    cot = cotangent.reshape(images * rows, width)
    vectors = (first_gain, first_shift, query_bias, value_bias, out_bias, second_gain, second_shift, down_bias)
    if hier:
        mine, other = gather_pieces(*pack(vectors, hidden_bias, in_proj, out_proj))
        updown = lax.all_gather(pack_mlp(up_proj, down_proj), "fsdp", axis=0, tiled=True)
    else:
        columns = jnp.concatenate(vectors[:3] + (jnp.zeros_like(query_bias),) + vectors[3:] + (hidden_bias,)).reshape(13, own).T
        packed = jnp.concatenate([in_proj, out_proj, columns, jnp.zeros((own, 243), BF)], axis=1)
        mine, other = gather_whole(packed)
        updown = jnp.concatenate([up_proj] + [down_proj[j * own:(j + 1) * own] for j in range(4)], axis=1)
        updown = regroup(lax.all_gather(updown, "fsdp", axis=0, tiled=True), own)
    qkv, probs, att, mid, sec, back, db, vec = attn_fwd(hier, counts, x, cot, mine, other)
    owners = width // own
    bias = vec[9:13].reshape(4, owners, own).transpose(1, 0, 2).reshape(1, ff)
    act, hg, hid, grads = mlp(sec, back, bias, updown)
    if not hier:
        sums = hid[:, 12:16].reshape(GROUPS, width // GROUPS, 4).transpose(0, 2, 1).reshape(owners, 4, own).transpose(0, 2, 1)
        hid = hid.at[:, 12:16].set(sums.reshape(width, 4))
        dg = grads[:, :, ff:].reshape(GROUPS, width // GROUPS, 4, width).transpose(0, 2, 1, 3).reshape(owners, 4, own, width)
        grads = jnp.concatenate([grads[:, :, :ff].reshape(width, ff), dg.transpose(0, 2, 1, 3).reshape(width, ff)], axis=1)
    mlp_grads = lax.psum_scatter(grads.reshape(width, 2 * ff), "fsdp", scatter_dimension=0, tiled=True)
    mg, qg, near, far = attn_bwd(hier, hg, mid, back, att, qkv, probs, x, vec, updown, db, hid, mine, other)
    blocks = images * rows // 256
    tok = lambda first, last, tie, old: tokens_grad(hier, first, last - first, x, qg, mg, vec, mine, other, tie, old)
    mix = lambda tie: mixed_out(0, blocks, counts, act, mid, vec, updown, tie, tie)
    if hier:
        got = permute(far, CORE)
        x_keep, x_send, y_keep, y_send = core_sum(near, got)
        x_got, y_got = permute(x_send, ACROSS), lax.ppermute(y_send, "rep", SWAP)
        mixed = mix(x_send)
        first_keep, first_send, second_keep, second_send = across_sum(x_keep, x_got, y_keep, y_got, mixed)
        first_got, second_got = lax.ppermute(first_send, "rep", SWAP), permute(second_send, ACROSS)
        toks = tok(0, blocks // 2, first_send, mixed)
        parts = plane_sum(first_keep, first_got, second_keep, second_got, toks)
        moved = [permute(after(parts[k], mlp_grads), ALONG[k]) for k in (2, 1, 3)]
        toks = tok(blocks // 2, blocks, parts[3], toks)
        mlp_grads = after(mlp_grads, parts[3])
        mlp_got = lax.ppermute(mlp_grads, "rep", SWAP)
        low = along_sum(parts[0], *moved, toks)
        grad_up, grad_down = finish_mlp(mlp_grads, mlp_got, low)
        grad_in, grad_out, *lines, hidden = finish(low, lax.ppermute(low, "rep", SWAP), grad_up, width)
    else:
        mixed = mix(far)
        toks = tok(0, blocks, far, far)
        pieces = jnp.stack([near, far]).transpose(2, 1, 0, 3, 4).reshape(width, near.shape[-1])
        a, b = over_rep(lax.psum_scatter(pieces, "fsdp", scatter_dimension=0, tiled=True))
        wide = a.astype(F32) + b.astype(F32)
        grad_in, grad_out, lines = wide[:, :3 * width], wide[:, 3 * width:4 * width], wide[:, 4 * width:].T
        hidden = lines[12:16].reshape(4 * own)
        a, b = over_rep(mlp_grads)
        mlp_grads = a.astype(F32) + b.astype(F32)
        grad_up = mlp_grads[:, :ff]
        grad_down = jnp.concatenate([mlp_grads[:, ff + j * width:ff + (j + 1) * width] for j in range(4)], axis=0)
    return (mixed.reshape(tokens.shape), toks.reshape(tokens.shape), lines[10], lines[11], grad_in, lines[4], lines[5],
            grad_out, lines[3], lines[1], lines[2], grad_up, hidden, grad_down, lines[0])


def solution(mesh):
    rows = P(("fsdp", "rep"), None, None)
    v, m = P("fsdp"), P("fsdp", None)
    in_specs = (rows, P(("fsdp", "rep")), rows, v, v, m, v, v, m, v, v, v, m, v, m, v)
    out_specs = (rows, rows, v, v, m, v, v, m, v, v, v, m, v, m, v)
    hier = mesh.shape["fsdp"] == GROUPS and mesh.shape["rep"] == 2
    return jax.shard_map(functools.partial(local, hier), mesh=mesh, in_specs=in_specs, out_specs=out_specs, check_vma=False)
```

```python
import functools
import jax
import jax.numpy as jnp
from jax import lax
from jax.experimental import pallas as pl
from jax.experimental.pallas import tpu as pltpu
from jax.sharding import PartitionSpec as P

HEADS = 12
HEAD = 64
EPS = 1e-06
BF = jnp.bfloat16
F32 = jnp.float32
VMEM = 63 << 20


def dot(a, b):
    return jnp.dot(a, b, preferred_element_type=F32)


def dot_rt(a, b):
    return lax.dot_general(a, b, (((1,), (1,)), ((), ())), preferred_element_type=F32)


def dot_lt(a, b):
    return lax.dot_general(a, b, (((0,), (0,)), ((), ())), preferred_element_type=F32)


def norm_stats(v):
    center = v - jnp.mean(v, axis=-1, keepdims=True)
    inv = lax.rsqrt(jnp.mean(center * center, axis=-1, keepdims=True) + EPS)
    return center, inv


def params(**kw):
    return pltpu.CompilerParams(vmem_limit_bytes=VMEM, **kw)


def full(shape):
    zeros = (0,) * len(shape)
    return pl.BlockSpec(shape, lambda *_: zeros, pipeline_mode=pl.Buffered(buffer_count=1))


def columns_of(rows, block, width):
    return pl.BlockSpec((rows, width), lambda *_: (0, block), pipeline_mode=pl.Buffered(buffer_count=1))


def pack_mlp_kernel(up, down, o_ref):
    rows, ff = up.shape
    width = ff // 4
    o_ref[:, :ff] = up[...]
    for j in range(4):
        o_ref[:, ff + j * width:ff + (j + 1) * width] = down[j * rows:(j + 1) * rows]


def pack_mlp(up, down):
    rows, ff = up.shape
    vm = pl.BlockSpec(memory_space=pltpu.VMEM)
    return pl.pallas_call(
        pack_mlp_kernel,
        in_specs=[vm, vm],
        out_specs=vm,
        out_shape=jax.ShapeDtypeStruct((rows, 2 * ff), BF),
        compiler_params=params(),
        name="pack_mlp",
    )(up, down)


def split_heads(pair, left):
    zero = jnp.zeros_like(pair)
    return jnp.concatenate([jnp.where(left, pair, zero), jnp.where(left, zero, pair)], axis=0)


def cost(flops, nbytes):
    return pl.CostEstimate(flops=int(flops), bytes_accessed=int(nbytes), transcendentals=0)


GROUPS = 16


def position(hier):
    if not hier:
        return 0, 0, 0
    me = lax.axis_index("fsdp")
    return me // 4, (me // 2) % 2, me % 2


def owner(hier, pos, k, other_x, other_c):
    if not hier:
        return (k * 2 + other_x) * 2 + other_c
    z, x, c = pos
    z = lax.rem(z + k, 4)
    x = 1 - x if other_x else x
    c = 1 - c if other_c else c
    return (z * 2 + x) * 2 + c


def rows_of(slot, rows):
    return pl.ds(pl.multiple_of(slot * rows, rows), rows)


def piece_copies(hier, mine, other, w_ref, sems, cols):
    pos = position(hier)
    out = []
    for c, ref in enumerate((mine, other)):
        for x in range(2):
            for k in range(4):
                slot = owner(hier, pos, (4 - k) % 4, x, c)
                out.append(pltpu.make_async_copy(ref.at[x * 4 + k, :, cols], w_ref.at[rows_of(slot, ref.shape[1])], sems.at[len(out)]))
    return out


def run_copies(copies):
    for copy in copies:
        copy.start()
    for copy in copies:
        copy.wait()


def pack_kernel(*refs):
    *vectors, hidden, in_proj, out_proj, o_ref, half_ref = refs
    rows = o_ref.shape[0]
    wide = in_proj.shape[1] + out_proj.shape[1]
    o_ref[:, :in_proj.shape[1]] = in_proj[...]
    o_ref[:, in_proj.shape[1]:wide] = out_proj[...]
    lines = [v[...].astype(F32).reshape(1, rows) for v in vectors]
    lines.insert(3, jnp.zeros((1, rows), F32))
    hidden = hidden[...].astype(F32).reshape(1, 4 * rows)
    lines += [hidden[:, j * rows:(j + 1) * rows] for j in range(4)] + [jnp.zeros((115, rows), F32)]
    o_ref[:, wide:wide + 128] = jnp.concatenate(lines, axis=0).T.astype(BF)
    o_ref[:, wide + 128:] = jnp.zeros((rows, 128), BF)
    some = half_ref.shape[1]
    half_ref[...] = o_ref[:, pl.ds(pl.multiple_of(lax.axis_index("rep") * some, 128), some)]


def pack(vectors, hidden, in_proj, out_proj):
    rows = in_proj.shape[0]
    wide = in_proj.shape[1] + out_proj.shape[1] + 256
    vm = pl.BlockSpec(memory_space=pltpu.VMEM)
    return pl.pallas_call(
        pack_kernel,
        in_specs=[vm] * (len(vectors) + 3),
        out_specs=[vm, vm],
        out_shape=[jax.ShapeDtypeStruct((rows, wide), BF), jax.ShapeDtypeStruct((rows, wide // 2), BF)],
        compiler_params=params(),
        name="pack",
    )(*vectors, hidden, in_proj, out_proj)


def assemble_kernel(own, across, *refs):
    *halves, o_ref = refs
    some = o_ref.shape[2] // 2
    rep = lax.axis_index("rep")
    here = pl.ds(pl.multiple_of(rep * some, 128), some)
    there = pl.ds(pl.multiple_of((1 - rep) * some, 128), some)
    o_ref[0] = own[...]
    o_ref[4] = across[...]
    for i in range(6):
        to = i + 1 if i < 3 else i + 2
        o_ref[to, :, here] = halves[2 * i][...]
        o_ref[to, :, there] = halves[2 * i + 1][...]


def assemble(own, across, halves):
    vm = pl.BlockSpec(memory_space=pltpu.VMEM)
    return pl.pallas_call(
        assemble_kernel,
        in_specs=[vm] * 14,
        out_specs=vm,
        out_shape=jax.ShapeDtypeStruct((8,) + own.shape, BF),
        compiler_params=params(),
        name="assemble",
    )(own, across, *halves)


def pair_cols(width, p):
    return [slice(j * width + p * 128, j * width + (p + 1) * 128) for j in range(3)]


def attn_fwd_kernel(chunk, hier, counts, x_ref, cot_ref, mine, other,
                    qkv_ref, probs_ref, att_ref, mid_ref, sec_ref, back_ref, db_ref, vec, w_ref, sems):
    step = pl.program_id(0)
    rows, width = x_ref.shape
    per = rows // 64

    @pl.when(step == 0)
    def _():
        run_copies(piece_copies(hier, mine, other, w_ref, sems, slice(None)))
        vec[...] = w_ref[:, 4 * width:4 * width + 128].astype(F32).T[:16]
        db_ref[...] = jnp.zeros_like(db_ref)

    left = lax.broadcasted_iota(jnp.int32, (64, 128), 1) < HEAD
    row = lax.broadcasted_iota(jnp.int32, (64, 128), 0)
    pos = lax.broadcasted_iota(jnp.int32, (64, width), 0)

    def project(at):
        center, inv = norm_stats(x_ref[at].astype(F32))
        first = (center * inv * vec[0:1] + vec[1:2]).astype(BF)
        for j in range(3):
            cols = slice(j * width, (j + 1) * width)
            qkv_ref[at, cols] = (dot(first, w_ref[:, cols]) + vec[2 + j:3 + j]).astype(BF)

    def attend(at):
        work = []
        for i in range(at.start // 64, at.stop // 64):
            here = slice(i * 64, (i + 1) * 64)
            work += [(i, here, row <= counts[step * per + i], pair_cols(width, p), p) for p in range(HEADS // 2)]
        scores = [dot_rt(qkv_ref[here, c[1]], split_heads(qkv_ref[here, c[0]], left)) for i, here, usable, c, p in work]
        lows = []
        for (i, here, usable, c, p), s in zip(work, scores):
            s = jnp.where(usable, s * 0.125, -1000000000.0)
            e = jnp.exp(s - jnp.max(s, axis=0, keepdims=True))
            low = (e * (1.0 / jnp.sum(e, axis=0, keepdims=True))).astype(BF)
            probs_ref[i, p] = low
            lows.append(low)
        for (i, here, usable, c, p), low in zip(work, lows):
            o = dot_lt(low, qkv_ref[here, c[2]])
            att_ref[here, c[0]] = jnp.where(left, o[:64], o[64:]).astype(BF)

    def output(at):
        mid = x_ref[at].astype(F32) + dot(att_ref[at], w_ref[:, 3 * width:4 * width]) + vec[5:6]
        mid_ref[at] = mid
        center, inv = norm_stats(mid)
        sec_ref[at] = (center * inv * vec[6:7] + vec[7:8]).astype(BF)

    chunks = [slice(r, r + chunk) for r in range(0, rows, chunk)]
    project(chunks[0])
    for c, at in enumerate(chunks):
        if c + 1 < len(chunks):
            project(chunks[c + 1])
        attend(at)
        output(at)
    total = jnp.zeros((1, width), F32)
    for i in range(per):
        at = slice(i * 64, (i + 1) * 64)
        back = jnp.where(pos <= counts[step * per + i], cot_ref[at].astype(F32), 0.0)
        back_ref[at] = back.astype(BF)
        total = total + jnp.sum(back, axis=0, keepdims=True)
    db_ref[...] += total


ANY = pl.BlockSpec(memory_space=pl.ANY)


def attn_fwd(hier, counts, x, cot, mine, other, rows=512, chunk=256):
    total, width = x.shape
    per = rows // 64
    blk = lambda w: pl.BlockSpec((rows, w), lambda i: (i, 0))
    return pl.pallas_call(
        functools.partial(attn_fwd_kernel, chunk, hier),
        grid=(total // rows,),
        in_specs=[pl.BlockSpec(memory_space=pltpu.SMEM), blk(width), blk(width), ANY, ANY],
        out_specs=[blk(3 * width), pl.BlockSpec((per, HEADS // 2, 64, 128), lambda i: (i, 0, 0, 0)),
                   blk(width), blk(width), blk(width), blk(width), pl.BlockSpec((1, width), lambda i: (0, 0)),
                   pl.BlockSpec((16, width), lambda i: (0, 0))],
        out_shape=[jax.ShapeDtypeStruct((total, 3 * width), BF),
                   jax.ShapeDtypeStruct((total // 64, HEADS // 2, 64, 128), BF),
                   jax.ShapeDtypeStruct((total, width), BF),
                   jax.ShapeDtypeStruct((total, width), F32),
                   jax.ShapeDtypeStruct((total, width), BF),
                   jax.ShapeDtypeStruct((total, width), BF),
                   jax.ShapeDtypeStruct((1, width), F32),
                   jax.ShapeDtypeStruct((16, width), F32)],
        scratch_shapes=[pltpu.VMEM((width, mine.shape[2]), BF), pltpu.SemaphoreType.DMA((GROUPS,))],
        compiler_params=params(),
        cost_estimate=cost(8 * total * width * width * 1.5, 20 * total * width),
        name="attn_fwd",
    )(counts, x, cot, mine, other)


def gelu_parts(h):
    cdf = 0.5 + 0.5 * lax.erf(h * 0.7071067811865476)
    pdf = jnp.exp(h * h * -0.5) * 0.3989422804014327
    return (h * cdf).astype(BF), cdf + h * pdf


def whole_rows(packed):
    owners, rows, four = packed.shape
    width = four // 4
    return jnp.concatenate([packed[o, :, j * width:(j + 1) * width] for o in range(owners) for j in range(4)], axis=0)


def mlp_kernel(chunk, sec_ref, back_ref, bias_ref, up, down, act_hbm, hg_hbm, hb_ref, g_hbm,
               act_ref, hg_ref, ug_ref, dg_ref, a_sems, g_sems):
    step = pl.program_id(0)
    last = pl.num_programs(0) - 1
    rows, width = sec_ref.shape
    owners, part, ff = dg_ref.shape
    slot = lax.rem(step, 2)

    def blocks(s, which):
        at = pl.ds(pl.multiple_of(s * width, width), width)
        return (pltpu.make_async_copy(act_ref.at[which], act_hbm.at[:, at], a_sems.at[which, 0]),
                pltpu.make_async_copy(hg_ref.at[which], hg_hbm.at[:, at], a_sems.at[which, 1]))

    def outputs(s):
        at = pl.ds(pl.multiple_of(s * width, width), width)
        return (pltpu.make_async_copy(dg_ref, g_hbm.at[pl.ds(s * owners, owners), :, ff:], g_sems.at[0]),
                pltpu.make_async_copy(ug_ref, g_hbm.at[:, :, at], g_sems.at[1]))

    @pl.when(step > 1)
    def _():
        for copy in blocks(step - 2, slot):
            copy.wait()

    @pl.when(step > 0)
    def _():
        for copy in outputs(step - 1):
            copy.wait()

    down = whole_rows(down)
    sums = jnp.zeros((8, width), F32)
    for r in range(rows // chunk):
        at = slice(r * chunk, (r + 1) * chunk)
        act, slope = gelu_parts(dot(sec_ref[at], up[...]) + bias_ref[...])
        act_ref[slot, at] = act
        hg = (dot_rt(back_ref[at], down) * slope).astype(BF)
        hg_ref[slot, at] = hg
        sums = sums + jnp.sum(hg.astype(F32).reshape(chunk // 8, 8, -1), axis=0)
    for copy in blocks(step, slot):
        copy.start()
    column = jnp.sum(jnp.concatenate([sums, jnp.zeros((120, width), F32)], axis=0).T, axis=1, keepdims=True)
    lane = lax.broadcasted_iota(jnp.int32, (part, 128), 1)
    for o in range(owners):
        rows_j = [column[(o * 4 + j) * part:(o * 4 + j + 1) * part] for j in range(4)]
        hb_ref[o * part:(o + 1) * part] = sum(jnp.where(lane == 12 + j, rows_j[j], 0.0) for j in range(4))
    dg = dot_lt(act_ref[slot], back_ref[...]).astype(BF)
    for o in range(owners):
        for j in range(4):
            dg_ref[o, :, j * width:(j + 1) * width] = dg[(o * 4 + j) * part:(o * 4 + j + 1) * part]
    outputs(step)[0].start()
    ug_ref[...] = dot_lt(sec_ref[...], hg_ref[slot]).astype(BF).reshape(ug_ref.shape)
    outputs(step)[1].start()

    @pl.when(step == last)
    def _():
        for copy in blocks(step - 1, 1 - slot) + blocks(step, slot) + outputs(step):
            copy.wait()


def mlp(sec, back, bias, updown, chunk=256):
    total, width = sec.shape
    ff = bias.shape[1]
    f = width
    part = width // GROUPS
    owners = GROUPS * f // ff
    col = lambda r: pl.BlockSpec((r, f), lambda i: (0, i))
    return pl.pallas_call(
        functools.partial(mlp_kernel, chunk),
        grid=(ff // f,),
        in_specs=[full(sec.shape), full(back.shape), col(1), col(width),
                  pl.BlockSpec((owners, part, ff), lambda i: (i, 0, 1))],
        out_specs=[ANY, ANY, pl.BlockSpec((owners * part, 128), lambda i: (i, 0)), ANY],
        out_shape=[jax.ShapeDtypeStruct((total, ff), BF), jax.ShapeDtypeStruct((total, ff), BF),
                   jax.ShapeDtypeStruct((width, 128), F32), jax.ShapeDtypeStruct((GROUPS, part, 2 * ff), BF)],
        scratch_shapes=[pltpu.VMEM((2, total, f), BF), pltpu.VMEM((2, total, f), BF), pltpu.VMEM((GROUPS, part, f), BF),
                        pltpu.VMEM((owners, part, ff), BF), pltpu.SemaphoreType.DMA((2, 2)), pltpu.SemaphoreType.DMA((2,))],
        compiler_params=params(),
        cost_estimate=cost(8 * total * width * ff, 12 * total * width),
        name="mlp",
    )(sec, back, bias, updown, updown.reshape(GROUPS, part, 2 * ff))


def attn_bwd_kernel(hier, hg_ref, mid_ref, back_ref, att_ref, qkv_ref, probs_ref, x_ref, vec, up, db_ref, hid_ref, mine, other,
                    mg_ref, qg_ref, near_hbm, far_hbm, out_acc, in_acc, sums, cs, ag_ref, low_ref, payload, w_ref, sems, out_sems):
    step = pl.program_id(0)
    steps = pl.num_programs(0) - 1
    rows, width = mid_ref.shape

    @pl.when(step == 0)
    def _():
        for copy in piece_copies(hier, mine, other, w_ref, sems, slice(None)):
            copy.start()
        for ref in (out_acc, in_acc, sums, cs):
            ref[...] = jnp.zeros_like(ref)

    left = lax.broadcasted_iota(jnp.int32, (64, 128), 1) < HEAD

    def body(here_too, before_too):
        if before_too:
            center, inv = norm_stats(x_ref[...].astype(F32))
            first = (center * inv).astype(BF)
            work = []
            for i in range(rows // 64):
                work += [(i, slice(i * 64, (i + 1) * 64), pair_cols(width, p), p) for p in range(HEADS // 2)]
            dps = []
            for i, here, c, p in work:
                da = split_heads(ag_ref[here, c[0]], left)
                qg_ref[here, c[2]] = dot(probs_ref[i, p], da).astype(BF)
                dps.append(dot_rt(qkv_ref[here, c[2]], da))
            dss = []
            for (i, here, c, p), dp in zip(work, dps):
                pr = probs_ref[i, p].astype(F32)
                t = dp * pr
                dss.append((t - pr * jnp.sum(t, axis=0, keepdims=True)).astype(BF))
            for (i, here, c, p), ds in zip(work, dss):
                qg_ref[here, c[1]] = (dot(ds, split_heads(qkv_ref[here, c[0]], left)) * 0.125).astype(BF)
                dq = dot_lt(ds, qkv_ref[here, c[1]])
                qg_ref[here, c[0]] = (jnp.where(left, dq[:64], dq[64:]) * 0.125).astype(BF)
        if here_too:
            sg = dot_rt(hg_ref[...], up[...])
        if before_too:
            out_acc[...] += dot_lt(att_ref[...], low_ref[...])
        if here_too:
            center, inv = norm_stats(mid_ref[...])
            n = center * inv
            e = sg * vec[6:7]
        if before_too:
            for j in range(3):
                cols = slice(j * width, (j + 1) * width)
                in_acc[:, cols] += dot_lt(first, qg_ref[:, cols])
                cs[:, cols] += jnp.sum(qg_ref[:, cols].astype(F32), axis=0, keepdims=True)
        if here_too:
            norm_grad = inv * (e - jnp.mean(e, axis=-1, keepdims=True) - n * jnp.mean(e * n, axis=-1, keepdims=True))
            mg = back_ref[...].astype(F32) + norm_grad
            mg_ref[...] = mg
            sums[0:1] += jnp.sum(sg * n, axis=0, keepdims=True)
            sums[1:2] += jnp.sum(sg, axis=0, keepdims=True)
            sums[2:3] += jnp.sum(mg, axis=0, keepdims=True)
            low = mg.astype(BF)
            low_ref[...] = low
            if not before_too:
                for copy in piece_copies(hier, mine, other, w_ref, sems, slice(None)):
                    copy.wait()
            ag_ref[...] = dot_rt(low, w_ref[:, 3 * width:4 * width]).astype(BF)

    @pl.when(step == 0)
    def _():
        body(True, False)

    @pl.when((step > 0) & (step < steps))
    def _():
        body(True, True)

    @pl.when(step == steps)
    def _():
        body(False, True)

    @pl.when(step == steps)
    def _():
        pos = position(hier)
        sent = []

        def send(cols):
            for away, ref in enumerate((near_hbm, far_hbm)):
                for x in range(2):
                    for k in range(4):
                        copy = pltpu.make_async_copy(payload.at[owner(hier, pos, k, x, away), :, cols], ref.at[x, k, :, cols],
                                                     out_sems.at[len(sent)])
                        copy.start()
                        sent.append(copy)

        def hold(cols, value):
            payload[:, :, cols] = value.astype(BF).reshape(payload.shape[0], payload.shape[1], cols.stop - cols.start)
            send(cols)

        hold(slice(3 * width, 4 * width), out_acc[...])
        tail = w_ref[:, 4 * width:4 * width + 128].astype(F32)
        gain, shift = tail[:, 0:1], tail[:, 1:2]
        gain_grad = jnp.zeros((width, 1), F32)
        shift_grad = jnp.zeros((width, 1), F32)
        for j in range(3):
            cols = slice(j * width, (j + 1) * width)
            w = w_ref[:, cols].astype(F32)
            hold(cols, gain * in_acc[:, cols] + shift * cs[:, cols])
            gain_grad = gain_grad + jnp.sum(w * in_acc[:, cols], axis=1, keepdims=True)
            shift_grad = shift_grad + jnp.sum(w * cs[:, cols], axis=1, keepdims=True)
        lines = jnp.concatenate([db_ref[...], sums[0:3], cs[:, :width], cs[:, 2 * width:], jnp.zeros((122, width), F32)], axis=0)
        lane = lax.broadcasted_iota(jnp.int32, (width, 128), 1)
        last = jnp.where(lane == 10, gain_grad, jnp.where(lane == 11, shift_grad, jnp.where(lane < 10, lines.T, hid_ref[...])))
        hold(slice(4 * width, 4 * width + 256), jnp.concatenate([last, jnp.zeros_like(last)], axis=1))
        for copy in sent:
            copy.wait()


def attn_bwd(hier, hg, mid, back, att, qkv, probs, x, vec, updown, db, hid, mine, other, rows=256):
    total, width = mid.shape
    ff = hg.shape[1]
    per = rows // 64
    wide = 4 * width + 256
    part = width // GROUPS
    steps = total // rows
    now = lambda w: pl.BlockSpec((rows, w), lambda i: (jnp.minimum(i, steps - 1), 0))
    ago = lambda w: pl.BlockSpec((rows, w), lambda i: (jnp.maximum(i - 1, 0), 0))
    return pl.pallas_call(
        functools.partial(attn_bwd_kernel, hier),
        grid=(steps + 1,),
        in_specs=[now(ff), now(width), now(width), ago(width), ago(3 * width),
                  pl.BlockSpec((per, HEADS // 2, 64, 128), lambda i: (jnp.maximum(i - 1, 0), 0, 0, 0)), ago(width),
                  full(vec.shape), columns_of(width, 0, ff), full(db.shape), full(hid.shape), ANY, ANY],
        out_specs=[now(width), ago(3 * width), ANY, ANY],
        out_shape=[jax.ShapeDtypeStruct((total, width), F32), jax.ShapeDtypeStruct((total, 3 * width), BF),
                   jax.ShapeDtypeStruct((2, 4, part, wide), BF), jax.ShapeDtypeStruct((2, 4, part, wide), BF)],
        scratch_shapes=[pltpu.VMEM((width, width), F32), pltpu.VMEM((width, 3 * width), F32), pltpu.VMEM((8, width), F32),
                        pltpu.VMEM((1, 3 * width), F32), pltpu.VMEM((rows, width), BF), pltpu.VMEM((rows, width), BF),
                        pltpu.VMEM((GROUPS, part, wide), BF), pltpu.VMEM((width, mine.shape[2]), BF), pltpu.SemaphoreType.DMA((GROUPS,)),
                        pltpu.SemaphoreType.DMA((5 * GROUPS,))],
        compiler_params=params(),
        cost_estimate=cost(2 * total * width * (ff + 9 * width), 28 * total * width),
        name="attn_bwd",
    )(hg, mid, back, att, qkv, probs, x, vec, updown, db, hid, mine, other)


def tokens_grad_kernel(hier, x_ref, qg_ref, mg_ref, vec, mine, other, tie, old, o_ref, w_ref, sems):
    @pl.when(pl.program_id(0) == 0)
    def _():
        run_copies(piece_copies(hier, mine, other, w_ref, sems, slice(0, w_ref.shape[1])))

    center, inv = norm_stats(x_ref[...].astype(F32))
    n = center * inv
    e = dot_rt(qg_ref[...], w_ref[...]) * vec[0:1]
    grad = inv * (e - jnp.mean(e, axis=-1, keepdims=True) - n * jnp.mean(e * n, axis=-1, keepdims=True))
    o_ref[...] = (mg_ref[...] + grad).astype(BF)


def part_of(rows, first, width):
    return pl.BlockSpec((rows, width), lambda i: (first + i, 0))


def tokens_grad(hier, first, blocks, x, qg, mg, vec, mine, other, tie, old, rows=256):
    total, width = x.shape
    blk = lambda w: part_of(rows, first, w)
    return pl.pallas_call(
        functools.partial(tokens_grad_kernel, hier),
        grid=(blocks,),
        in_specs=[blk(width), blk(3 * width), blk(width), full(vec.shape), ANY, ANY, ANY, ANY],
        out_specs=blk(width),
        out_shape=jax.ShapeDtypeStruct((total, width), BF),
        scratch_shapes=[pltpu.VMEM((width, 3 * width), BF), pltpu.SemaphoreType.DMA((GROUPS,))],
        input_output_aliases={7: 0} if first else {},
        compiler_params=params(),
        cost_estimate=cost(6 * blocks * rows * width * width, 14 * blocks * rows * width),
        name="tokens_grad",
    )(x, qg, mg, vec, mine, other, tie, old)


def mixed_kernel(first, counts, act_ref, mid_ref, vec, down, tie, old, o_ref):
    step = pl.program_id(0)
    per = o_ref.shape[0] // 64
    r = mid_ref[...] + dot(act_ref[...], whole_rows(down)) + vec[8:9]
    pos = lax.broadcasted_iota(jnp.int32, (64, o_ref.shape[1]), 0)
    for i in range(per):
        count = counts[(first + step) * per + i]
        o_ref[i * 64:(i + 1) * 64] = jnp.where(pos <= count, r[i * 64:(i + 1) * 64], 0.0).astype(BF)


def mixed_out(first, blocks, counts, act, mid, vec, updown, tie, old, rows=256):
    total, width = mid.shape
    ff = act.shape[1]
    blk = lambda w: part_of(rows, first, w)
    packed = updown.reshape(GROUPS, width // GROUPS, 2 * ff)
    return pl.pallas_call(
        functools.partial(mixed_kernel, first),
        grid=(blocks,),
        in_specs=[pl.BlockSpec(memory_space=pltpu.SMEM), blk(ff), blk(width), full(vec.shape),
                  pl.BlockSpec((GROUPS, width // GROUPS, ff), lambda i: (0, 0, 1), pipeline_mode=pl.Buffered(buffer_count=1)), ANY, ANY],
        out_specs=blk(width),
        out_shape=jax.ShapeDtypeStruct((total, width), BF),
        input_output_aliases={6: 0} if first else {},
        compiler_params=params(),
        cost_estimate=cost(2 * blocks * rows * width * ff, 14 * blocks * rows * width),
        name="mixed",
    )(counts, act, mid, vec, packed, tie, old)


FIRST = 512
SECOND = 1152


def add(a, b):
    return (a.astype(F32) + b.astype(F32)).astype(BF)


def core_sum_kernel(near, got, x_keep, x_send, y_keep, y_send):
    rep = lax.axis_index("rep")
    first = slice(0, 2 * FIRST)
    x_keep[0] = add(near[0, 0, :, first], got[0, 0, :, first])
    x_send[0] = add(near[1, 0, :, first], got[1, 0, :, first])
    for x in range(2):
        for ref, half in ((y_keep, rep), (y_send, 1 - rep)):
            at = pl.ds(pl.multiple_of(2 * FIRST + half * SECOND, 128), SECOND)
            ref[x, 0] = add(near[x, 0, :, at], got[x, 0, :, at])


def core_sum(near, got):
    _, along, rows, wide = near.shape
    blk = pl.BlockSpec((2, 1, rows, wide), lambda i: (0, i, 0, 0))
    one = pl.BlockSpec((1, rows, 2 * FIRST), lambda i: (i, 0, 0))
    two = pl.BlockSpec((2, 1, rows, SECOND), lambda i: (0, i, 0, 0))
    return pl.pallas_call(
        core_sum_kernel,
        grid=(along,),
        in_specs=[blk, blk],
        out_specs=[one, one, two, two],
        out_shape=[jax.ShapeDtypeStruct((along, rows, 2 * FIRST), BF)] * 2 + [jax.ShapeDtypeStruct((2, along, rows, SECOND), BF)] * 2,
        compiler_params=params(),
        name="core_sum",
    )(near, got)


def across_sum_kernel(x_keep, x_got, y_keep, y_got, tie, first_keep, first_send, second_keep, second_send):
    rep = lax.axis_index("rep")
    for ref, half in ((first_keep, rep), (first_send, 1 - rep)):
        at = pl.ds(pl.multiple_of(half * FIRST, 128), FIRST)
        ref[...] = add(x_keep[:, :, at], x_got[:, :, at])
    second_keep[...] = add(y_keep[0], y_got[0])
    second_send[...] = add(y_keep[1], y_got[1])


def across_sum(x_keep, x_got, y_keep, y_got, tie):
    along, rows, _ = x_keep.shape
    vm = pl.BlockSpec(memory_space=pltpu.VMEM)
    return pl.pallas_call(
        across_sum_kernel,
        in_specs=[vm] * 4 + [ANY],
        out_specs=[vm] * 4,
        out_shape=[jax.ShapeDtypeStruct((along, rows, FIRST), BF)] * 2 + [jax.ShapeDtypeStruct((along, rows, SECOND), BF)] * 2,
        compiler_params=params(),
        name="across_sum",
    )(x_keep, x_got, y_keep, y_got, tie)


def plane_sum_kernel(first_keep, first_got, second_keep, second_got, tie, *outs):
    for k, o_ref in enumerate(outs):
        o_ref[:, :FIRST] = add(first_keep[k], first_got[k])
        o_ref[:, FIRST:] = add(second_keep[k], second_got[k])


def plane_sum(first_keep, first_got, second_keep, second_got, tie):
    along, rows, _ = first_keep.shape
    vm = pl.BlockSpec(memory_space=pltpu.VMEM)
    return pl.pallas_call(
        plane_sum_kernel,
        in_specs=[vm] * 4 + [ANY],
        out_specs=[vm] * along,
        out_shape=[jax.ShapeDtypeStruct((rows, FIRST + SECOND), BF)] * along,
        compiler_params=params(),
        name="plane_sum",
    )(first_keep, first_got, second_keep, second_got, tie)


def along_sum_kernel(a, b, c, d, tie, o_ref):
    total = (a[...].astype(F32) + b[...].astype(F32)) + (c[...].astype(F32) + d[...].astype(F32))
    o_ref[...] = total.astype(BF)


def along_sum(a, b, c, d, tie):
    vm = pl.BlockSpec(memory_space=pltpu.VMEM)
    return pl.pallas_call(
        along_sum_kernel,
        in_specs=[vm] * 4 + [ANY],
        out_specs=vm,
        out_shape=jax.ShapeDtypeStruct(a.shape, BF),
        compiler_params=params(),
        name="along_sum",
    )(a, b, c, d, tie)


def finish_kernel(a_ref, b_ref, tie, in_ref, out_ref, *vectors):
    rows = a_ref.shape[0]
    front = lax.axis_index("rep") == 0
    a, b = a_ref[...].astype(F32), b_ref[...].astype(F32)
    low, high = jnp.where(front, a, b), jnp.where(front, b, a)
    total = jnp.concatenate([low[:, :FIRST], high[:, :FIRST], low[:, FIRST:], high[:, FIRST:]], axis=1)
    wide = in_ref.shape[1] + out_ref.shape[1]
    in_ref[...] = total[:, :in_ref.shape[1]]
    out_ref[...] = total[:, in_ref.shape[1]:wide]
    lines = total[:, wide:wide + 128].T
    for i, v in enumerate(vectors[:-1]):
        v[...] = lines[i:i + 1].reshape(rows)
    hidden = jnp.concatenate([lines[12 + j:13 + j] for j in range(4)], axis=1)
    vectors[-1][...] = hidden.reshape(4 * rows)


def finish(a, b, tie, width):
    rows = a.shape[0]
    vm = pl.BlockSpec(memory_space=pltpu.VMEM)
    return pl.pallas_call(
        finish_kernel,
        in_specs=[vm, vm, ANY],
        out_specs=[vm] * 15,
        out_shape=[jax.ShapeDtypeStruct((rows, 3 * width), F32), jax.ShapeDtypeStruct((rows, width), F32)]
        + [jax.ShapeDtypeStruct((rows,), F32)] * 12 + [jax.ShapeDtypeStruct((4 * rows,), F32)],
        compiler_params=params(),
        name="finish",
    )(a, b, tie)


def finish_mlp_kernel(a_ref, b_ref, tie, up_ref, down_ref):
    rows, ff = up_ref.shape
    width = ff // 4
    total = a_ref[...].astype(F32) + b_ref[...].astype(F32)
    up_ref[...] = total[:, :ff]
    for j in range(4):
        down_ref[j * rows:(j + 1) * rows] = total[:, ff + j * width:ff + (j + 1) * width]


def finish_mlp(a, b, tie):
    rows, wide = a.shape
    vm = pl.BlockSpec(memory_space=pltpu.VMEM)
    return pl.pallas_call(
        finish_mlp_kernel,
        in_specs=[vm, vm, ANY],
        out_specs=[vm, vm],
        out_shape=[jax.ShapeDtypeStruct((rows, wide // 2), F32), jax.ShapeDtypeStruct((4 * rows, wide // 8), F32)],
        compiler_params=params(),
        name="finish_mlp",
    )(a, b, tie)


CORE = [(i, i ^ 1) for i in range(16)]
ACROSS = [(i, i ^ 2) for i in range(16)]
ALONG = [[(i, ((i // 4 + k) % 4) * 4 + i % 4) for i in range(16)] for k in range(4)]
SWAP = [(0, 1), (1, 0)]


def permute(v, pairs):
    return lax.ppermute(v, "fsdp", pairs)


def gather_pieces(whole, half):
    swap = lambda v: lax.ppermute(v, "rep", SWAP)
    across = permute(whole, ACROSS)
    along = {k: permute(half, ALONG[k]) for k in (1, 3, 2)}
    both = {k: permute(along[k], ACROSS) for k in (1, 3, 2)}
    halves = []
    for k in (1, 2, 3):
        halves += [along[k], swap(along[k])]
    for k in (1, 2, 3):
        halves += [both[k], swap(both[k])]
    mine = assemble(whole, across, halves)
    return mine, permute(mine, CORE)


def gather_whole(shard):
    whole = lax.all_gather(shard, "fsdp", axis=0, tiled=True)
    whole = whole.reshape(4, 2, 2, whole.shape[0] // GROUPS, whole.shape[1])
    order = jnp.concatenate([whole[:1], whole[3:0:-1]], axis=0).transpose(2, 1, 0, 3, 4)
    return order[0].reshape((8,) + order.shape[3:]), order[1].reshape((8,) + order.shape[3:])


def regroup(updown, own):
    width = updown.shape[0]
    ff = 4 * width
    down = updown[:, ff:].reshape(width // own, own, 4, width).transpose(0, 2, 1, 3).reshape(GROUPS, 4, width // GROUPS, width)
    return jnp.concatenate([updown[:, :ff], down.transpose(0, 2, 1, 3).reshape(width, ff)], axis=1)


def over_rep(shard):
    low = shard.astype(BF)
    return low, lax.ppermute(low, "rep", SWAP)


def after(value, other):
    return lax.optimization_barrier((value, other))[0]


def local(hier, tokens, counts, cotangent, first_gain, first_shift, in_proj, query_bias, value_bias, out_proj, out_bias,
          second_gain, second_shift, up_proj, hidden_bias, down_proj, down_bias):
    images, rows, width = tokens.shape
    own = first_gain.shape[0]
    ff = 4 * width
    x = tokens.reshape(images * rows, width)
    cot = cotangent.reshape(images * rows, width)
    vectors = (first_gain, first_shift, query_bias, value_bias, out_bias, second_gain, second_shift, down_bias)
    if hier:
        mine, other = gather_pieces(*pack(vectors, hidden_bias, in_proj, out_proj))
        updown = lax.all_gather(pack_mlp(up_proj, down_proj), "fsdp", axis=0, tiled=True)
    else:
        columns = jnp.concatenate(vectors[:3] + (jnp.zeros_like(query_bias),) + vectors[3:] + (hidden_bias,)).reshape(13, own).T
        packed = jnp.concatenate([in_proj, out_proj, columns, jnp.zeros((own, 243), BF)], axis=1)
        mine, other = gather_whole(packed)
        updown = jnp.concatenate([up_proj] + [down_proj[j * own:(j + 1) * own] for j in range(4)], axis=1)
        updown = regroup(lax.all_gather(updown, "fsdp", axis=0, tiled=True), own)
    qkv, probs, att, mid, sec, back, db, vec = attn_fwd(hier, counts, x, cot, mine, other)
    owners = width // own
    bias = vec[9:13].reshape(4, owners, own).transpose(1, 0, 2).reshape(1, ff)
    act, hg, hid, grads = mlp(sec, back, bias, updown)
    if not hier:
        sums = hid[:, 12:16].reshape(GROUPS, width // GROUPS, 4).transpose(0, 2, 1).reshape(owners, 4, own).transpose(0, 2, 1)
        hid = hid.at[:, 12:16].set(sums.reshape(width, 4))
        dg = grads[:, :, ff:].reshape(GROUPS, width // GROUPS, 4, width).transpose(0, 2, 1, 3).reshape(owners, 4, own, width)
        grads = jnp.concatenate([grads[:, :, :ff].reshape(width, ff), dg.transpose(0, 2, 1, 3).reshape(width, ff)], axis=1)
    mlp_grads = lax.psum_scatter(grads.reshape(width, 2 * ff), "fsdp", scatter_dimension=0, tiled=True)
    mg, qg, near, far = attn_bwd(hier, hg, mid, back, att, qkv, probs, x, vec, updown, db, hid, mine, other)
    blocks = images * rows // 256
    tok = lambda first, last, tie, old: tokens_grad(hier, first, last - first, x, qg, mg, vec, mine, other, tie, old)
    mix = lambda tie: mixed_out(0, blocks, counts, act, mid, vec, updown, tie, tie)
    if hier:
        got = permute(far, CORE)
        x_keep, x_send, y_keep, y_send = core_sum(near, got)
        x_got, y_got = permute(x_send, ACROSS), lax.ppermute(y_send, "rep", SWAP)
        mixed = mix(x_send)
        first_keep, first_send, second_keep, second_send = across_sum(x_keep, x_got, y_keep, y_got, mixed)
        first_got, second_got = lax.ppermute(first_send, "rep", SWAP), permute(second_send, ACROSS)
        toks = tok(0, 5 * blocks // 8, first_send, mixed)
        parts = plane_sum(first_keep, first_got, second_keep, second_got, toks)
        moved = [permute(parts[k] if k == 2 else after(parts[k], mlp_grads), ALONG[k]) for k in (2, 1, 3)]
        toks = tok(5 * blocks // 8, blocks, parts[3], toks)
        mlp_grads = after(mlp_grads, parts[3])
        mlp_got = lax.ppermute(mlp_grads, "rep", SWAP)
        low = along_sum(parts[0], *moved, toks)
        grad_up, grad_down = finish_mlp(mlp_grads, mlp_got, low)
        grad_in, grad_out, *lines, hidden = finish(low, lax.ppermute(low, "rep", SWAP), grad_up, width)
    else:
        mixed = mix(far)
        toks = tok(0, blocks, far, far)
        pieces = jnp.stack([near, far]).transpose(2, 1, 0, 3, 4).reshape(width, near.shape[-1])
        a, b = over_rep(lax.psum_scatter(pieces, "fsdp", scatter_dimension=0, tiled=True))
        wide = a.astype(F32) + b.astype(F32)
        grad_in, grad_out, lines = wide[:, :3 * width], wide[:, 3 * width:4 * width], wide[:, 4 * width:].T
        hidden = lines[12:16].reshape(4 * own)
        a, b = over_rep(mlp_grads)
        mlp_grads = a.astype(F32) + b.astype(F32)
        grad_up = mlp_grads[:, :ff]
        grad_down = jnp.concatenate([mlp_grads[:, ff + j * width:ff + (j + 1) * width] for j in range(4)], axis=0)
    return (mixed.reshape(tokens.shape), toks.reshape(tokens.shape), lines[10], lines[11], grad_in, lines[4], lines[5],
            grad_out, lines[3], lines[1], lines[2], grad_up, hidden, grad_down, lines[0])


def solution(mesh):
    rows = P(("fsdp", "rep"), None, None)
    v, m = P("fsdp"), P("fsdp", None)
    in_specs = (rows, P(("fsdp", "rep")), rows, v, v, m, v, v, m, v, v, v, m, v, m, v)
    out_specs = (rows, rows, v, v, m, v, v, m, v, v, v, m, v, m, v)
    hier = mesh.shape["fsdp"] == GROUPS and mesh.shape["rep"] == 2
    return jax.shard_map(functools.partial(local, hier), mesh=mesh, in_specs=in_specs, out_specs=out_specs, check_vma=False)
```
